32 devices in a mesh: parts: 2 (over y), layer: 4 (over x, core), blk: 4 (over z).
Axes of the slice: x: 2, y: 2, z: 4, core: 2. Of those that a mesh axis runs over, the one named last changes fastest.
Arguments:
- queries: bfloat16 [4, 256, 4096], P('layer', ('parts', 'blk')), parts along dimension 1, may hold values from -6 to 6
- store: bfloat16 [4, 8192, 4096], P('layer', ('parts', 'blk')), parts along dimension 1, may hold values from -0.09375 to 0.09375
- left_factor: float32 [4, 64, 64], P('layer')
- right_factor: float32 [4, 64, 64], P('layer')
- candidates: int32 [256, 16], P(('parts', 'layer')), parts along dimension 0, may hold values from 0 to 31, as said below
Outputs:
- scores: bfloat16 [256, 4096], P(('parts', 'layer'), 'blk'), parts along dimension 0
The draws below stay inside these ranges and needn't reach their ends.
There are 2 independent parts, one for each index of `parts`. The reference program is written for one: setup_inputs(seed, part) draws one part's arguments, and reference() takes and returns one part's arrays. A program takes and returns all parts, laid end to end along the dimension named above; an argument that names none is the same for every part. Nothing has to cross between parts.
Inputs may be any that keep to these rules, and one draw needn't show every extreme that they name: `candidates`: each row lists 16 different tiles.
All inputs are finite; a program needn't handle non-finite values.
Results may differ from the reference program's by a relative error of at most 0.0049.
Values may be sent and summed in bfloat16 or wider, within the bound.
No kernel may reach another device: no remote copies, remote signals or barrier semaphores. Data moves between devices by JAX's collectives and lax.ppermute only.
A program may use at most 64 MiB of HBM per device.

```python
import jax
import jax.numpy as jnp
from jax import lax

RANK = 64
PROJ = 4096
LAYERS = 4
EXAMPLES = 4096
QN = 128
TILE = 128
NTILES = 32
NC = 16


def factor_matrix(key):
    first, second = jax.random.split(key)
    diag_part = jnp.exp(jax.random.uniform(first, (LAYERS, RANK), jnp.float32, jnp.log(0.5), jnp.log(2.0)))
    spread = jax.random.normal(second, (LAYERS, RANK, RANK), jnp.float32) * (0.5 / jnp.sqrt(jnp.float32(RANK)))
    identity = jnp.eye(RANK, dtype=jnp.float32)
    return spread * (1.0 - identity) + diag_part[:, :, None] * identity


def draw_left_factor(key, part):
    key = jax.random.fold_in(key, 11)
    return factor_matrix(key)


def draw_right_factor(key, part):
    key = jax.random.fold_in(key, 23)
    return factor_matrix(key)


def draw_candidates(key, part):
    key = jax.random.fold_in(key, 37)
    row_keys = jax.random.split(key, QN)

    def one_row(row_key):
        return jax.random.permutation(row_key, NTILES)[:NC]
    return jax.vmap(one_row)(row_keys).astype(jnp.int32)


def level_of(stream_key, extent, shards, smallest, largest):
    gain, own = 1.0, jax.random.fold_in(stream_key, 6)
    for axis_at, blocks in shards:
        steps = jnp.exp(jax.random.uniform(jax.random.fold_in(own, axis_at), (blocks,), jnp.float32, smallest / len(shards), largest / len(shards)))
        gain = gain * jnp.repeat(steps, extent[axis_at] // blocks).reshape([-1 if axis == axis_at else 1 for axis in range(len(extent))])
    return gain


def noise(stream_key, shape, deviation, most, cuts=(), kind=jnp.bfloat16):
    drawn = deviation * jax.random.normal(stream_key, shape, jnp.float32)
    if cuts:
        drawn = drawn * level_of(stream_key, shape, cuts, -0.22, 0.18)
    return jnp.clip(drawn, -most, most).astype(kind)


def setup_inputs(seed: int = 0, part: int = 0) -> dict:
    key_list = jax.random.split(jax.random.key(seed), 6)
    own_keys = jax.random.split(jax.random.fold_in(key_list[5], part), 6)
    queries = noise(own_keys[0], (LAYERS, QN, PROJ), 1.0, 6.0, ((0, 4), (1, 4)))
    store = noise(own_keys[1], (LAYERS, EXAMPLES, PROJ), PROJ ** -0.5, 0.09375, ((0, 4), (1, 4)))
    left_factor = draw_left_factor(jax.random.fold_in(key_list[5], 71), part)
    right_factor = draw_right_factor(jax.random.fold_in(key_list[5], 71), part)
    candidates = draw_candidates(jax.random.fold_in(jax.random.fold_in(key_list[5], part), 71), part)
    return dict(queries=queries, store=store, left_factor=left_factor, right_factor=right_factor, candidates=candidates)


def precondition(queries, left_factor, right_factor):
    count = queries.shape[1]
    grid = queries.astype(jnp.float32).reshape(queries.shape[0], count, RANK, RANK)
    halfway = jnp.einsum('lij,lqjk->lqik', left_factor, grid, precision=lax.Precision.HIGHEST)
    result = jnp.einsum('lqik,lkm->lqim', halfway, right_factor, precision=lax.Precision.HIGHEST)
    return result.reshape(queries.shape[0], count, RANK * RANK).astype(jnp.bfloat16)

def reference(queries, store, left_factor, right_factor, candidates):
    conditioned = precondition(queries, left_factor, right_factor)

    def add_layer(total, pair):
        return (total + jnp.dot(pair[0], pair[1].T, preferred_element_type=jnp.float32), None)
    start = jnp.zeros((QN, EXAMPLES), jnp.float32)
    total, unused = lax.scan(add_layer, start, (conditioned, store))
    chosen = jnp.any(candidates[:, :, None] == jnp.arange(NTILES, dtype=jnp.int32)[None, None, :], axis=1)
    keep = jnp.repeat(chosen, TILE, axis=1)
    scaled = total / jnp.sqrt(jnp.float32(LAYERS))
    return jnp.where(keep, scaled, jnp.float32(0.0)).astype(jnp.bfloat16)
```

```python
import functools

import jax
import jax.numpy as jnp
from jax import lax
from jax.experimental import pallas as pl
from jax.experimental.pallas import tpu as pltpu
from jax.sharding import PartitionSpec as P

TILE = 128
GROUP = 32
LANES = 128
ROWS = 8
PIECES = 4
VMEM = 56 * 1024 * 1024


def two_parts(value):
    high = value.astype(jnp.bfloat16)
    low = (value - high.astype(jnp.float32)).astype(jnp.bfloat16)
    return high, low


def iota(shape, axis):
    return lax.broadcasted_iota(jnp.int32, shape, axis)


def dot(left, right):
    return jnp.dot(left, right, preferred_element_type=jnp.float32)


def ones_where(condition):
    return jnp.where(condition, 1.0, 0.0).astype(jnp.bfloat16)


def spread_left(left_factor, first, count):
    side = left_factor.shape[0]
    wide = ones_where(iota((side, side * ROWS), 1) // ROWS == iota((side, side * ROWS), 0))
    tall = ones_where(iota((count * ROWS, side), 0) // ROWS + first == iota((count * ROWS, side), 1))
    shape = (count * ROWS, side * ROWS)
    same = iota(shape, 0) % ROWS == iota(shape, 1) % ROWS

    def one(part):
        columns = dot(part, wide).astype(jnp.bfloat16)
        return jnp.where(same, dot(tall, columns), 0.0).astype(jnp.bfloat16)

    return [one(part) for part in two_parts(left_factor)]


def spread_right(right_factor):
    side = right_factor.shape[0]
    tall = ones_where(iota((2 * side, side), 0) % side == iota((2 * side, side), 1))
    wide = ones_where(iota((side, 8 * side), 1) % side == iota((side, 8 * side), 0))
    shape = (2 * side, 8 * side)
    same = iota(shape, 0) // side == iota(shape, 1) // (4 * side)

    def one(part):
        rows = dot(tall, part).astype(jnp.bfloat16)
        return jnp.where(same, dot(rows, wide), 0.0).astype(jnp.bfloat16)

    return [one(part) for part in two_parts(right_factor)]


def condition_kernel(first, count, queries, left_factor, right_factor, *outs):
    side = left_factor.shape[0]
    pairs = side // 2
    per_out = count // len(outs)
    lefts = spread_left(left_factor[...], first, count)
    rights = spread_right(right_factor[...])
    low_half = iota((1, 1, LANES), 2) < side
    for block in range(queries.shape[0] // GROUP):
        rows = pl.ds(block * GROUP, GROUP)
        stacked = jnp.concatenate(
            [queries[rows, pl.ds(pair * LANES, LANES)] for pair in range(pairs)], axis=0
        )
        mixed = dot(stacked, rights[0]) + dot(stacked, rights[1])
        mixed = mixed.reshape(pairs, GROUP // ROWS, ROWS, 8 * side)

        def lanes(group, parity, half):
            start = parity * 4 * side + half * LANES
            return mixed[:, group, :, start : start + LANES]

        def half_of(half):
            both = [
                jnp.where(low_half, lanes(2 * half, parity, half), lanes(2 * half + 1, parity, half))
                for parity in range(2)
            ]
            return jnp.stack(both, axis=1).reshape(side * ROWS, LANES)

        high, low = two_parts(jnp.concatenate([half_of(0), half_of(1)], axis=1))
        result = dot(lefts[0], high) + dot(lefts[0], low) + dot(lefts[1], high)
        result = result.reshape(count // 2, 2, ROWS, 2 * LANES)
        groups = []
        for half in range(2):
            even = result[:, 0, :, half * LANES : (half + 1) * LANES]
            odd = result[:, 1, :, half * LANES : (half + 1) * LANES]
            groups.append(jnp.where(low_half, even, pltpu.roll(odd, side, 2)))
            groups.append(jnp.where(low_half, pltpu.roll(even, side, 2), odd))
        done = jnp.concatenate(groups, axis=1).astype(jnp.bfloat16)
        for pair in range(count // 2):
            out = outs[2 * pair // per_out]
            out[rows, pl.ds((pair % (per_out // 2)) * LANES, LANES)] = done[pair]


def condition(queries, left_factor, right_factor, first, count, pieces):
    block_rows = queries.shape[0]
    side = left_factor.shape[0]
    width = count * side // pieces
    return pl.pallas_call(
        functools.partial(condition_kernel, first, count),
        out_shape=[jax.ShapeDtypeStruct((block_rows, width), jnp.bfloat16)] * pieces,
        compiler_params=pltpu.CompilerParams(vmem_limit_bytes=VMEM),
        cost_estimate=pl.CostEstimate(
            flops=2 * block_rows * count * side * side * 8, bytes_accessed=queries.size * 2, transcendentals=0
        ),
        name="condition",
    )(queries, left_factor, right_factor)


def score_dot(blocks, store):
    queries = jnp.concatenate([block[...] for block in blocks], axis=0)
    return lax.dot_general(
        queries, store[...], (((1,), (1,)), ((), ())), preferred_element_type=jnp.float32
    )


def score_kernel(has_sum, blocks_count, *refs):
    blocks, rest = refs[:blocks_count], refs[blocks_count:]
    value = score_dot(blocks, rest[0])
    if has_sum:
        value = value + rest[1][...]
    rest[-1][...] = value


def last_score_kernel(blocks_count, block_rows, own_rows, *refs):
    blocks, rest = refs[:blocks_count], refs[blocks_count:]
    store, so_far, outs, total = rest[0], rest[1], rest[2:-1], rest[-1]
    total[...] = score_dot(blocks, store) + so_far[...]
    cycle_index = lax.axis_index("blk")
    layer_index = lax.axis_index("layer")
    piece = min(own_rows, block_rows)
    for shift, out in enumerate(outs):
        owner = lax.rem(layer_index + shift, len(outs))
        for start in range(0, own_rows, piece):
            row = owner * own_rows + start
            slot = lax.rem(cycle_index - row // block_rows + blocks_count, blocks_count)
            place = pl.multiple_of(slot * block_rows + lax.rem(row, block_rows), piece)
            out[pl.ds(start, piece), :] = total[pl.ds(place, piece), :].astype(out.dtype)


def score(blocks, store, so_far, piece, last, layers):
    block_rows, width = blocks[0].shape
    count = block_rows * len(blocks)
    examples = store.shape[0]
    tile = 256
    whole = [pl.BlockSpec((block_rows, width), lambda e: (0, 0))] * len(blocks)
    columns = pl.BlockSpec((count, tile), lambda e: (0, e))
    operands = [*blocks, store] + ([] if so_far is None else [so_far])
    in_specs = whole + [pl.BlockSpec((tile, width), lambda e: (e, piece))]
    in_specs += [] if so_far is None else [columns]
    cost = pl.CostEstimate(
        flops=2 * count * width * examples, bytes_accessed=examples * width * 2, transcendentals=0
    )
    params = pltpu.CompilerParams(vmem_limit_bytes=VMEM)
    if not last:
        return pl.pallas_call(
            functools.partial(score_kernel, so_far is not None, len(blocks)),
            grid=(examples // tile,),
            in_specs=in_specs,
            out_specs=columns,
            out_shape=jax.ShapeDtypeStruct((count, examples), jnp.float32),
            compiler_params=params,
            cost_estimate=cost,
            name="score",
        )(*operands)
    own_rows = count // layers
    return pl.pallas_call(
        functools.partial(last_score_kernel, len(blocks), block_rows, own_rows),
        grid=(examples // tile,),
        in_specs=in_specs,
        out_specs=[pl.BlockSpec((own_rows, tile), lambda e: (0, e))] * layers,
        out_shape=[
            jax.ShapeDtypeStruct((own_rows, examples), jnp.float32 if shift == 0 else jnp.bfloat16)
            for shift in range(layers)
        ],
        scratch_shapes=[pltpu.VMEM((count, tile), jnp.float32)],
        compiler_params=params,
        cost_estimate=cost,
        name="last_score",
    )(*operands)


def finish_kernel(layers, candidates, *refs):
    parts, out = refs[:-1], refs[-1]
    total = parts[0][...]
    for part in parts[1:]:
        total = total + part[...].astype(jnp.float32)
    scaled = total / jnp.sqrt(jnp.float32(layers))
    tiles_here = out.shape[1] // TILE
    first = lax.axis_index("blk") * tiles_here
    listed = candidates[...]
    for tile in range(tiles_here):
        hit = jnp.max(jnp.where(listed == first + tile, 1.0, 0.0), axis=1, keepdims=True)
        columns = slice(tile * TILE, (tile + 1) * TILE)
        out[:, columns] = jnp.where(hit > 0.0, scaled[:, columns], 0.0).astype(out.dtype)


def finish(parts, candidates, layers):
    return pl.pallas_call(
        functools.partial(finish_kernel, layers),
        out_shape=jax.ShapeDtypeStruct(parts[0].shape, jnp.bfloat16),
        compiler_params=pltpu.CompilerParams(vmem_limit_bytes=VMEM),
        name="finish",
    )(candidates, *parts)


def shifted(value, axis, steps):
    count = lax.axis_size(axis)
    return lax.ppermute(value, axis, [(source, (source + steps) % count) for source in range(count)])


def per_device(queries, store, left_factor, right_factor, candidates):
    queries, store = queries[0], store[0]
    left_factor, right_factor = left_factor[0], right_factor[0]
    side = left_factor.shape[0]
    cycle = lax.axis_size("blk")
    layers = lax.axis_size("layer")
    count = side // PIECES
    own = condition(queries, left_factor, right_factor, 0, count, 1)
    own += condition(queries, left_factor, right_factor, count, side - count, PIECES - 1)
    held = [[piece] for piece in own]
    for _ in range(cycle - 1):
        for blocks in held:
            blocks.append(shifted(blocks[-1], "blk", 1))
    so_far = None
    for piece, blocks in enumerate(held):
        so_far = score(blocks, store, so_far, piece, piece == PIECES - 1, layers)
    parts = [so_far[0]]
    for shift in range(1, layers):
        parts.append(shifted(so_far[shift], "layer", shift))
    return finish(parts, candidates, layers)


def solution(mesh):
    placed = (
        P("layer", ("parts", "blk"), None),
        P("layer", ("parts", "blk"), None),
        P("layer", None, None),
        P("layer", None, None),
        P(("parts", "layer"), None),
    )
    return jax.shard_map(
        per_device,
        mesh=mesh,
        in_specs=placed,
        out_specs=P(("parts", "layer"), "blk"),
        check_vma=False,
    )
```

```python
import functools

import jax
import jax.numpy as jnp
from jax import lax
from jax.experimental import pallas as pl
from jax.experimental.pallas import tpu as pltpu
from jax.sharding import PartitionSpec as P

TILE = 128
GROUP = 32
LANES = 128
ROWS = 8
VMEM = 24 * 1024 * 1024


def two_parts(value):
    high = value.astype(jnp.bfloat16)
    low = (value - high.astype(jnp.float32)).astype(jnp.bfloat16)
    return high, low


def iota(shape, axis):
    return lax.broadcasted_iota(jnp.int32, shape, axis)


def dot(left, right):
    return jnp.dot(left, right, preferred_element_type=jnp.float32)


def ones_where(condition):
    return jnp.where(condition, 1.0, 0.0).astype(jnp.bfloat16)


def spread_left(left_factor):
    side = left_factor.shape[0]
    wide = ones_where(iota((side, side * ROWS), 1) // ROWS == iota((side, side * ROWS), 0))
    columns = dot(jnp.concatenate(two_parts(left_factor), axis=0), wide).reshape(2, side, 1, side * ROWS)
    same = iota((1, ROWS, side * ROWS), 1) == iota((1, ROWS, side * ROWS), 2) % ROWS
    parts = [jnp.where(same, columns[part], 0.0).reshape(side * ROWS, side * ROWS) for part in range(2)]
    return jnp.concatenate([part.astype(jnp.bfloat16) for part in parts], axis=1)


def spread_right(right_factor):
    side = right_factor.shape[0]
    wide = ones_where(iota((side, 4 * side), 1) % side == iota((side, 4 * side), 0))
    same = iota((4 * side, 4 * side), 0) // side == iota((4 * side, 4 * side), 1) // side
    high, low = [
        jnp.where(same, jnp.concatenate([dot(part, wide)] * 4, axis=0), 0.0).astype(jnp.bfloat16)
        for part in two_parts(right_factor)
    ]
    return jnp.concatenate([high, low, high], axis=0)


def condition_kernel(queries, left_factor, right_factor, whole, *halves):
    side = left_factor.shape[0]
    pairs = side // 2
    left = spread_left(left_factor[...])
    right = spread_right(right_factor[...])
    low_half = iota((1, 1, LANES), 2) < side
    per_half = pairs // len(halves)
    for block in range(queries.shape[0] // GROUP):
        rows = pl.ds(block * GROUP, GROUP)
        straight = jnp.stack(
            [queries[rows, pl.ds(pair * LANES, LANES)].astype(jnp.float32) for pair in range(pairs)]
        )
        swapped = pltpu.roll(straight, side, 2).reshape(pairs, GROUP // ROWS, ROWS, LANES)
        straight = straight.reshape(pairs, GROUP // ROWS, ROWS, LANES)
        columns = []
        for group in (0, 2):
            even = jnp.where(low_half, straight[:, group], swapped[:, group + 1])
            odd = jnp.where(low_half, swapped[:, group], straight[:, group + 1])
            columns.append(jnp.stack([even, odd], axis=1).reshape(side * ROWS, LANES))
        grid = jnp.concatenate(columns, axis=1).astype(jnp.bfloat16)
        halfway = dot(left, jnp.concatenate([grid, grid], axis=0))
        high, low = two_parts(halfway)
        result = dot(jnp.concatenate([high, high, low], axis=1), right)
        result = result.reshape(pairs, 2, ROWS, 2 * LANES)
        groups = []
        for half in range(2):
            even = result[:, 0, :, half * LANES : (half + 1) * LANES]
            odd = result[:, 1, :, half * LANES : (half + 1) * LANES]
            groups.append(jnp.where(low_half, even, pltpu.roll(odd, side, 2)))
            groups.append(jnp.where(low_half, pltpu.roll(even, side, 2), odd))
        done = jnp.concatenate(groups, axis=1).astype(jnp.bfloat16)
        for pair in range(pairs):
            whole[rows, pl.ds(pair * LANES, LANES)] = done[pair]
            halves[pair // per_half][rows, pl.ds(pair % per_half * LANES, LANES)] = done[pair]


def in_vmem(count):
    return [pl.BlockSpec(memory_space=pltpu.VMEM)] * count


def condition(queries, left_factor, right_factor):
    block_rows, entries = queries.shape
    shapes = [entries, entries // 2, entries // 2]
    return pl.pallas_call(
        condition_kernel,
        in_specs=in_vmem(3),
        out_specs=in_vmem(3),
        out_shape=[jax.ShapeDtypeStruct((block_rows, width), jnp.bfloat16) for width in shapes],
        compiler_params=pltpu.CompilerParams(vmem_limit_bytes=VMEM),
        cost_estimate=pl.CostEstimate(
            flops=block_rows * entries * 4096, bytes_accessed=queries.size * 4, transcendentals=0
        ),
        name="condition",
    )(queries, left_factor, right_factor)


def score_block(blocks, store, first, write):
    rows = [jnp.concatenate([piece[...] for piece in pieces], axis=1) for pieces in blocks]
    queries = jnp.concatenate(rows, axis=0)
    turned = queries.T
    width = queries.shape[1]
    tile = 256

    def one(step, carry):
        place = pl.ds(pl.multiple_of(step * tile, tile), tile)
        value = dot(store[place, pl.ds(first, width)], turned)
        write(place, value.T)
        return carry

    lax.fori_loop(0, store.shape[0] // tile, one, 0)


def score_kernel(layout, first, *refs):
    refs = list(refs)
    blocks = [[refs.pop(0) for _ in range(pieces)] for pieces in layout]
    store, out = refs

    def write(place, value):
        out[:, place] = value

    score_block(blocks, store, first, write)


def score(blocks, store, first):
    count = sum(pieces[0].shape[0] for pieces in blocks)
    width = sum(piece.shape[1] for piece in blocks[0])
    operands = [piece for pieces in blocks for piece in pieces]
    examples = store.shape[0]
    return pl.pallas_call(
        functools.partial(score_kernel, [len(pieces) for pieces in blocks], first),
        in_specs=in_vmem(len(operands) + 1),
        out_specs=in_vmem(1)[0],
        out_shape=jax.ShapeDtypeStruct((count, examples), jnp.float32),
        compiler_params=pltpu.CompilerParams(vmem_limit_bytes=VMEM),
        cost_estimate=pl.CostEstimate(
            flops=2 * count * width * examples, bytes_accessed=examples * width * 2, transcendentals=0
        ),
        name="score",
    )(*operands, store)


def last_score_kernel(first, slot_of, last_piece, store, early, late, out, total):
    early_rows = early.shape[0]
    block_rows = last_piece.shape[0]
    total[pl.ds(0, early_rows), :] = early[...]

    def write(place, value):
        total[pl.ds(early_rows, block_rows), place] = late[:, place] + value

    score_block([[last_piece]], store, first, write)
    index = lax.axis_index("blk")
    owners, own_rows = out.shape[:2]
    piece = min(own_rows, block_rows)
    for owner in range(owners):
        for start in range(0, own_rows, piece):
            block, row = divmod(owner * own_rows + start, block_rows)
            place = pl.multiple_of(slot_of(index, block) * block_rows + row, piece)
            out[owner, pl.ds(start, piece), :] = total[pl.ds(place, piece), :].astype(out.dtype)


def last_score(last_piece, store, first, early, late, slot_of, layers):
    block_rows, width = last_piece.shape
    examples = store.shape[0]
    count = early.shape[0] + block_rows
    return pl.pallas_call(
        functools.partial(last_score_kernel, first, slot_of),
        in_specs=in_vmem(4),
        out_specs=in_vmem(1)[0],
        out_shape=jax.ShapeDtypeStruct((layers, count // layers, examples), jnp.bfloat16),
        scratch_shapes=[pltpu.VMEM((count, examples), jnp.float32)],
        compiler_params=pltpu.CompilerParams(vmem_limit_bytes=VMEM),
        cost_estimate=pl.CostEstimate(
            flops=2 * block_rows * width * examples, bytes_accessed=examples * width * 2, transcendentals=0
        ),
        name="last_score",
    )(last_piece, store, early, late)


def finish_kernel(layers, candidates, parts, out):
    total = parts[0].astype(jnp.float32)
    for layer in range(1, layers):
        total = total + parts[layer].astype(jnp.float32)
    scaled = total / jnp.sqrt(jnp.float32(layers))
    tiles_here = out.shape[1] // TILE
    first = lax.axis_index("blk") * tiles_here
    listed = candidates[...]
    for tile in range(tiles_here):
        hit = jnp.max(jnp.where(listed == first + tile, 1.0, 0.0), axis=1, keepdims=True)
        columns = slice(tile * TILE, (tile + 1) * TILE)
        out[:, columns] = jnp.where(hit > 0.0, scaled[:, columns], 0.0).astype(out.dtype)


def finish(parts, candidates):
    layers, own_rows, examples = parts.shape
    return pl.pallas_call(
        functools.partial(finish_kernel, layers),
        in_specs=in_vmem(2),
        out_specs=in_vmem(1)[0],
        out_shape=jax.ShapeDtypeStruct((own_rows, examples), jnp.bfloat16),
        compiler_params=pltpu.CompilerParams(vmem_limit_bytes=VMEM),
        name="finish",
    )(candidates, parts)


def permuted(value, target_of):
    count = lax.axis_size("blk")
    return lax.ppermute(value, "blk", [(source, target_of(source) % count) for source in range(count)])


def gather_line(own):
    whole, halves = own[0], own[1:]
    far = [permuted(half, lambda source: source ^ 2) for half in halves]
    near = permuted(whole, lambda source: source ^ 1)
    last = [permuted(half, lambda source: source ^ 1) for half in far]
    return [[whole], [near], far], last, lax.bitwise_xor


def gather_ring(own):
    count = lax.axis_size("blk")
    held, moving = [[own[0]]], own[1:]
    for _ in range(count - 1):
        moving = [permuted(half, lambda source: source + 1) for half in moving]
        held.append(moving)
    return held[:-1], held[-1], lambda index, block: lax.rem(index - block + count, count)


def per_device(queries, store, left_factor, right_factor, candidates):
    queries, store = queries[0], store[0]
    layers = lax.axis_size("layer")
    own = condition(queries, left_factor[0], right_factor[0])
    gather = gather_line if lax.axis_size("blk") == 4 else gather_ring
    early, last, slot_of = gather(own)
    half = last[0].shape[1]
    early_scores = score(early, store, 0)
    late_scores = score([[last[0]]], store, 0)
    partial = last_score(last[1], store, half, early_scores, late_scores, slot_of, layers)
    return finish(lax.all_to_all(partial, "layer", 0, 0), candidates)


def solution(mesh):
    placed = (
        P("layer", ("parts", "blk"), None),
        P("layer", ("parts", "blk"), None),
        P("layer", None, None),
        P("layer", None, None),
        P(("parts", "layer"), None),
    )
    return jax.shard_map(
        per_device,
        mesh=mesh,
        in_specs=placed,
        out_specs=P(("parts", "layer"), "blk"),
        check_vma=False,
    )
```

```python
import functools

import jax
import jax.numpy as jnp
from jax import lax
from jax.experimental import pallas as pl
from jax.experimental.pallas import tpu as pltpu
from jax.sharding import PartitionSpec as P

TILE = 128
GROUP = 32
LANES = 128
ROWS = 8
VMEM = 24 * 1024 * 1024


def two_parts(value):
    high = value.astype(jnp.bfloat16)
    low = (value - high.astype(jnp.float32)).astype(jnp.bfloat16)
    return high, low


def iota(shape, axis):
    return lax.broadcasted_iota(jnp.int32, shape, axis)


def dot(left, right):
    return jnp.dot(left, right, preferred_element_type=jnp.float32)


def ones_where(condition):
    return jnp.where(condition, 1.0, 0.0).astype(jnp.bfloat16)


def spread_left(left_factor):
    side = left_factor.shape[0]
    wide = ones_where(iota((side, side * ROWS), 1) // ROWS == iota((side, side * ROWS), 0))
    columns = dot(jnp.concatenate(two_parts(left_factor), axis=0), wide).reshape(2, side, 1, side * ROWS)
    same = iota((1, ROWS, side * ROWS), 1) == iota((1, ROWS, side * ROWS), 2) % ROWS
    parts = [jnp.where(same, columns[part], 0.0).reshape(side * ROWS, side * ROWS) for part in range(2)]
    return jnp.concatenate([part.astype(jnp.bfloat16) for part in parts], axis=1)


def spread_right(right_factor):
    side = right_factor.shape[0]
    wide = ones_where(iota((side, 4 * side), 1) % side == iota((side, 4 * side), 0))
    same = iota((4 * side, 4 * side), 0) // side == iota((4 * side, 4 * side), 1) // side
    high, low = [
        jnp.where(same, jnp.concatenate([dot(part, wide)] * 4, axis=0), 0.0).astype(jnp.bfloat16)
        for part in two_parts(right_factor)
    ]
    return jnp.concatenate([high, low, high], axis=0)


def condition_kernel(queries_in, left_in, right_in, whole, low, high, queries, left_factor, right_factor, arrived):
    halves = (low, high)
    copies = [
        pltpu.make_async_copy(source.at[0], target, arrived.at[place])
        for place, (source, target) in enumerate(
            [(left_in, left_factor), (right_in, right_factor), (queries_in, queries)]
        )
    ]
    for copy in copies:
        copy.start()
    side = left_factor.shape[0]
    pairs = side // 2
    copies[0].wait()
    copies[1].wait()
    left = spread_left(left_factor[...])
    right = spread_right(right_factor[...])
    low_half = iota((1, 1, LANES), 2) < side
    per_half = pairs // len(halves)
    copies[2].wait()
    for block in range(queries.shape[0] // GROUP):
        rows = pl.ds(block * GROUP, GROUP)
        straight = jnp.stack(
            [queries[rows, pl.ds(pair * LANES, LANES)].astype(jnp.float32) for pair in range(pairs)]
        )
        swapped = pltpu.roll(straight, side, 2).reshape(pairs, GROUP // ROWS, ROWS, LANES)
        straight = straight.reshape(pairs, GROUP // ROWS, ROWS, LANES)
        columns = []
        for group in (0, 2):
            even = jnp.where(low_half, straight[:, group], swapped[:, group + 1])
            odd = jnp.where(low_half, swapped[:, group], straight[:, group + 1])
            columns.append(jnp.stack([even, odd], axis=1).reshape(side * ROWS, LANES))
        grid = jnp.concatenate(columns, axis=1).astype(jnp.bfloat16)
        halfway = dot(left, jnp.concatenate([grid, grid], axis=0))
        high, low = two_parts(halfway)
        result = dot(jnp.concatenate([high, high, low], axis=1), right)
        result = result.reshape(pairs, 2, ROWS, 2 * LANES)
        groups = []
        for half in range(2):
            even = result[:, 0, :, half * LANES : (half + 1) * LANES]
            odd = result[:, 1, :, half * LANES : (half + 1) * LANES]
            groups.append(jnp.where(low_half, even, pltpu.roll(odd, side, 2)))
            groups.append(jnp.where(low_half, pltpu.roll(even, side, 2), odd))
        done = jnp.concatenate(groups, axis=1).astype(jnp.bfloat16)
        for pair in range(pairs):
            whole[rows, pl.ds(pair * LANES, LANES)] = done[pair]
            halves[pair // per_half][rows, pl.ds(pair % per_half * LANES, LANES)] = done[pair]


def in_vmem(count):
    return [pl.BlockSpec(memory_space=pltpu.VMEM)] * count


def condition(queries, left_factor, right_factor):
    unused, block_rows, entries = queries.shape
    side = left_factor.shape[1]
    shapes = [entries, entries // 2, entries // 2]
    return pl.pallas_call(
        condition_kernel,
        in_specs=[pl.BlockSpec(memory_space=pltpu.HBM)] * 3,
        out_specs=in_vmem(3),
        out_shape=[jax.ShapeDtypeStruct((block_rows, width), jnp.bfloat16) for width in shapes],
        scratch_shapes=[
            pltpu.VMEM((block_rows, entries), jnp.bfloat16),
            pltpu.VMEM((side, side), jnp.float32),
            pltpu.VMEM((side, side), jnp.float32),
            pltpu.SemaphoreType.DMA((3,)),
        ],
        compiler_params=pltpu.CompilerParams(vmem_limit_bytes=VMEM),
        cost_estimate=pl.CostEstimate(
            flops=block_rows * entries * 4096, bytes_accessed=queries.size * 4, transcendentals=0
        ),
        name="condition",
    )(*[pltpu.with_memory_space_constraint(value, pltpu.HBM) for value in (queries, left_factor, right_factor)])


STEP = 256


def score_block(blocks, store, first, write, arrived=None):
    rows = [jnp.concatenate([piece[...] for piece in pieces], axis=1) for pieces in blocks]
    queries = jnp.concatenate(rows, axis=0)
    turned = queries.T
    width = queries.shape[1]

    def one(step, carry):
        place = pl.ds(pl.multiple_of(step * STEP, STEP), STEP)
        if arrived is not None:
            arrived(step)
        value = dot(store[0, place, pl.ds(first, width)], turned)
        write(place, value.T)
        return carry

    lax.fori_loop(0, store.shape[1] // STEP, one, 0)


def score_kernel(layout, first, *refs):
    refs = list(refs)
    blocks = [[refs.pop(0) for _ in range(pieces)] for pieces in layout]
    store, out = refs

    def write(place, value):
        out[:, place] = value

    score_block(blocks, store, first, write)


def call_score(kernel, blocks, store, others, name, store_space=pltpu.VMEM, **shapes):
    operands = [piece for pieces in blocks for piece in pieces]
    count = sum(pieces[0].shape[0] for pieces in blocks)
    width = sum(piece.shape[1] for piece in blocks[0])
    examples = store.shape[1]
    return pl.pallas_call(
        kernel,
        in_specs=in_vmem(len(operands)) + [pl.BlockSpec(memory_space=store_space)] + in_vmem(len(others)),
        out_specs=jax.tree.map(lambda unused: in_vmem(1)[0], shapes["out_shape"]),
        compiler_params=pltpu.CompilerParams(vmem_limit_bytes=VMEM),
        cost_estimate=pl.CostEstimate(
            flops=2 * count * width * examples, bytes_accessed=examples * width * 2, transcendentals=0
        ),
        name=name,
        **shapes,
    )(*operands, store, *others)


def score(blocks, store, first):
    count = sum(pieces[0].shape[0] for pieces in blocks)
    layout = [len(pieces) for pieces in blocks]
    shape = jax.ShapeDtypeStruct((count, store.shape[1]), jnp.float32)
    kernel = functools.partial(score_kernel, layout, first)
    return call_score(kernel, blocks, store, [], "score", out_shape=shape)


def pair_kernel(layout, first, has_sum, layers, *refs):
    refs = list(refs)
    blocks = [[refs.pop(0) for _ in range(pieces)] for pieces in layout]
    store = refs.pop(0)
    so_far = refs.pop(0) if has_sum else None
    arrived = None
    if not has_sum:
        far_store = store
        store, semaphores = refs[-2:]
        refs = refs[:-2]

        def copy_of(step):
            place = pl.ds(pl.multiple_of(step * STEP, STEP), STEP)
            return pltpu.make_async_copy(far_store.at[0, place], store.at[0, place], semaphores.at[step])

        for step in range(store.shape[1] // STEP):
            copy_of(step).start()

        def arrived(step):
            copy_of(step).wait()

    outs, total = refs[:-1], refs[-1]

    def write(place, value):
        total[:, place] = value if so_far is None else value + so_far[:, place]

    score_block(blocks, store, first, write, arrived)
    rows = outs[0].shape[0]
    index, layer = lax.axis_index("blk"), lax.axis_index("layer")
    for shift, out in enumerate(outs):
        owner = lax.rem(layer + shift, layers)
        slot = lax.bitwise_and(lax.bitwise_xor(index, owner), 1)
        out[...] = total[pl.ds(pl.multiple_of(slot * rows, rows), rows), :].astype(out.dtype)


def score_pair(blocks, store, first, so_far, layers):
    rows = blocks[0][0].shape[0]
    examples = store.shape[1]
    kernel = functools.partial(pair_kernel, [len(pieces) for pieces in blocks], first, so_far is not None, layers)
    scratch = [pltpu.VMEM((2 * rows, examples), jnp.float32)]
    if so_far is None:
        scratch += [pltpu.VMEM(store.shape, store.dtype), pltpu.SemaphoreType.DMA((examples // STEP,))]
        store = pltpu.with_memory_space_constraint(store, pltpu.HBM)
    return call_score(
        kernel,
        blocks,
        store,
        [] if so_far is None else [so_far],
        "score_pair",
        pltpu.HBM if so_far is None else pltpu.VMEM,
        out_shape=[
            jax.ShapeDtypeStruct((rows, examples), jnp.float32 if shift == 0 else jnp.bfloat16)
            for shift in range(layers)
        ],
        scratch_shapes=scratch,
    )


def write_rows(total, layers, listed, out):
    scaled = total / jnp.sqrt(jnp.float32(layers))
    tiles_here = out.shape[1] // TILE
    first = lax.axis_index("blk") * tiles_here
    for tile in range(tiles_here):
        hit = jnp.max(jnp.where(listed == first + tile, 1.0, 0.0), axis=1, keepdims=True)
        columns = slice(tile * TILE, (tile + 1) * TILE)
        out[:, columns] = jnp.where(hit > 0.0, scaled[:, columns], 0.0).astype(out.dtype)


def finish_kernel(layers, candidates, *refs):
    sets, out = refs[:-1], refs[-1]
    sets = [sets[start : start + layers] for start in range(0, len(sets), layers)]
    index, layer = lax.axis_index("blk"), lax.axis_index("layer")
    which = lax.bitwise_xor(index, layer) // 2
    for place, parts in enumerate(sets):

        @pl.when((which == place) | (len(sets) == 1))
        def _():
            total = parts[0][...].astype(jnp.float32)
            for part in parts[1:]:
                total = total + part[...].astype(jnp.float32)
            write_rows(total, layers, candidates[...], out)


def finish(sets, candidates, layers):
    parts = [part for one_set in sets for part in one_set]
    return pl.pallas_call(
        functools.partial(finish_kernel, layers),
        in_specs=in_vmem(1 + len(parts)),
        out_specs=in_vmem(1)[0],
        out_shape=jax.ShapeDtypeStruct(parts[0].shape, jnp.bfloat16),
        compiler_params=pltpu.CompilerParams(vmem_limit_bytes=VMEM),
        name="finish",
    )(candidates, *parts)


def permuted(value, target_of):
    count = lax.axis_size("blk")
    return lax.ppermute(value, "blk", [(source, target_of(source) % count) for source in range(count)])


def to_owners(parts, slots):
    layers, count = lax.axis_size("layer"), lax.axis_size("blk")
    out = [parts[0]]
    for shift in range(1, layers):
        pairs = [
            (((index ^ slot) - shift) % layers * count + index, (index ^ slot) * count + index)
            for index in range(count)
            for slot in slots
        ]
        out.append(lax.ppermute(parts[shift], ("layer", "blk"), pairs))
    return out


def on_line(own, store, candidates, layers):
    whole, halves = own[0], own[1:]
    half = halves[0].shape[1]
    far_low = permuted(halves[0], lambda source: source ^ 2)
    near = permuted(whole, lambda source: source ^ 1)
    far_high = permuted(halves[1], lambda source: source ^ 2)
    last_low = permuted(far_low, lambda source: source ^ 1)
    near, far_low = lax.optimization_barrier((near, far_low))
    early = score_pair([[whole], [near]], store, 0, None, layers)
    far_high, early = lax.optimization_barrier((far_high, early))
    last_high = permuted(far_high, lambda source: source ^ 1)
    early = to_owners(early, (0, 1))
    low_scores = score([[far_low], [last_low]], store, 0)
    late = to_owners(score_pair([[far_high], [last_high]], store, half, low_scores, layers), (2, 3))
    return finish([early, late], candidates, layers)


def on_ring(own, store, candidates, layers):
    count = lax.axis_size("blk")
    rows = own[0].shape[0]
    slots, moving = [score([[own[0]]], store, 0)], own[0]
    for _ in range(count - 1):
        moving = permuted(moving, lambda source: source + 1)
        slots.append(score([[moving]], store, 0))
    turns = lax.rem(lax.axis_index("blk") - jnp.arange(count) + count, count)
    total = jnp.stack(slots)[turns].reshape(layers, count * rows // layers, store.shape[1])
    parts = lax.all_to_all(total.astype(jnp.bfloat16), "layer", 0, 0)
    return finish([[parts[layer] for layer in range(layers)]], candidates, layers)


def per_device(queries, store, left_factor, right_factor, candidates):
    layers, count = lax.axis_size("layer"), lax.axis_size("blk")
    own = condition(queries, left_factor, right_factor)
    way = on_line if layers == 4 and count == 4 else on_ring
    return way(own, store, candidates, layers)


def solution(mesh):
    placed = (
        P("layer", ("parts", "blk"), None),
        P("layer", ("parts", "blk"), None),
        P("layer", None, None),
        P("layer", None, None),
        P(("parts", "layer"), None),
    )
    return jax.shard_map(
        per_device,
        mesh=mesh,
        in_specs=placed,
        out_specs=P(("parts", "layer"), "blk"),
        check_vma=False,
    )
```

```python
import functools

import jax
import jax.numpy as jnp
from jax import lax
from jax.experimental import pallas as pl
from jax.experimental.pallas import tpu as pltpu
from jax.sharding import PartitionSpec as P

TILE = 128
GROUP = 32
LANES = 128
ROWS = 8
VMEM = 24 * 1024 * 1024


def two_parts(value):
    high = value.astype(jnp.bfloat16)
    low = (value - high.astype(jnp.float32)).astype(jnp.bfloat16)
    return high, low


def iota(shape, axis):
    return lax.broadcasted_iota(jnp.int32, shape, axis)


def dot(left, right):
    return jnp.dot(left, right, preferred_element_type=jnp.float32)


def ones_where(condition):
    return jnp.where(condition, 1.0, 0.0).astype(jnp.bfloat16)


def spread_left(left_factor):
    side = left_factor.shape[0]
    wide = ones_where(iota((side, side * ROWS), 1) // ROWS == iota((side, side * ROWS), 0))
    columns = dot(jnp.concatenate(two_parts(left_factor), axis=0), wide).reshape(2, side, 1, side * ROWS)
    same = iota((1, ROWS, side * ROWS), 1) == iota((1, ROWS, side * ROWS), 2) % ROWS
    parts = [jnp.where(same, columns[part], 0.0).reshape(side * ROWS, side * ROWS) for part in range(2)]
    return jnp.concatenate([part.astype(jnp.bfloat16) for part in parts], axis=1)


def spread_right(right_factor):
    side = right_factor.shape[0]
    wide = ones_where(iota((side, 4 * side), 1) % side == iota((side, 4 * side), 0))
    same = iota((4 * side, 4 * side), 0) // side == iota((4 * side, 4 * side), 1) // side
    high, low = [
        jnp.where(same, jnp.concatenate([dot(part, wide)] * 4, axis=0), 0.0).astype(jnp.bfloat16)
        for part in two_parts(right_factor)
    ]
    return jnp.concatenate([high, low, high], axis=0)


def condition_kernel(queries_in, left_in, right_in, low, high, queries, left_factor, right_factor, arrived):
    halves = (low, high)
    copies = [
        pltpu.make_async_copy(source.at[0], target, arrived.at[place])
        for place, (source, target) in enumerate(
            [(left_in, left_factor), (right_in, right_factor), (queries_in, queries)]
        )
    ]
    for copy in copies:
        copy.start()
    side = left_factor.shape[0]
    pairs = side // 2
    copies[0].wait()
    copies[1].wait()
    left = spread_left(left_factor[...])
    right = spread_right(right_factor[...])
    low_half = iota((1, 1, LANES), 2) < side
    per_half = pairs // len(halves)
    copies[2].wait()
    for block in range(queries.shape[0] // GROUP):
        rows = pl.ds(block * GROUP, GROUP)
        straight = jnp.stack(
            [queries[rows, pl.ds(pair * LANES, LANES)].astype(jnp.float32) for pair in range(pairs)]
        )
        swapped = pltpu.roll(straight, side, 2).reshape(pairs, GROUP // ROWS, ROWS, LANES)
        straight = straight.reshape(pairs, GROUP // ROWS, ROWS, LANES)
        columns = []
        for group in (0, 2):
            even = jnp.where(low_half, straight[:, group], swapped[:, group + 1])
            odd = jnp.where(low_half, swapped[:, group], straight[:, group + 1])
            columns.append(jnp.stack([even, odd], axis=1).reshape(side * ROWS, LANES))
        grid = jnp.concatenate(columns, axis=1).astype(jnp.bfloat16)
        halfway = dot(left, jnp.concatenate([grid, grid], axis=0))
        high, low = two_parts(halfway)
        result = dot(jnp.concatenate([high, high, low], axis=1), right)
        result = result.reshape(pairs, 2, ROWS, 2 * LANES)
        groups = []
        for half in range(2):
            even = result[:, 0, :, half * LANES : (half + 1) * LANES]
            odd = result[:, 1, :, half * LANES : (half + 1) * LANES]
            groups.append(jnp.where(low_half, even, pltpu.roll(odd, side, 2)))
            groups.append(jnp.where(low_half, pltpu.roll(even, side, 2), odd))
        done = jnp.concatenate(groups, axis=1).astype(jnp.bfloat16)
        for pair in range(pairs):
            halves[pair // per_half][rows, pl.ds(pair % per_half * LANES, LANES)] = done[pair]


def in_vmem(count):
    return [pl.BlockSpec(memory_space=pltpu.VMEM)] * count


def condition(queries, left_factor, right_factor):
    unused, block_rows, entries = queries.shape
    side = left_factor.shape[1]
    return pl.pallas_call(
        condition_kernel,
        in_specs=[pl.BlockSpec(memory_space=pltpu.HBM)] * 3,
        out_specs=in_vmem(2),
        out_shape=[jax.ShapeDtypeStruct((block_rows, entries // 2), jnp.bfloat16)] * 2,
        scratch_shapes=[
            pltpu.VMEM((block_rows, entries), jnp.bfloat16),
            pltpu.VMEM((side, side), jnp.float32),
            pltpu.VMEM((side, side), jnp.float32),
            pltpu.SemaphoreType.DMA((3,)),
        ],
        compiler_params=pltpu.CompilerParams(vmem_limit_bytes=VMEM),
        cost_estimate=pl.CostEstimate(
            flops=block_rows * entries * 4096, bytes_accessed=queries.size * 4, transcendentals=0
        ),
        name="condition",
    )(*[pltpu.with_memory_space_constraint(value, pltpu.HBM) for value in (queries, left_factor, right_factor)])


STEP = 256


def score_block(queries, store, first, write, arrived=None):
    turned = queries.T
    width = queries.shape[1]

    def one(step, carry):
        place = pl.ds(pl.multiple_of(step * STEP, STEP), STEP)
        if arrived is not None:
            arrived(step)
        value = dot(store[0, place, pl.ds(first, width)], turned)
        write(place, value.T)
        return carry

    lax.fori_loop(0, store.shape[1] // STEP, one, 0)


def own_kernel(queries, far_store, out, store, semaphores):
    def copy_of(step):
        place = pl.ds(pl.multiple_of(step * STEP, STEP), STEP)
        return pltpu.make_async_copy(far_store.at[0, place], store.at[0, place], semaphores.at[step])

    for step in range(store.shape[1] // STEP):
        copy_of(step).start()

    def write(place, value):
        out[:, place] = value

    score_block(queries[...], store, 0, write, lambda step: copy_of(step).wait())


def score_cost(count, width, examples):
    return pl.CostEstimate(
        flops=2 * count * width * examples, bytes_accessed=examples * width * 2, transcendentals=0
    )


def score_own(queries, store):
    rows, entries = queries.shape
    examples = store.shape[1]
    return pl.pallas_call(
        own_kernel,
        in_specs=in_vmem(1) + [pl.BlockSpec(memory_space=pltpu.HBM)],
        out_specs=in_vmem(1)[0],
        out_shape=jax.ShapeDtypeStruct((rows, examples), jnp.float32),
        scratch_shapes=[pltpu.VMEM(store.shape, store.dtype), pltpu.SemaphoreType.DMA((examples // STEP,))],
        compiler_params=pltpu.CompilerParams(vmem_limit_bytes=VMEM),
        cost_estimate=score_cost(rows, entries, examples),
        name="score_own",
    )(queries, pltpu.with_memory_space_constraint(store, pltpu.HBM))


def three_blocks(near, far, last, first):
    return jnp.concatenate([near[:, pl.ds(first, far.shape[1])], far[...], last[...]], axis=0)


def low_kernel(near, far, last, store, out):
    def write(place, value):
        out[:, place] = value

    score_block(three_blocks(near, far, last, 0), store, 0, write)


def score_low(near, far, last, store):
    rows, width = far.shape
    examples = store.shape[1]
    return pl.pallas_call(
        low_kernel,
        in_specs=in_vmem(4),
        out_specs=in_vmem(1)[0],
        out_shape=jax.ShapeDtypeStruct((3 * rows, examples), jnp.float32),
        compiler_params=pltpu.CompilerParams(vmem_limit_bytes=VMEM),
        cost_estimate=score_cost(3 * rows, width, examples),
        name="score_low",
    )(near, far, last, store)


def high_kernel(first, near, far, last, store, own, low, *refs):
    outs, total = refs[:-1], refs[-1]
    rows = own.shape[0]
    total[pl.ds(0, rows), :] = own[...]

    def write(place, value):
        total[pl.ds(rows, 3 * rows), place] = value + low[:, place]

    score_block(three_blocks(near, far, last, first), store, first, write)
    home = lax.bitwise_xor(lax.axis_index("blk"), lax.axis_index("layer"))
    for mask, out in enumerate(outs):
        slot = lax.bitwise_xor(home, mask)
        out[...] = total[pl.ds(pl.multiple_of(slot * rows, rows), rows), :].astype(out.dtype)


def score_high(near, far, last, store, own, low):
    rows, width = far.shape
    examples = store.shape[1]
    return pl.pallas_call(
        functools.partial(high_kernel, near.shape[1] - width),
        in_specs=in_vmem(6),
        out_specs=in_vmem(4),
        out_shape=[
            jax.ShapeDtypeStruct((rows, examples), jnp.bfloat16 if mask else jnp.float32) for mask in range(4)
        ],
        scratch_shapes=[pltpu.VMEM((4 * rows, examples), jnp.float32)],
        compiler_params=pltpu.CompilerParams(vmem_limit_bytes=VMEM),
        cost_estimate=score_cost(3 * rows, width, examples),
        name="score_high",
    )(near, far, last, store, own, low)


def write_rows(total, layers, listed, out):
    scaled = total / jnp.sqrt(jnp.float32(layers))
    tiles_here = out.shape[1] // TILE
    first = lax.axis_index("blk") * tiles_here
    for tile in range(tiles_here):
        hit = jnp.max(jnp.where(listed == first + tile, 1.0, 0.0), axis=1, keepdims=True)
        columns = slice(tile * TILE, (tile + 1) * TILE)
        out[:, columns] = jnp.where(hit > 0.0, scaled[:, columns], 0.0).astype(out.dtype)


def finish_kernel(layers, candidates, *refs):
    parts, out = refs[:-1], refs[-1]
    total = parts[0][...].astype(jnp.float32)
    for part in parts[1:]:
        total = total + part[...].astype(jnp.float32)
    write_rows(total, layers, candidates[...], out)


def finish(parts, candidates, layers):
    return pl.pallas_call(
        functools.partial(finish_kernel, layers),
        in_specs=in_vmem(1 + len(parts)),
        out_specs=in_vmem(1)[0],
        out_shape=jax.ShapeDtypeStruct(parts[0].shape, jnp.bfloat16),
        compiler_params=pltpu.CompilerParams(vmem_limit_bytes=VMEM),
        name="finish",
    )(candidates, *parts)


def permuted(value, axis, target_of):
    count = lax.axis_size(axis)
    return lax.ppermute(value, axis, [(source, target_of(source) % count) for source in range(count)])


def swapped(value, axis, mask):
    return permuted(value, axis, lambda source: source ^ mask)


def on_line(own, store, candidates, layers):
    far = [swapped(half, "blk", 2) for half in own]
    whole = jnp.concatenate(own, axis=1)
    near = swapped(whole, "blk", 1)
    own_scores = score_own(whole, store)
    far[0], own_scores = lax.optimization_barrier((far[0], own_scores))
    last = [swapped(half, "blk", 1) for half in far]
    low_scores = score_low(near, far[0], last[0], store)
    parts = score_high(near, far[1], last[1], store, own_scores, low_scores)
    received = {mask: swapped(parts[mask], "layer", mask) for mask in (3, 2, 1)}
    return finish([parts[0]] + [received[mask] for mask in (1, 2, 3)], candidates, layers)


def on_ring(own, store, candidates, layers):
    count = lax.axis_size("blk")
    moving = jnp.concatenate(own, axis=1)
    rows = moving.shape[0]
    slots = [score_own(moving, store)]
    for _ in range(count - 1):
        moving = permuted(moving, "blk", lambda source: source + 1)
        slots.append(score_own(moving, store))
    turns = lax.rem(lax.axis_index("blk") - jnp.arange(count) + count, count)
    total = jnp.stack(slots)[turns].reshape(layers, count * rows // layers, store.shape[1])
    parts = lax.all_to_all(total.astype(jnp.bfloat16), "layer", 0, 0)
    return finish([parts[layer] for layer in range(layers)], candidates, layers)


def per_device(queries, store, left_factor, right_factor, candidates):
    layers, count = lax.axis_size("layer"), lax.axis_size("blk")
    own = condition(queries, left_factor, right_factor)
    way = on_line if layers == 4 and count == 4 else on_ring
    return way(own, store, candidates, layers)


def solution(mesh):
    placed = (
        P("layer", ("parts", "blk"), None),
        P("layer", ("parts", "blk"), None),
        P("layer", None, None),
        P("layer", None, None),
        P(("parts", "layer"), None),
    )
    return jax.shard_map(
        per_device,
        mesh=mesh,
        in_specs=placed,
        out_specs=P(("parts", "layer"), "blk"),
        check_vma=False,
    )
```

```python
import functools

import jax
import jax.numpy as jnp
from jax import lax
from jax.experimental import pallas as pl
from jax.experimental.pallas import tpu as pltpu
from jax.sharding import PartitionSpec as P

TILE = 128
GROUP = 32
LANES = 128
ROWS = 8
VMEM = 24 * 1024 * 1024


def two_parts(value):
    high = value.astype(jnp.bfloat16)
    low = (value - high.astype(jnp.float32)).astype(jnp.bfloat16)
    return high, low


def iota(shape, axis):
    return lax.broadcasted_iota(jnp.int32, shape, axis)


def dot(left, right):
    return jnp.dot(left, right, preferred_element_type=jnp.float32)


def ones_where(condition):
    return jnp.where(condition, 1.0, 0.0).astype(jnp.bfloat16)


def spread_left(left_factor):
    side = left_factor.shape[0]
    wide = ones_where(iota((side, side * ROWS), 1) // ROWS == iota((side, side * ROWS), 0))
    columns = dot(jnp.concatenate(two_parts(left_factor), axis=0), wide).reshape(2, side, 1, side * ROWS)
    same = iota((1, ROWS, side * ROWS), 1) == iota((1, ROWS, side * ROWS), 2) % ROWS
    parts = [jnp.where(same, columns[part], 0.0).reshape(side * ROWS, side * ROWS) for part in range(2)]
    return jnp.concatenate([part.astype(jnp.bfloat16) for part in parts], axis=1)


def spread_right(right_factor):
    side = right_factor.shape[0]
    wide = ones_where(iota((side, 4 * side), 1) % side == iota((side, 4 * side), 0))
    same = iota((4 * side, 4 * side), 0) // side == iota((4 * side, 4 * side), 1) // side
    high, low = [
        jnp.where(same, jnp.concatenate([dot(part, wide)] * 4, axis=0), 0.0).astype(jnp.bfloat16)
        for part in two_parts(right_factor)
    ]
    return jnp.concatenate([high, low, high], axis=0)


def condition_kernel(rows_each, count, unused, *refs):
    sources, (left_in, right_in), refs = refs[: len(rows_each)], refs[len(rows_each) :][:2], refs[len(rows_each) + 2 + unused :]
    outs, (queries, left_factor, right_factor, arrived) = refs[:count], refs[count:]
    copies = [pltpu.make_async_copy(left_in.at[0], left_factor, arrived.at[0])]
    copies += [pltpu.make_async_copy(right_in.at[0], right_factor, arrived.at[1])]
    start = 0
    for place, (source, rows) in enumerate(zip(sources, rows_each)):
        target = queries.at[pl.ds(start, rows)]
        copies.append(pltpu.make_async_copy(source.at[0], target, arrived.at[2 + place]))
        start += rows
    for copy in copies:
        copy.start()
    side = left_factor.shape[0]
    pairs = side // 2
    copies[0].wait()
    copies[1].wait()
    left = spread_left(left_factor[...])
    right = spread_right(right_factor[...])
    low_half = iota((1, 1, LANES), 2) < side
    for copy in copies[2:]:
        copy.wait()
    for block in range(queries.shape[0] // GROUP):
        rows = pl.ds(block * GROUP, GROUP)
        straight = jnp.stack(
            [queries[rows, pl.ds(pair * LANES, LANES)].astype(jnp.float32) for pair in range(pairs)]
        )
        swapped = pltpu.roll(straight, side, 2).reshape(pairs, GROUP // ROWS, ROWS, LANES)
        straight = straight.reshape(pairs, GROUP // ROWS, ROWS, LANES)
        columns = []
        for group in (0, 2):
            even = jnp.where(low_half, straight[:, group], swapped[:, group + 1])
            odd = jnp.where(low_half, swapped[:, group], straight[:, group + 1])
            columns.append(jnp.stack([even, odd], axis=1).reshape(side * ROWS, LANES))
        grid = jnp.concatenate(columns, axis=1).astype(jnp.bfloat16)
        halfway = dot(left, jnp.concatenate([grid, grid], axis=0))
        high, low = two_parts(halfway)
        result = dot(jnp.concatenate([high, high, low], axis=1), right)
        result = result.reshape(pairs, 2, ROWS, 2 * LANES)
        groups = []
        for half in range(2):
            even = result[:, 0, :, half * LANES : (half + 1) * LANES]
            odd = result[:, 1, :, half * LANES : (half + 1) * LANES]
            groups.append(jnp.where(low_half, even, pltpu.roll(odd, side, 2)))
            groups.append(jnp.where(low_half, pltpu.roll(even, side, 2), odd))
        done = jnp.concatenate(groups, axis=1).astype(jnp.bfloat16)
        for pair in range(pairs):
            outs[0][rows, pl.ds(pair * LANES, LANES)] = done[pair]
        for out in outs[1:]:
            kept = out.shape[0]
            for pair in range(pairs):
                out[:, pl.ds(pair * LANES, LANES)] = done[pair, GROUP - kept :]


def in_vmem(count):
    return [pl.BlockSpec(memory_space=pltpu.VMEM)] * count


def condition(sources, left_factor, right_factor, pieces, others=()):
    rows_each = [source.shape[1] for source in sources]
    block_rows, entries = sum(rows_each), sources[0].shape[2]
    side = left_factor.shape[1]
    shapes = [(block_rows, entries)] + ([(pieces, entries)] if pieces else [])
    operands = (*sources, left_factor, right_factor, *others)
    return pl.pallas_call(
        functools.partial(condition_kernel, rows_each, len(shapes), len(others)),
        in_specs=[pl.BlockSpec(memory_space=pl.ANY)] * len(operands),
        out_specs=in_vmem(len(shapes)),
        out_shape=[jax.ShapeDtypeStruct(shape, jnp.bfloat16) for shape in shapes],
        scratch_shapes=[
            pltpu.VMEM((block_rows, entries), jnp.bfloat16),
            pltpu.VMEM((side, side), jnp.float32),
            pltpu.VMEM((side, side), jnp.float32),
            pltpu.SemaphoreType.DMA((len(operands),)),
        ],
        compiler_params=pltpu.CompilerParams(vmem_limit_bytes=VMEM),
        cost_estimate=pl.CostEstimate(
            flops=block_rows * entries * 4096, bytes_accessed=block_rows * entries * 4, transcendentals=0
        ),
        name="condition",
    )(*operands)


STEP = 256


def score_block(queries, store, first, write, arrived=None):
    turned = queries.T
    width = queries.shape[1]

    def one(step, carry):
        place = pl.ds(pl.multiple_of(step * STEP, STEP), STEP)
        if arrived is not None:
            arrived(step)
        value = dot(store[0, place, pl.ds(first, width)], turned)
        write(place, value.T)
        return carry

    lax.fori_loop(0, store.shape[1] // STEP, one, 0)


def own_kernel(queries, far_store, out, store, semaphores):
    def copy_of(step):
        place = pl.ds(pl.multiple_of(step * STEP, STEP), STEP)
        return pltpu.make_async_copy(far_store.at[0, place], store.at[0, place], semaphores.at[step])

    for step in range(store.shape[1] // STEP):
        copy_of(step).start()

    def write(place, value):
        out[:, place] = value

    score_block(queries[...], store, 0, write, lambda step: copy_of(step).wait())


def score_cost(count, width, examples):
    return pl.CostEstimate(
        flops=2 * count * width * examples, bytes_accessed=examples * width * 2, transcendentals=0
    )


def score_own(queries, store):
    rows, entries = queries.shape
    examples = store.shape[1]
    return pl.pallas_call(
        own_kernel,
        in_specs=in_vmem(1) + [pl.BlockSpec(memory_space=pltpu.HBM)],
        out_specs=in_vmem(1)[0],
        out_shape=jax.ShapeDtypeStruct((rows, examples), jnp.float32),
        scratch_shapes=[pltpu.VMEM(store.shape, store.dtype), pltpu.SemaphoreType.DMA((examples // STEP,))],
        compiler_params=pltpu.CompilerParams(vmem_limit_bytes=VMEM),
        cost_estimate=score_cost(rows, entries, examples),
        name="score_own",
    )(queries, pltpu.with_memory_space_constraint(store, pltpu.HBM))


def all_blocks(own, near, mixed, far, last, first):
    rows, width = last.shape
    entries = pl.ds(first, width)
    slots = [own[:, entries], near[:, entries]]
    slots += [mixed[pl.ds(0, rows), entries], far[:, entries], mixed[pl.ds(rows, rows), entries], last[...]]
    return jnp.concatenate(slots, axis=0)


def low_kernel(own, near, mixed, far, last, store, out):
    def write(place, value):
        out[:, place] = value

    score_block(all_blocks(own, near, mixed, far, last, 0), store, 0, write)


def high_kernel(first, own, near, mixed, far, last, store, low, *refs):
    outs, total = refs[:-1], refs[-1]
    rows = own.shape[0]

    def write(place, value):
        total[:, place] = value + low[:, place]

    score_block(all_blocks(own, near, mixed, far, last, first), store, first, write)
    home = lax.bitwise_xor(lax.axis_index("blk"), lax.axis_index("layer"))
    for mask, out in enumerate(outs):
        slot = lax.bitwise_xor(home, mask)
        out[...] = total[pl.ds(pl.multiple_of(slot * rows, rows), rows), :].astype(out.dtype)


def score_low(own, near, mixed, far, last, store):
    count, width = 4 * own.shape[0], last.shape[1]
    examples = store.shape[1]
    return pl.pallas_call(
        low_kernel,
        in_specs=in_vmem(6),
        out_specs=in_vmem(1)[0],
        out_shape=jax.ShapeDtypeStruct((count, examples), jnp.float32),
        compiler_params=pltpu.CompilerParams(vmem_limit_bytes=VMEM),
        cost_estimate=score_cost(count, width, examples),
        name="score_low",
    )(own, near, mixed, far, last, store)


def score_high(own, near, mixed, far, last, store, low):
    rows, entries = own.shape
    width = last.shape[1]
    examples = store.shape[1]
    return pl.pallas_call(
        functools.partial(high_kernel, entries - width),
        in_specs=in_vmem(7),
        out_specs=in_vmem(4),
        out_shape=[
            jax.ShapeDtypeStruct((rows, examples), jnp.bfloat16 if mask else jnp.float32) for mask in range(4)
        ],
        scratch_shapes=[pltpu.VMEM((4 * rows, examples), jnp.float32)],
        compiler_params=pltpu.CompilerParams(vmem_limit_bytes=VMEM),
        cost_estimate=score_cost(4 * rows, width, examples),
        name="score_high",
    )(own, near, mixed, far, last, store, low)


def keep_kernel(tiles_here, candidates, out):
    listed = candidates[...]
    first = lax.axis_index("blk") * tiles_here
    kept = jnp.zeros(out.shape, jnp.float32)
    for tile in range(tiles_here):
        hit = jnp.max(jnp.where(listed == first + tile, 1.0, 0.0), axis=1, keepdims=True)
        kept = jnp.where(iota(out.shape, 1) == tile, hit, kept)
    out[...] = kept


def kept_tiles(candidates, examples):
    return pl.pallas_call(
        functools.partial(keep_kernel, examples // TILE),
        in_specs=in_vmem(1),
        out_specs=in_vmem(1)[0],
        out_shape=jax.ShapeDtypeStruct((candidates.shape[0], LANES), jnp.float32),
        compiler_params=pltpu.CompilerParams(vmem_limit_bytes=VMEM),
        name="kept_tiles",
    )(candidates)


def finish_kernel(layers, kept, *refs):
    parts, out = refs[:-1], refs[-1]
    for tile in range(out.shape[1] // TILE):
        columns = slice(tile * TILE, (tile + 1) * TILE)
        total = parts[0][:, columns].astype(jnp.float32)
        for part in parts[1:]:
            total = total + part[:, columns].astype(jnp.float32)
        scaled = total / jnp.sqrt(jnp.float32(layers))
        out[:, columns] = jnp.where(kept[:, tile : tile + 1] > 0.0, scaled, 0.0).astype(out.dtype)


def finish(parts, kept, layers):
    return pl.pallas_call(
        functools.partial(finish_kernel, layers),
        in_specs=in_vmem(1 + len(parts)),
        out_specs=in_vmem(1)[0],
        out_shape=jax.ShapeDtypeStruct(parts[0].shape, jnp.bfloat16),
        compiler_params=pltpu.CompilerParams(vmem_limit_bytes=VMEM),
        name="finish",
    )(kept, *parts)


def permuted(value, axis, target_of):
    count = lax.axis_size(axis)
    return lax.ppermute(value, axis, [(source, target_of(source) % count) for source in range(count)])


def swapped(value, axis, mask):
    return permuted(value, axis, lambda source: source ^ mask)


def on_line(queries, store, factors, candidates, layers):
    rows = queries.shape[1] // 2
    raw_far = swapped(queries[:, :rows], "blk", 2)
    raw_near = swapped(queries, "blk", 1)
    stays = [pltpu.with_memory_space_constraint(value, pltpu.HBM) for value in (queries, store)]
    own, leaving = condition(stays[:1], *factors, rows, stays[1:])
    far = swapped(leaving, "blk", 2)
    candidates, own = lax.optimization_barrier((candidates, own))
    kept = kept_tiles(candidates, store.shape[1])
    raw_near, kept = lax.optimization_barrier((raw_near, kept))
    (near,) = condition([raw_near], *factors, 0)
    raw_far, near = lax.optimization_barrier((raw_far, near))
    raw_last = swapped(raw_far, "blk", 1)
    half = far.shape[1] // 2
    last = [swapped(far[:, start : start + half], "blk", 1) for start in (0, half)]
    (mixed,) = condition([raw_far, raw_last], *factors, 0)
    low_scores = score_low(own, near, mixed, far, last[0], store)
    parts = score_high(own, near, mixed, far, last[1], store, low_scores)
    received = {mask: swapped(parts[mask], "layer", mask) for mask in (3, 2, 1)}
    return finish([parts[0]] + [received[mask] for mask in (1, 2, 3)], kept, layers)


def on_ring(queries, store, factors, candidates, layers):
    count = lax.axis_size("blk")
    (moving,) = condition([queries], *factors, 0)
    rows = moving.shape[0]
    slots = [score_own(moving, store)]
    for _ in range(count - 1):
        moving = permuted(moving, "blk", lambda source: source + 1)
        slots.append(score_own(moving, store))
    turns = lax.rem(lax.axis_index("blk") - jnp.arange(count) + count, count)
    total = jnp.stack(slots)[turns].reshape(layers, count * rows // layers, store.shape[1])
    parts = lax.all_to_all(total.astype(jnp.bfloat16), "layer", 0, 0)
    kept = kept_tiles(candidates, store.shape[1])
    return finish([parts[layer] for layer in range(layers)], kept, layers)


def per_device(queries, store, left_factor, right_factor, candidates):
    layers, count = lax.axis_size("layer"), lax.axis_size("blk")
    factors = [pltpu.with_memory_space_constraint(factor, pltpu.HBM) for factor in (left_factor, right_factor)]
    way = on_line if layers == 4 and count == 4 else on_ring
    return way(queries, store, factors, candidates, layers)


def solution(mesh):
    placed = (
        P("layer", ("parts", "blk"), None),
        P("layer", ("parts", "blk"), None),
        P("layer", None, None),
        P("layer", None, None),
        P(("parts", "layer"), None),
    )
    return jax.shard_map(
        per_device,
        mesh=mesh,
        in_specs=placed,
        out_specs=P(("parts", "layer"), "blk"),
        check_vma=False,
    )
```

```python
import functools

import jax
import jax.numpy as jnp
from jax import lax
from jax.experimental import pallas as pl
from jax.experimental.pallas import tpu as pltpu
from jax.sharding import PartitionSpec as P

TILE = 128
GROUP = 32
LANES = 128
ROWS = 8
VMEM = 24 * 1024 * 1024


def two_parts(value):
    high = value.astype(jnp.bfloat16)
    low = (value - high.astype(jnp.float32)).astype(jnp.bfloat16)
    return high, low


def iota(shape, axis):
    return lax.broadcasted_iota(jnp.int32, shape, axis)


def dot(left, right):
    return jnp.dot(left, right, preferred_element_type=jnp.float32)


def ones_where(condition):
    return jnp.where(condition, 1.0, 0.0).astype(jnp.bfloat16)


def spread_left(left_factor):
    side = left_factor.shape[0]
    wide = ones_where(iota((side, side * ROWS), 1) // ROWS == iota((side, side * ROWS), 0))
    columns = dot(jnp.concatenate(two_parts(left_factor), axis=0), wide).reshape(2, side, 1, side * ROWS)
    same = iota((1, ROWS, side * ROWS), 1) == iota((1, ROWS, side * ROWS), 2) % ROWS
    parts = [jnp.where(same, columns[part], 0.0).reshape(side * ROWS, side * ROWS) for part in range(2)]
    return jnp.concatenate([part.astype(jnp.bfloat16) for part in parts], axis=1)


def spread_right(right_factor):
    side = right_factor.shape[0]
    wide = ones_where(iota((side, 4 * side), 1) % side == iota((side, 4 * side), 0))
    same = iota((4 * side, 4 * side), 0) // side == iota((4 * side, 4 * side), 1) // side
    high, low = [
        jnp.where(same, jnp.concatenate([dot(part, wide)] * 4, axis=0), 0.0).astype(jnp.bfloat16)
        for part in two_parts(right_factor)
    ]
    return jnp.concatenate([high, low, high], axis=0)


def condition_kernel(queries_in, left_in, right_in, low, high, queries, left_factor, right_factor, arrived):
    halves = (low, high)
    copies = [
        pltpu.make_async_copy(source.at[0], target, arrived.at[place])
        for place, (source, target) in enumerate(
            [(left_in, left_factor), (right_in, right_factor), (queries_in, queries)]
        )
    ]
    for copy in copies:
        copy.start()
    side = left_factor.shape[0]
    pairs = side // 2
    copies[0].wait()
    copies[1].wait()
    left = spread_left(left_factor[...])
    right = spread_right(right_factor[...])
    low_half = iota((1, 1, LANES), 2) < side
    per_half = pairs // len(halves)
    copies[2].wait()
    for block in range(queries.shape[0] // GROUP):
        rows = pl.ds(block * GROUP, GROUP)
        straight = jnp.stack(
            [queries[rows, pl.ds(pair * LANES, LANES)].astype(jnp.float32) for pair in range(pairs)]
        )
        swapped = pltpu.roll(straight, side, 2).reshape(pairs, GROUP // ROWS, ROWS, LANES)
        straight = straight.reshape(pairs, GROUP // ROWS, ROWS, LANES)
        columns = []
        for group in (0, 2):
            even = jnp.where(low_half, straight[:, group], swapped[:, group + 1])
            odd = jnp.where(low_half, swapped[:, group], straight[:, group + 1])
            columns.append(jnp.stack([even, odd], axis=1).reshape(side * ROWS, LANES))
        grid = jnp.concatenate(columns, axis=1).astype(jnp.bfloat16)
        halfway = dot(left, jnp.concatenate([grid, grid], axis=0))
        high, low = two_parts(halfway)
        result = dot(jnp.concatenate([high, high, low], axis=1), right)
        result = result.reshape(pairs, 2, ROWS, 2 * LANES)
        groups = []
        for half in range(2):
            even = result[:, 0, :, half * LANES : (half + 1) * LANES]
            odd = result[:, 1, :, half * LANES : (half + 1) * LANES]
            groups.append(jnp.where(low_half, even, pltpu.roll(odd, side, 2)))
            groups.append(jnp.where(low_half, pltpu.roll(even, side, 2), odd))
        done = jnp.concatenate(groups, axis=1).astype(jnp.bfloat16)
        for pair in range(pairs):
            halves[pair // per_half][rows, pl.ds(pair % per_half * LANES, LANES)] = done[pair]


def in_vmem(count):
    return [pl.BlockSpec(memory_space=pltpu.VMEM)] * count


def condition(queries, left_factor, right_factor):
    unused, block_rows, entries = queries.shape
    side = left_factor.shape[1]
    return pl.pallas_call(
        condition_kernel,
        in_specs=[pl.BlockSpec(memory_space=pltpu.HBM)] * 3,
        out_specs=in_vmem(2),
        out_shape=[jax.ShapeDtypeStruct((block_rows, entries // 2), jnp.bfloat16)] * 2,
        scratch_shapes=[
            pltpu.VMEM((block_rows, entries), jnp.bfloat16),
            pltpu.VMEM((side, side), jnp.float32),
            pltpu.VMEM((side, side), jnp.float32),
            pltpu.SemaphoreType.DMA((3,)),
        ],
        compiler_params=pltpu.CompilerParams(vmem_limit_bytes=VMEM),
        cost_estimate=pl.CostEstimate(
            flops=block_rows * entries * 4096, bytes_accessed=queries.size * 4, transcendentals=0
        ),
        name="condition",
    )(*[pltpu.with_memory_space_constraint(value, pltpu.HBM) for value in (queries, left_factor, right_factor)])


STEP = 256


def score_block(queries, store, first, write):
    turned = queries.T
    width = queries.shape[1]

    def one(step, carry):
        place = pl.ds(pl.multiple_of(step * STEP, STEP), STEP)
        value = dot(store[0, place, pl.ds(first, width)], turned)
        write(place, value.T)
        return carry

    lax.fori_loop(0, store.shape[1] // STEP, one, 0)


def fetch_kernel(far_store, store, semaphores):
    copies = []
    for step in range(store.shape[1] // STEP):
        place = pl.ds(step * STEP, STEP)
        copies.append(pltpu.make_async_copy(far_store.at[0, place], store.at[0, place], semaphores.at[step]))
    for copy in copies:
        copy.start()
    for copy in copies:
        copy.wait()


def fetch(store):
    return pl.pallas_call(
        fetch_kernel,
        in_specs=[pl.BlockSpec(memory_space=pltpu.HBM)],
        out_specs=in_vmem(1)[0],
        out_shape=jax.ShapeDtypeStruct(store.shape, store.dtype),
        scratch_shapes=[pltpu.SemaphoreType.DMA((store.shape[1] // STEP,))],
        compiler_params=pltpu.CompilerParams(vmem_limit_bytes=VMEM),
        cost_estimate=pl.CostEstimate(flops=0, bytes_accessed=2 * store.size * 2, transcendentals=0),
        name="fetch",
    )(pltpu.with_memory_space_constraint(store, pltpu.HBM))


def score_cost(count, width, examples):
    return pl.CostEstimate(
        flops=2 * count * width * examples, bytes_accessed=examples * width * 2, transcendentals=0
    )


def stacked(blocks):
    return jnp.concatenate([block[...] for block in blocks], axis=0)


def low_kernel(*refs):
    blocks, (store, out) = refs[:-2], refs[-2:]

    def write(place, value):
        out[:, place] = value

    score_block(stacked(blocks), store, 0, write)


def score_low(blocks, store):
    count, width = sum(block.shape[0] for block in blocks), blocks[0].shape[1]
    examples = store.shape[1]
    return pl.pallas_call(
        low_kernel,
        in_specs=in_vmem(len(blocks) + 1),
        out_specs=in_vmem(1)[0],
        out_shape=jax.ShapeDtypeStruct((count, examples), jnp.float32),
        compiler_params=pltpu.CompilerParams(vmem_limit_bytes=VMEM),
        cost_estimate=score_cost(count, width, examples),
        name="score_low",
    )(*blocks, store)


def high_kernel(first, count, *refs):
    blocks, (store, low), outs, total = refs[:count], refs[count : count + 2], refs[count + 2 : -1], refs[-1]

    def write(place, value):
        total[:, place] = value + low[:, place]

    score_block(stacked(blocks), store, first, write)
    rows = blocks[0].shape[0]
    home = lax.bitwise_xor(lax.axis_index("blk"), lax.axis_index("layer"))
    for mask, out in enumerate(outs):
        slot = lax.bitwise_xor(home, mask)
        out[...] = total[pl.ds(pl.multiple_of(slot * rows, rows), rows), :].astype(out.dtype)


def score_high(blocks, store, low):
    rows, width = blocks[0].shape
    count = len(blocks)
    examples = store.shape[1]
    return pl.pallas_call(
        functools.partial(high_kernel, store.shape[2] - width, count),
        in_specs=in_vmem(count + 2),
        out_specs=in_vmem(count),
        out_shape=[
            jax.ShapeDtypeStruct((rows, examples), jnp.bfloat16 if mask else jnp.float32)
            for mask in range(count)
        ],
        scratch_shapes=[pltpu.VMEM((count * rows, examples), jnp.float32)],
        compiler_params=pltpu.CompilerParams(vmem_limit_bytes=VMEM),
        cost_estimate=score_cost(count * rows, width, examples),
        name="score_high",
    )(*blocks, store, low)


def keep_kernel(tiles_here, candidates, out):
    listed = candidates[...]
    first = lax.axis_index("blk") * tiles_here
    kept = jnp.zeros(out.shape, jnp.float32)
    for tile in range(tiles_here):
        hit = jnp.max(jnp.where(listed == first + tile, 1.0, 0.0), axis=1, keepdims=True)
        kept = jnp.where(iota(out.shape, 1) == tile, hit, kept)
    out[...] = kept


def kept_tiles(candidates, examples):
    return pl.pallas_call(
        functools.partial(keep_kernel, examples // TILE),
        in_specs=in_vmem(1),
        out_specs=in_vmem(1)[0],
        out_shape=jax.ShapeDtypeStruct((candidates.shape[0], LANES), jnp.float32),
        compiler_params=pltpu.CompilerParams(vmem_limit_bytes=VMEM),
        name="kept_tiles",
    )(candidates)


def finish_kernel(layers, kept, *refs):
    parts, out = refs[:-1], refs[-1]
    for tile in range(out.shape[1] // TILE):
        columns = slice(tile * TILE, (tile + 1) * TILE)
        total = parts[0][:, columns].astype(jnp.float32)
        for part in parts[1:]:
            total = total + part[:, columns].astype(jnp.float32)
        scaled = total / jnp.sqrt(jnp.float32(layers))
        out[:, columns] = jnp.where(kept[:, tile : tile + 1] > 0.0, scaled, 0.0).astype(out.dtype)


def finish(parts, kept, layers):
    return pl.pallas_call(
        functools.partial(finish_kernel, layers),
        in_specs=in_vmem(1 + len(parts)),
        out_specs=in_vmem(1)[0],
        out_shape=jax.ShapeDtypeStruct(parts[0].shape, jnp.bfloat16),
        compiler_params=pltpu.CompilerParams(vmem_limit_bytes=VMEM),
        name="finish",
    )(kept, *parts)


def permuted(value, axis, target_of):
    count = lax.axis_size(axis)
    return lax.ppermute(value, axis, [(source, target_of(source) % count) for source in range(count)])


def swapped(value, axis, mask):
    return permuted(value, axis, lambda source: source ^ mask)


def on_line(own, store, candidates, layers):
    far = [swapped(half, "blk", 2) for half in own]
    near = [swapped(half, "blk", 1) for half in own]
    candidates, store, own[1] = lax.optimization_barrier((candidates, store, own[1]))
    kept, store = kept_tiles(candidates, store.shape[1]), fetch(store)
    far[0], kept, store = lax.optimization_barrier((far[0], kept, store))
    last = [swapped(half, "blk", 1) for half in far]
    low, high = zip(own, near, far, last)
    parts = score_high(high, store, score_low(low, store))
    received = {mask: swapped(parts[mask], "layer", mask) for mask in (3, 2, 1)}
    return finish([parts[0]] + [received[mask] for mask in (1, 2, 3)], kept, layers)


def on_ring(own, store, candidates, layers):
    count = lax.axis_size("blk")
    moving = jnp.concatenate(own, axis=1)
    rows = moving.shape[0]
    slots = [score_low([moving], store)]
    for _ in range(count - 1):
        moving = permuted(moving, "blk", lambda source: source + 1)
        slots.append(score_low([moving], store))
    turns = lax.rem(lax.axis_index("blk") - jnp.arange(count) + count, count)
    total = jnp.stack(slots)[turns].reshape(layers, count * rows // layers, store.shape[1])
    parts = lax.all_to_all(total.astype(jnp.bfloat16), "layer", 0, 0)
    return finish([parts[layer] for layer in range(layers)], kept_tiles(candidates, store.shape[1]), layers)


def per_device(queries, store, left_factor, right_factor, candidates):
    layers, count = lax.axis_size("layer"), lax.axis_size("blk")
    own = list(condition(queries, left_factor, right_factor))
    way = on_line if layers == 4 and count == 4 else on_ring
    return way(own, store, candidates, layers)


def solution(mesh):
    placed = (
        P("layer", ("parts", "blk"), None),
        P("layer", ("parts", "blk"), None),
        P("layer", None, None),
        P("layer", None, None),
        P(("parts", "layer"), None),
    )
    return jax.shard_map(
        per_device,
        mesh=mesh,
        in_specs=placed,
        out_specs=P(("parts", "layer"), "blk"),
        check_vma=False,
    )
```

```python
import functools

import jax
import jax.numpy as jnp
from jax import lax
from jax.experimental import pallas as pl
from jax.experimental.pallas import tpu as pltpu
from jax.sharding import PartitionSpec as P

TILE = 128
GROUP = 32
LANES = 128
ROWS = 8
VMEM = 24 * 1024 * 1024


def two_parts(value):
    high = value.astype(jnp.bfloat16)
    low = (value - high.astype(jnp.float32)).astype(jnp.bfloat16)
    return high, low


def iota(shape, axis):
    return lax.broadcasted_iota(jnp.int32, shape, axis)


def dot(left, right):
    return jnp.dot(left, right, preferred_element_type=jnp.float32)


def ones_where(condition):
    return jnp.where(condition, 1.0, 0.0).astype(jnp.bfloat16)


def spread_left(left_factor):
    side = left_factor.shape[0]
    wide = ones_where(iota((side, side * ROWS), 1) // ROWS == iota((side, side * ROWS), 0))
    columns = dot(jnp.concatenate(two_parts(left_factor), axis=0), wide).reshape(2, side, 1, side * ROWS)
    same = iota((1, ROWS, side * ROWS), 1) == iota((1, ROWS, side * ROWS), 2) % ROWS
    parts = [jnp.where(same, columns[part], 0.0).reshape(side * ROWS, side * ROWS) for part in range(2)]
    return jnp.concatenate([part.astype(jnp.bfloat16) for part in parts], axis=1)


def spread_right(right_factor):
    side = right_factor.shape[0]
    wide = ones_where(iota((side, 4 * side), 1) % side == iota((side, 4 * side), 0))
    same = iota((4 * side, 4 * side), 0) // side == iota((4 * side, 4 * side), 1) // side
    high, low = [
        jnp.where(same, jnp.concatenate([dot(part, wide)] * 4, axis=0), 0.0).astype(jnp.bfloat16)
        for part in two_parts(right_factor)
    ]
    return jnp.concatenate([high, low, high], axis=0)


def condition_kernel(queries_in, left_in, right_in, low, high, queries, left_factor, right_factor, arrived):
    halves = (low, high)
    copies = [
        pltpu.make_async_copy(source.at[0], target, arrived.at[place])
        for place, (source, target) in enumerate(
            [(left_in, left_factor), (right_in, right_factor), (queries_in, queries)]
        )
    ]
    for copy in copies:
        copy.start()
    side = left_factor.shape[0]
    pairs = side // 2
    copies[0].wait()
    copies[1].wait()
    left = spread_left(left_factor[...])
    right = spread_right(right_factor[...])
    low_half = iota((1, 1, LANES), 2) < side
    per_half = pairs // len(halves)
    copies[2].wait()
    for block in range(queries.shape[0] // GROUP):
        rows = pl.ds(block * GROUP, GROUP)
        straight = jnp.stack(
            [queries[rows, pl.ds(pair * LANES, LANES)].astype(jnp.float32) for pair in range(pairs)]
        )
        swapped = pltpu.roll(straight, side, 2).reshape(pairs, GROUP // ROWS, ROWS, LANES)
        straight = straight.reshape(pairs, GROUP // ROWS, ROWS, LANES)
        columns = []
        for group in (0, 2):
            even = jnp.where(low_half, straight[:, group], swapped[:, group + 1])
            odd = jnp.where(low_half, swapped[:, group], straight[:, group + 1])
            columns.append(jnp.stack([even, odd], axis=1).reshape(side * ROWS, LANES))
        grid = jnp.concatenate(columns, axis=1).astype(jnp.bfloat16)
        halfway = dot(left, jnp.concatenate([grid, grid], axis=0))
        high, low = two_parts(halfway)
        result = dot(jnp.concatenate([high, high, low], axis=1), right)
        result = result.reshape(pairs, 2, ROWS, 2 * LANES)
        groups = []
        for half in range(2):
            even = result[:, 0, :, half * LANES : (half + 1) * LANES]
            odd = result[:, 1, :, half * LANES : (half + 1) * LANES]
            groups.append(jnp.where(low_half, even, pltpu.roll(odd, side, 2)))
            groups.append(jnp.where(low_half, pltpu.roll(even, side, 2), odd))
        done = jnp.concatenate(groups, axis=1).astype(jnp.bfloat16)
        for pair in range(pairs):
            halves[pair // per_half][rows, pl.ds(pair % per_half * LANES, LANES)] = done[pair]


def in_vmem(count):
    return [pl.BlockSpec(memory_space=pltpu.VMEM)] * count


def condition(queries, left_factor, right_factor):
    unused, block_rows, entries = queries.shape
    side = left_factor.shape[1]
    return pl.pallas_call(
        condition_kernel,
        in_specs=[pl.BlockSpec(memory_space=pltpu.HBM)] * 3,
        out_specs=in_vmem(2),
        out_shape=[jax.ShapeDtypeStruct((block_rows, entries // 2), jnp.bfloat16)] * 2,
        scratch_shapes=[
            pltpu.VMEM((block_rows, entries), jnp.bfloat16),
            pltpu.VMEM((side, side), jnp.float32),
            pltpu.VMEM((side, side), jnp.float32),
            pltpu.SemaphoreType.DMA((3,)),
        ],
        compiler_params=pltpu.CompilerParams(vmem_limit_bytes=VMEM),
        cost_estimate=pl.CostEstimate(
            flops=block_rows * entries * 4096, bytes_accessed=queries.size * 4, transcendentals=0
        ),
        name="condition",
    )(*[pltpu.with_memory_space_constraint(value, pltpu.HBM) for value in (queries, left_factor, right_factor)])


STEP = 256


def score_block(queries, store, write):
    turned = queries.T

    def one(step, carry):
        place = pl.ds(pl.multiple_of(step * STEP, STEP), STEP)
        write(place, dot(store[place, :], turned).T)
        return carry

    lax.fori_loop(0, store.shape[0] // STEP, one, 0)


def copies_of(far_store, first, store, semaphores):
    copies = []
    for step in range(store.shape[0] // STEP):
        place = pl.ds(step * STEP, STEP)
        source = far_store.at[0, place, pl.ds(first, store.shape[1])]
        copies.append(pltpu.make_async_copy(source, store.at[place], semaphores.at[step]))
    return copies


def fetch_kernel(far_store, store, semaphores):
    copies = copies_of(far_store, 0, store, semaphores)
    for copy in copies:
        copy.start()
    for copy in copies:
        copy.wait()


def fetch_low(store, width):
    examples = store.shape[1]
    return pl.pallas_call(
        fetch_kernel,
        in_specs=[pl.BlockSpec(memory_space=pltpu.HBM)],
        out_specs=in_vmem(1)[0],
        out_shape=jax.ShapeDtypeStruct((examples, width), store.dtype),
        scratch_shapes=[pltpu.SemaphoreType.DMA((examples // STEP,))],
        compiler_params=pltpu.CompilerParams(vmem_limit_bytes=VMEM),
        cost_estimate=pl.CostEstimate(flops=0, bytes_accessed=4 * examples * width, transcendentals=0),
        name="fetch_low",
    )(store)


def score_cost(count, width, examples):
    return pl.CostEstimate(
        flops=2 * count * width * examples, bytes_accessed=examples * width * 2, transcendentals=0
    )


def stacked(blocks):
    return jnp.concatenate([block[...] for block in blocks], axis=0)


def low_kernel(count, *refs):
    blocks, (low_store, far_store, out, high_store, semaphores) = refs[:count], refs[count:]
    copies = copies_of(far_store, low_store.shape[1], high_store, semaphores)
    for copy in copies:
        copy.start()

    def write(place, value):
        out[:, place] = value

    score_block(stacked(blocks), low_store, write)
    for copy in copies:
        copy.wait()


def score_low(blocks, low_store, far_store):
    count = sum(block.shape[0] for block in blocks)
    examples, width = low_store.shape
    rest = far_store.shape[2] - width
    return pl.pallas_call(
        functools.partial(low_kernel, len(blocks)),
        in_specs=in_vmem(len(blocks) + 1) + [pl.BlockSpec(memory_space=pltpu.HBM)],
        out_specs=in_vmem(2),
        out_shape=[
            jax.ShapeDtypeStruct((count, examples), jnp.float32),
            jax.ShapeDtypeStruct((examples, rest), far_store.dtype),
        ],
        scratch_shapes=[pltpu.SemaphoreType.DMA((examples // STEP,))],
        compiler_params=pltpu.CompilerParams(vmem_limit_bytes=VMEM),
        cost_estimate=score_cost(count, width, examples),
        name="score_low",
    )(*blocks, low_store, far_store)


def high_kernel(count, *refs):
    blocks, (store, low), outs, total = refs[:count], refs[count : count + 2], refs[count + 2 : -1], refs[-1]

    def write(place, value):
        total[:, place] = value + low[:, place]

    score_block(stacked(blocks), store, write)
    rows = blocks[0].shape[0]
    home = lax.bitwise_xor(lax.axis_index("blk"), lax.axis_index("layer"))
    for mask, out in enumerate(outs):
        slot = lax.bitwise_xor(home, mask)
        out[...] = total[pl.ds(pl.multiple_of(slot * rows, rows), rows), :].astype(out.dtype)


def score_high(blocks, store, low):
    rows, width = blocks[0].shape
    count = len(blocks)
    examples = store.shape[0]
    return pl.pallas_call(
        functools.partial(high_kernel, count),
        in_specs=in_vmem(count + 2),
        out_specs=in_vmem(count),
        out_shape=[
            jax.ShapeDtypeStruct((rows, examples), jnp.bfloat16 if mask else jnp.float32)
            for mask in range(count)
        ],
        scratch_shapes=[pltpu.VMEM((count * rows, examples), jnp.float32)],
        compiler_params=pltpu.CompilerParams(vmem_limit_bytes=VMEM),
        cost_estimate=score_cost(count * rows, width, examples),
        name="score_high",
    )(*blocks, store, low)


def keep_kernel(tiles_here, candidates, out):
    listed = candidates[...]
    first = lax.axis_index("blk") * tiles_here
    kept = jnp.zeros(out.shape, jnp.float32)
    for tile in range(tiles_here):
        hit = jnp.max(jnp.where(listed == first + tile, 1.0, 0.0), axis=1, keepdims=True)
        kept = jnp.where(iota(out.shape, 1) == tile, hit, kept)
    out[...] = kept


def kept_tiles(candidates, examples):
    return pl.pallas_call(
        functools.partial(keep_kernel, examples // TILE),
        in_specs=in_vmem(1),
        out_specs=in_vmem(1)[0],
        out_shape=jax.ShapeDtypeStruct((candidates.shape[0], LANES), jnp.float32),
        compiler_params=pltpu.CompilerParams(vmem_limit_bytes=VMEM),
        name="kept_tiles",
    )(candidates)


def finish_kernel(layers, kept, *refs):
    parts, out = refs[:-1], refs[-1]
    for tile in range(out.shape[1] // TILE):
        columns = slice(tile * TILE, (tile + 1) * TILE)
        total = parts[0][:, columns].astype(jnp.float32)
        for part in parts[1:]:
            total = total + part[:, columns].astype(jnp.float32)
        scaled = total / jnp.sqrt(jnp.float32(layers))
        out[:, columns] = jnp.where(kept[:, tile : tile + 1] > 0.0, scaled, 0.0).astype(out.dtype)


def finish(parts, kept, layers):
    return pl.pallas_call(
        functools.partial(finish_kernel, layers),
        in_specs=in_vmem(1 + len(parts)),
        out_specs=in_vmem(1)[0],
        out_shape=jax.ShapeDtypeStruct(parts[0].shape, jnp.bfloat16),
        compiler_params=pltpu.CompilerParams(vmem_limit_bytes=VMEM),
        name="finish",
    )(kept, *parts)


def permuted(value, axis, target_of):
    count = lax.axis_size(axis)
    return lax.ppermute(value, axis, [(source, target_of(source) % count) for source in range(count)])


def swapped(value, axis, mask):
    return permuted(value, axis, lambda source: source ^ mask)


def on_line(own, store, candidates, layers):
    far = [swapped(half, "blk", 2) for half in own]
    near = [swapped(half, "blk", 1) for half in own]
    candidates, own[1] = lax.optimization_barrier((candidates, own[1]))
    kept = kept_tiles(candidates, store.shape[1])
    far[0], kept = lax.optimization_barrier((far[0], kept))
    last = [swapped(half, "blk", 1) for half in far]
    store = pltpu.with_memory_space_constraint(store, pltpu.HBM)
    near[0], far[1], store = lax.optimization_barrier((near[0], far[1], store))
    low, high = zip(own, near, far, last)
    low_scores, high_store = score_low(low, fetch_low(store, own[0].shape[1]), store)
    parts = score_high(high, high_store, low_scores)
    received = {mask: swapped(parts[mask], "layer", mask) for mask in (3, 2, 1)}
    return finish([parts[0]] + [received[mask] for mask in (1, 2, 3)], kept, layers)


def on_ring(own, store, candidates, layers):
    count = lax.axis_size("blk")
    moving = jnp.concatenate(own, axis=1)
    rows = moving.shape[0]

    def scores():
        return lax.dot_general(moving, store[0], (((1,), (1,)), ((), ())), preferred_element_type=jnp.float32)

    slots = [scores()]
    for _ in range(count - 1):
        moving = permuted(moving, "blk", lambda source: source + 1)
        slots.append(scores())
    turns = lax.rem(lax.axis_index("blk") - jnp.arange(count) + count, count)
    total = jnp.stack(slots)[turns].reshape(layers, count * rows // layers, store.shape[1])
    parts = lax.all_to_all(total.astype(jnp.bfloat16), "layer", 0, 0)
    return finish([parts[layer] for layer in range(layers)], kept_tiles(candidates, store.shape[1]), layers)


def per_device(queries, store, left_factor, right_factor, candidates):
    layers, count = lax.axis_size("layer"), lax.axis_size("blk")
    own = list(condition(queries, left_factor, right_factor))
    way = on_line if layers == 4 and count == 4 else on_ring
    return way(own, store, candidates, layers)


def solution(mesh):
    placed = (
        P("layer", ("parts", "blk"), None),
        P("layer", ("parts", "blk"), None),
        P("layer", None, None),
        P("layer", None, None),
        P(("parts", "layer"), None),
    )
    return jax.shard_map(
        per_device,
        mesh=mesh,
        in_specs=placed,
        out_specs=P(("parts", "layer"), "blk"),
        check_vma=False,
    )
```

```python
import functools

import jax
import jax.numpy as jnp
from jax import lax
from jax.experimental import pallas as pl
from jax.experimental.pallas import tpu as pltpu
from jax.sharding import PartitionSpec as P

TILE = 128
GROUP = 32
LANES = 128
ROWS = 8
VMEM = 24 * 1024 * 1024


def two_parts(value):
    high = value.astype(jnp.bfloat16)
    low = (value - high.astype(jnp.float32)).astype(jnp.bfloat16)
    return high, low


def iota(shape, axis):
    return lax.broadcasted_iota(jnp.int32, shape, axis)


def dot(left, right):
    return jnp.dot(left, right, preferred_element_type=jnp.float32)


def ones_where(condition):
    return jnp.where(condition, 1.0, 0.0).astype(jnp.bfloat16)


def spread_left(left_factor):
    side = left_factor.shape[0]
    wide = ones_where(iota((side, side * ROWS), 1) // ROWS == iota((side, side * ROWS), 0))
    columns = dot(jnp.concatenate(two_parts(left_factor), axis=0), wide).reshape(2, side, 1, side * ROWS)
    same = iota((1, ROWS, side * ROWS), 1) == iota((1, ROWS, side * ROWS), 2) % ROWS
    parts = [jnp.where(same, columns[part], 0.0).reshape(side * ROWS, side * ROWS) for part in range(2)]
    return jnp.concatenate([part.astype(jnp.bfloat16) for part in parts], axis=1)


def spread_right(right_factor):
    side = right_factor.shape[0]
    wide = ones_where(iota((side, 4 * side), 1) % side == iota((side, 4 * side), 0))
    same = iota((4 * side, 4 * side), 0) // side == iota((4 * side, 4 * side), 1) // side
    high, low = [
        jnp.where(same, jnp.concatenate([dot(part, wide)] * 4, axis=0), 0.0).astype(jnp.bfloat16)
        for part in two_parts(right_factor)
    ]
    return jnp.concatenate([high, low, high], axis=0)


def condition_kernel(queries_in, left_in, right_in, low, high, queries, left_factor, right_factor, arrived):
    halves = (low, high)
    copies = [
        pltpu.make_async_copy(source.at[0], target, arrived.at[place])
        for place, (source, target) in enumerate(
            [(left_in, left_factor), (right_in, right_factor), (queries_in, queries)]
        )
    ]
    for copy in copies:
        copy.start()
    side = left_factor.shape[0]
    pairs = side // 2
    copies[0].wait()
    copies[1].wait()
    left = spread_left(left_factor[...])
    right = spread_right(right_factor[...])
    low_half = iota((1, 1, LANES), 2) < side
    per_half = pairs // len(halves)
    copies[2].wait()
    for block in range(queries.shape[0] // GROUP):
        rows = pl.ds(block * GROUP, GROUP)
        straight = jnp.stack(
            [queries[rows, pl.ds(pair * LANES, LANES)].astype(jnp.float32) for pair in range(pairs)]
        )
        swapped = pltpu.roll(straight, side, 2).reshape(pairs, GROUP // ROWS, ROWS, LANES)
        straight = straight.reshape(pairs, GROUP // ROWS, ROWS, LANES)
        columns = []
        for group in (0, 2):
            even = jnp.where(low_half, straight[:, group], swapped[:, group + 1])
            odd = jnp.where(low_half, swapped[:, group], straight[:, group + 1])
            columns.append(jnp.stack([even, odd], axis=1).reshape(side * ROWS, LANES))
        grid = jnp.concatenate(columns, axis=1).astype(jnp.bfloat16)
        halfway = dot(left, jnp.concatenate([grid, grid], axis=0))
        high, low = two_parts(halfway)
        result = dot(jnp.concatenate([high, high, low], axis=1), right)
        result = result.reshape(pairs, 2, ROWS, 2 * LANES)
        groups = []
        for half in range(2):
            even = result[:, 0, :, half * LANES : (half + 1) * LANES]
            odd = result[:, 1, :, half * LANES : (half + 1) * LANES]
            groups.append(jnp.where(low_half, even, pltpu.roll(odd, side, 2)))
            groups.append(jnp.where(low_half, pltpu.roll(even, side, 2), odd))
        done = jnp.concatenate(groups, axis=1).astype(jnp.bfloat16)
        for pair in range(pairs):
            halves[pair // per_half][rows, pl.ds(pair % per_half * LANES, LANES)] = done[pair]


def in_vmem(count):
    return [pl.BlockSpec(memory_space=pltpu.VMEM)] * count


def condition(queries, left_factor, right_factor):
    unused, block_rows, entries = queries.shape
    side = left_factor.shape[1]
    return pl.pallas_call(
        condition_kernel,
        in_specs=[pl.BlockSpec(memory_space=pltpu.HBM)] * 3,
        out_specs=in_vmem(2),
        out_shape=[jax.ShapeDtypeStruct((block_rows, entries // 2), jnp.bfloat16)] * 2,
        scratch_shapes=[
            pltpu.VMEM((block_rows, entries), jnp.bfloat16),
            pltpu.VMEM((side, side), jnp.float32),
            pltpu.VMEM((side, side), jnp.float32),
            pltpu.SemaphoreType.DMA((3,)),
        ],
        compiler_params=pltpu.CompilerParams(vmem_limit_bytes=VMEM),
        cost_estimate=pl.CostEstimate(
            flops=block_rows * entries * 4096, bytes_accessed=queries.size * 4, transcendentals=0
        ),
        name="condition",
    )(*[pltpu.with_memory_space_constraint(value, pltpu.HBM) for value in (queries, left_factor, right_factor)])


STEP = 256


def score_block(queries, store, first, write, arrived=None, step_rows=STEP):
    turned = queries.T
    width = queries.shape[1]

    def one(step, carry):
        place = pl.ds(pl.multiple_of(step * step_rows, step_rows), step_rows)
        if arrived is not None:
            arrived(step)
        value = dot(store[0, place, pl.ds(first, width)], turned)
        write(place, value.T)
        return carry

    lax.fori_loop(0, store.shape[1] // step_rows, one, 0)


def own_kernel(queries, far_store, out, store, semaphores):
    def copy_of(step):
        place = pl.ds(pl.multiple_of(step * STEP, STEP), STEP)
        return pltpu.make_async_copy(far_store.at[0, place], store.at[0, place], semaphores.at[step])

    for step in range(store.shape[1] // STEP):
        copy_of(step).start()

    def write(place, value):
        out[:, place] = value

    score_block(queries[...], store, 0, write, lambda step: copy_of(step).wait())


def score_cost(count, width, examples):
    return pl.CostEstimate(
        flops=2 * count * width * examples, bytes_accessed=examples * width * 2, transcendentals=0
    )


def score_own(queries, store):
    rows, entries = queries.shape
    examples = store.shape[1]
    return pl.pallas_call(
        own_kernel,
        in_specs=in_vmem(1) + [pl.BlockSpec(memory_space=pltpu.HBM)],
        out_specs=in_vmem(1)[0],
        out_shape=jax.ShapeDtypeStruct((rows, examples), jnp.float32),
        scratch_shapes=[pltpu.VMEM(store.shape, store.dtype), pltpu.SemaphoreType.DMA((examples // STEP,))],
        compiler_params=pltpu.CompilerParams(vmem_limit_bytes=VMEM),
        cost_estimate=score_cost(rows, entries, examples),
        name="score_own",
    )(queries, pltpu.with_memory_space_constraint(store, pltpu.HBM))


def three_blocks(near, far, last, first):
    return jnp.concatenate([near[:, pl.ds(first, far.shape[1])], far[...], last[...]], axis=0)


def low_kernel(near, far, last, store, out):
    def write(place, value):
        out[:, place] = value

    score_block(three_blocks(near, far, last, 0), store, 0, write, step_rows=store.shape[1])


def score_low(near, far, last, store):
    rows, width = far.shape
    examples = store.shape[1]
    return pl.pallas_call(
        low_kernel,
        in_specs=in_vmem(4),
        out_specs=in_vmem(1)[0],
        out_shape=jax.ShapeDtypeStruct((3 * rows, examples), jnp.float32),
        compiler_params=pltpu.CompilerParams(vmem_limit_bytes=VMEM),
        cost_estimate=score_cost(3 * rows, width, examples),
        name="score_low",
    )(near, far, last, store)


def high_kernel(first, near, far, last, store, own, low, *refs):
    outs, total = refs[:-1], refs[-1]
    rows = own.shape[0]
    total[pl.ds(0, rows), :] = own[...]

    def write(place, value):
        total[pl.ds(rows, 3 * rows), place] = value + low[:, place]

    score_block(three_blocks(near, far, last, first), store, first, write, step_rows=store.shape[1])
    home = lax.bitwise_xor(lax.axis_index("blk"), lax.axis_index("layer"))
    for mask, out in enumerate(outs):
        slot = lax.bitwise_xor(home, mask)
        out[...] = total[pl.ds(pl.multiple_of(slot * rows, rows), rows), :].astype(out.dtype)


def score_high(near, far, last, store, own, low):
    rows, width = far.shape
    examples = store.shape[1]
    return pl.pallas_call(
        functools.partial(high_kernel, near.shape[1] - width),
        in_specs=in_vmem(6),
        out_specs=in_vmem(4),
        out_shape=[
            jax.ShapeDtypeStruct((rows, examples), jnp.bfloat16 if mask else jnp.float32) for mask in range(4)
        ],
        scratch_shapes=[pltpu.VMEM((4 * rows, examples), jnp.float32)],
        compiler_params=pltpu.CompilerParams(vmem_limit_bytes=VMEM),
        cost_estimate=score_cost(3 * rows, width, examples),
        name="score_high",
    )(near, far, last, store, own, low)


def write_rows(total, layers, listed, out):
    scaled = total / jnp.sqrt(jnp.float32(layers))
    tiles_here = out.shape[1] // TILE
    first = lax.axis_index("blk") * tiles_here
    for tile in range(tiles_here):
        hit = jnp.max(jnp.where(listed == first + tile, 1.0, 0.0), axis=1, keepdims=True)
        columns = slice(tile * TILE, (tile + 1) * TILE)
        out[:, columns] = jnp.where(hit > 0.0, scaled[:, columns], 0.0).astype(out.dtype)


def finish_kernel(layers, candidates, *refs):
    parts, out = refs[:-1], refs[-1]
    total = parts[0][...].astype(jnp.float32)
    for part in parts[1:]:
        total = total + part[...].astype(jnp.float32)
    write_rows(total, layers, candidates[...], out)


def finish(parts, candidates, layers):
    return pl.pallas_call(
        functools.partial(finish_kernel, layers),
        in_specs=in_vmem(1 + len(parts)),
        out_specs=in_vmem(1)[0],
        out_shape=jax.ShapeDtypeStruct(parts[0].shape, jnp.bfloat16),
        compiler_params=pltpu.CompilerParams(vmem_limit_bytes=VMEM),
        name="finish",
    )(candidates, *parts)


def permuted(value, axis, target_of):
    count = lax.axis_size(axis)
    return lax.ppermute(value, axis, [(source, target_of(source) % count) for source in range(count)])


def swapped(value, axis, mask):
    return permuted(value, axis, lambda source: source ^ mask)


def on_line(own, store, candidates, layers):
    far = [swapped(half, "blk", 2) for half in own]
    whole = jnp.concatenate(own, axis=1)
    near = swapped(whole, "blk", 1)
    own_scores = score_own(whole, store)
    far[0], own_scores = lax.optimization_barrier((far[0], own_scores))
    last = [swapped(half, "blk", 1) for half in far]
    low_scores = score_low(near, far[0], last[0], store)
    parts = score_high(near, far[1], last[1], store, own_scores, low_scores)
    received = {mask: swapped(parts[mask], "layer", mask) for mask in (3, 2, 1)}
    return finish([parts[0]] + [received[mask] for mask in (1, 2, 3)], candidates, layers)


def on_ring(own, store, candidates, layers):
    count = lax.axis_size("blk")
    moving = jnp.concatenate(own, axis=1)
    rows = moving.shape[0]
    slots = [score_own(moving, store)]
    for _ in range(count - 1):
        moving = permuted(moving, "blk", lambda source: source + 1)
        slots.append(score_own(moving, store))
    turns = lax.rem(lax.axis_index("blk") - jnp.arange(count) + count, count)
    total = jnp.stack(slots)[turns].reshape(layers, count * rows // layers, store.shape[1])
    parts = lax.all_to_all(total.astype(jnp.bfloat16), "layer", 0, 0)
    return finish([parts[layer] for layer in range(layers)], candidates, layers)


def per_device(queries, store, left_factor, right_factor, candidates):
    layers, count = lax.axis_size("layer"), lax.axis_size("blk")
    own = condition(queries, left_factor, right_factor)
    way = on_line if layers == 4 and count == 4 else on_ring
    return way(own, store, candidates, layers)


def solution(mesh):
    placed = (
        P("layer", ("parts", "blk"), None),
        P("layer", ("parts", "blk"), None),
        P("layer", None, None),
        P("layer", None, None),
        P(("parts", "layer"), None),
    )
    return jax.shard_map(
        per_device,
        mesh=mesh,
        in_specs=placed,
        out_specs=P(("parts", "layer"), "blk"),
        check_vma=False,
    )
```

```python
import functools

import jax
import jax.numpy as jnp
from jax import lax
from jax.experimental import pallas as pl
from jax.experimental.pallas import tpu as pltpu
from jax.sharding import PartitionSpec as P

TILE = 128
GROUP = 32
LANES = 128
ROWS = 8
VMEM = 24 * 1024 * 1024


def two_parts(value):
    high = value.astype(jnp.bfloat16)
    low = (value - high.astype(jnp.float32)).astype(jnp.bfloat16)
    return high, low


def iota(shape, axis):
    return lax.broadcasted_iota(jnp.int32, shape, axis)


def dot(left, right):
    return jnp.dot(left, right, preferred_element_type=jnp.float32)


def ones_where(condition):
    return jnp.where(condition, 1.0, 0.0).astype(jnp.bfloat16)


def spread_left(left_factor):
    side = left_factor.shape[0]
    wide = ones_where(iota((side, side * ROWS), 1) // ROWS == iota((side, side * ROWS), 0))
    columns = dot(jnp.concatenate(two_parts(left_factor), axis=0), wide).reshape(2, side, 1, side * ROWS)
    same = iota((1, ROWS, side * ROWS), 1) == iota((1, ROWS, side * ROWS), 2) % ROWS
    parts = [jnp.where(same, columns[part], 0.0).reshape(side * ROWS, side * ROWS) for part in range(2)]
    return jnp.concatenate([part.astype(jnp.bfloat16) for part in parts], axis=1)


def spread_right(right_factor):
    side = right_factor.shape[0]
    wide = ones_where(iota((side, 4 * side), 1) % side == iota((side, 4 * side), 0))
    same = iota((4 * side, 4 * side), 0) // side == iota((4 * side, 4 * side), 1) // side
    high, low = [
        jnp.where(same, jnp.concatenate([dot(part, wide)] * 4, axis=0), 0.0).astype(jnp.bfloat16)
        for part in two_parts(right_factor)
    ]
    return jnp.concatenate([high, low, high], axis=0)


def condition_kernel(queries_in, left_in, right_in, low, high, queries, left_factor, right_factor, arrived):
    halves = (low, high)
    copies = [
        pltpu.make_async_copy(source.at[0], target, arrived.at[place])
        for place, (source, target) in enumerate(
            [(left_in, left_factor), (right_in, right_factor), (queries_in, queries)]
        )
    ]
    for copy in copies:
        copy.start()
    side = left_factor.shape[0]
    pairs = side // 2
    copies[0].wait()
    copies[1].wait()
    left = spread_left(left_factor[...])
    right = spread_right(right_factor[...])
    low_half = iota((1, 1, LANES), 2) < side
    per_half = pairs // len(halves)
    copies[2].wait()
    for block in range(queries.shape[0] // GROUP):
        rows = pl.ds(block * GROUP, GROUP)
        straight = jnp.stack(
            [queries[rows, pl.ds(pair * LANES, LANES)].astype(jnp.float32) for pair in range(pairs)]
        )
        swapped = pltpu.roll(straight, side, 2).reshape(pairs, GROUP // ROWS, ROWS, LANES)
        straight = straight.reshape(pairs, GROUP // ROWS, ROWS, LANES)
        columns = []
        for group in (0, 2):
            even = jnp.where(low_half, straight[:, group], swapped[:, group + 1])
            odd = jnp.where(low_half, swapped[:, group], straight[:, group + 1])
            columns.append(jnp.stack([even, odd], axis=1).reshape(side * ROWS, LANES))
        grid = jnp.concatenate(columns, axis=1).astype(jnp.bfloat16)
        halfway = dot(left, jnp.concatenate([grid, grid], axis=0))
        high, low = two_parts(halfway)
        result = dot(jnp.concatenate([high, high, low], axis=1), right)
        result = result.reshape(pairs, 2, ROWS, 2 * LANES)
        groups = []
        for half in range(2):
            even = result[:, 0, :, half * LANES : (half + 1) * LANES]
            odd = result[:, 1, :, half * LANES : (half + 1) * LANES]
            groups.append(jnp.where(low_half, even, pltpu.roll(odd, side, 2)))
            groups.append(jnp.where(low_half, pltpu.roll(even, side, 2), odd))
        done = jnp.concatenate(groups, axis=1).astype(jnp.bfloat16)
        for pair in range(pairs):
            halves[pair // per_half][rows, pl.ds(pair % per_half * LANES, LANES)] = done[pair]


def in_vmem(count):
    return [pl.BlockSpec(memory_space=pltpu.VMEM)] * count


def condition(queries, left_factor, right_factor):
    unused, block_rows, entries = queries.shape
    side = left_factor.shape[1]
    return pl.pallas_call(
        condition_kernel,
        in_specs=[pl.BlockSpec(memory_space=pltpu.HBM)] * 3,
        out_specs=in_vmem(2),
        out_shape=[jax.ShapeDtypeStruct((block_rows, entries // 2), jnp.bfloat16)] * 2,
        scratch_shapes=[
            pltpu.VMEM((block_rows, entries), jnp.bfloat16),
            pltpu.VMEM((side, side), jnp.float32),
            pltpu.VMEM((side, side), jnp.float32),
            pltpu.SemaphoreType.DMA((3,)),
        ],
        compiler_params=pltpu.CompilerParams(vmem_limit_bytes=VMEM),
        cost_estimate=pl.CostEstimate(
            flops=block_rows * entries * 4096, bytes_accessed=queries.size * 4, transcendentals=0
        ),
        name="condition",
    )(*[pltpu.with_memory_space_constraint(value, pltpu.HBM) for value in (queries, left_factor, right_factor)])


STEP = 256
MASKS = (0, 3, 2, 1)


def score_block(queries, store, first, write, arrived=None, step_rows=STEP):
    turned = queries.T
    width = queries.shape[1]

    def one(step, carry):
        place = pl.ds(pl.multiple_of(step * step_rows, step_rows), step_rows)
        if arrived is not None:
            arrived(step)
        value = dot(store[0, place, pl.ds(first, width)], turned)
        write(place, value.T)
        return carry

    lax.fori_loop(0, store.shape[1] // step_rows, one, 0)


def own_kernel(queries, far_store, out, store, semaphores):
    def copy_of(step):
        place = pl.ds(pl.multiple_of(step * STEP, STEP), STEP)
        return pltpu.make_async_copy(far_store.at[0, place], store.at[0, place], semaphores.at[step])

    for step in range(store.shape[1] // STEP):
        copy_of(step).start()

    def write(place, value):
        out[:, place] = value

    score_block(queries[...], store, 0, write, lambda step: copy_of(step).wait())


def score_cost(count, width, examples):
    return pl.CostEstimate(
        flops=2 * count * width * examples, bytes_accessed=examples * width * 2, transcendentals=0
    )


def score_own(queries, store):
    rows, entries = queries.shape
    examples = store.shape[1]
    return pl.pallas_call(
        own_kernel,
        in_specs=in_vmem(1) + [pl.BlockSpec(memory_space=pltpu.HBM)],
        out_specs=in_vmem(1)[0],
        out_shape=jax.ShapeDtypeStruct((rows, examples), jnp.float32),
        scratch_shapes=[pltpu.VMEM(store.shape, store.dtype), pltpu.SemaphoreType.DMA((examples // STEP,))],
        compiler_params=pltpu.CompilerParams(vmem_limit_bytes=VMEM),
        cost_estimate=score_cost(rows, entries, examples),
        name="score_own",
    )(queries, pltpu.with_memory_space_constraint(store, pltpu.HBM))


def three_blocks(near, far, last, first):
    return jnp.concatenate([near[:, pl.ds(first, far.shape[1])], far[...], last[...]], axis=0)


def low_kernel(near, far, last, store, out):
    def write(place, value):
        out[:, place] = value

    score_block(three_blocks(near, far, last, 0), store, 0, write, step_rows=store.shape[1])


def score_low(near, far, last, store):
    rows, width = far.shape
    examples = store.shape[1]
    return pl.pallas_call(
        low_kernel,
        in_specs=in_vmem(4),
        out_specs=in_vmem(1)[0],
        out_shape=jax.ShapeDtypeStruct((3 * rows, examples), jnp.float32),
        compiler_params=pltpu.CompilerParams(vmem_limit_bytes=VMEM),
        cost_estimate=score_cost(3 * rows, width, examples),
        name="score_low",
    )(near, far, last, store)


def high_kernel(first, near, far, last, store, own, low, *refs):
    outs, total = refs[:-1], refs[-1]
    rows = own.shape[0]
    total[pl.ds(0, rows), :] = own[...]

    def write(place, value):
        total[pl.ds(rows, 3 * rows), place] = value + low[:, place]

    score_block(three_blocks(near, far, last, first), store, first, write, step_rows=store.shape[1])
    home = lax.bitwise_xor(lax.axis_index("blk"), lax.axis_index("layer"))
    for mask, out in zip(MASKS, outs):
        slot = lax.bitwise_xor(home, mask)
        out[...] = total[pl.ds(pl.multiple_of(slot * rows, rows), rows), :].astype(out.dtype)


def score_high(near, far, last, store, own, low):
    rows, width = far.shape
    examples = store.shape[1]
    return pl.pallas_call(
        functools.partial(high_kernel, near.shape[1] - width),
        in_specs=in_vmem(6),
        out_specs=in_vmem(4),
        out_shape=[
            jax.ShapeDtypeStruct((rows, examples), jnp.bfloat16 if mask else jnp.float32) for mask in MASKS
        ],
        scratch_shapes=[pltpu.VMEM((4 * rows, examples), jnp.float32)],
        compiler_params=pltpu.CompilerParams(vmem_limit_bytes=VMEM),
        cost_estimate=score_cost(3 * rows, width, examples),
        name="score_high",
    )(near, far, last, store, own, low)


def write_rows(total, layers, listed, out):
    scaled = total / jnp.sqrt(jnp.float32(layers))
    tiles_here = out.shape[1] // TILE
    first = lax.axis_index("blk") * tiles_here
    for tile in range(tiles_here):
        hit = jnp.max(jnp.where(listed == first + tile, 1.0, 0.0), axis=1, keepdims=True)
        columns = slice(tile * TILE, (tile + 1) * TILE)
        out[:, columns] = jnp.where(hit > 0.0, scaled[:, columns], 0.0).astype(out.dtype)


def finish_kernel(layers, candidates, *refs):
    parts, out = refs[:-1], refs[-1]
    total = parts[0][...].astype(jnp.float32)
    for part in parts[1:]:
        total = total + part[...].astype(jnp.float32)
    write_rows(total, layers, candidates[...], out)


def finish(parts, candidates, layers):
    return pl.pallas_call(
        functools.partial(finish_kernel, layers),
        in_specs=in_vmem(1 + len(parts)),
        out_specs=in_vmem(1)[0],
        out_shape=jax.ShapeDtypeStruct(parts[0].shape, jnp.bfloat16),
        compiler_params=pltpu.CompilerParams(vmem_limit_bytes=VMEM),
        name="finish",
    )(candidates, *parts)


def permuted(value, axis, target_of):
    count = lax.axis_size(axis)
    return lax.ppermute(value, axis, [(source, target_of(source) % count) for source in range(count)])


def swapped(value, axis, mask):
    return permuted(value, axis, lambda source: source ^ mask)


def on_line(own, store, candidates, layers):
    far = [swapped(half, "blk", 2) for half in own]
    whole = jnp.concatenate(own, axis=1)
    near = swapped(whole, "blk", 1)
    own_scores = score_own(whole, store)
    far[0], own_scores = lax.optimization_barrier((far[0], own_scores))
    last = [swapped(half, "blk", 1) for half in far]
    low_scores = score_low(near, far[0], last[0], store)
    parts = score_high(near, far[1], last[1], store, own_scores, low_scores)
    received = [swapped(part, "layer", mask) for mask, part in zip(MASKS[1:], parts[1:])]
    return finish([parts[0]] + received, candidates, layers)


def on_ring(own, store, candidates, layers):
    count = lax.axis_size("blk")
    moving = jnp.concatenate(own, axis=1)
    rows = moving.shape[0]
    slots = [score_own(moving, store)]
    for _ in range(count - 1):
        moving = permuted(moving, "blk", lambda source: source + 1)
        slots.append(score_own(moving, store))
    turns = lax.rem(lax.axis_index("blk") - jnp.arange(count) + count, count)
    total = jnp.stack(slots)[turns].reshape(layers, count * rows // layers, store.shape[1])
    parts = lax.all_to_all(total.astype(jnp.bfloat16), "layer", 0, 0)
    return finish([parts[layer] for layer in range(layers)], candidates, layers)


def per_device(queries, store, left_factor, right_factor, candidates):
    layers, count = lax.axis_size("layer"), lax.axis_size("blk")
    own = condition(queries, left_factor, right_factor)
    way = on_line if layers == 4 and count == 4 else on_ring
    return way(own, store, candidates, layers)


def solution(mesh):
    placed = (
        P("layer", ("parts", "blk"), None),
        P("layer", ("parts", "blk"), None),
        P("layer", None, None),
        P("layer", None, None),
        P(("parts", "layer"), None),
    )
    return jax.shard_map(
        per_device,
        mesh=mesh,
        in_specs=placed,
        out_specs=P(("parts", "layer"), "blk"),
        check_vma=False,
    )
```

```python
import functools

import jax
import jax.numpy as jnp
from jax import lax
from jax.experimental import pallas as pl
from jax.experimental.pallas import tpu as pltpu
from jax.sharding import PartitionSpec as P

TILE = 128
GROUP = 32
LANES = 128
ROWS = 8
VMEM = 24 * 1024 * 1024


def two_parts(value):
    high = value.astype(jnp.bfloat16)
    low = (value - high.astype(jnp.float32)).astype(jnp.bfloat16)
    return high, low


def iota(shape, axis):
    return lax.broadcasted_iota(jnp.int32, shape, axis)


def dot(left, right):
    return jnp.dot(left, right, preferred_element_type=jnp.float32)


def ones_where(condition):
    return jnp.where(condition, 1.0, 0.0).astype(jnp.bfloat16)


def spread_left(left_factor, first, count):
    side = left_factor.shape[0]
    wide = ones_where(iota((side, side * ROWS), 1) // ROWS == iota((side, side * ROWS), 0))
    parts = [part[first : first + count] for part in two_parts(left_factor)]
    columns = dot(jnp.concatenate(parts, axis=0), wide).reshape(2, count, 1, side * ROWS)
    same = iota((1, ROWS, side * ROWS), 1) == iota((1, ROWS, side * ROWS), 2) % ROWS
    parts = [jnp.where(same, columns[part], 0.0).reshape(count * ROWS, side * ROWS) for part in range(2)]
    return jnp.concatenate([part.astype(jnp.bfloat16) for part in parts], axis=1)


def spread_right(right_factor):
    side = right_factor.shape[0]
    wide = ones_where(iota((side, 4 * side), 1) % side == iota((side, 4 * side), 0))
    same = iota((4 * side, 4 * side), 0) // side == iota((4 * side, 4 * side), 1) // side
    high, low = [
        jnp.where(same, jnp.concatenate([dot(part, wide)] * 4, axis=0), 0.0).astype(jnp.bfloat16)
        for part in two_parts(right_factor)
    ]
    return jnp.concatenate([high, low, high], axis=0)


def condition_kernel(first, count, queries_in, left_in, right_in, out, queries, left_factor, right_factor, arrived):
    copies = [
        pltpu.make_async_copy(source.at[0], target, arrived.at[place])
        for place, (source, target) in enumerate(
            [(left_in, left_factor), (right_in, right_factor), (queries_in, queries)]
        )
    ]
    for copy in copies:
        copy.start()
    side = left_factor.shape[0]
    pairs = side // 2
    copies[0].wait()
    copies[1].wait()
    left = spread_left(left_factor[...], first, count)
    right = spread_right(right_factor[...])
    low_half = iota((1, 1, LANES), 2) < side
    copies[2].wait()
    for block in range(queries.shape[0] // GROUP):
        rows = pl.ds(block * GROUP, GROUP)
        straight = jnp.stack(
            [queries[rows, pl.ds(pair * LANES, LANES)].astype(jnp.float32) for pair in range(pairs)]
        )
        swapped = pltpu.roll(straight, side, 2).reshape(pairs, GROUP // ROWS, ROWS, LANES)
        straight = straight.reshape(pairs, GROUP // ROWS, ROWS, LANES)
        columns = []
        for group in (0, 2):
            even = jnp.where(low_half, straight[:, group], swapped[:, group + 1])
            odd = jnp.where(low_half, swapped[:, group], straight[:, group + 1])
            columns.append(jnp.stack([even, odd], axis=1).reshape(side * ROWS, LANES))
        grid = jnp.concatenate(columns, axis=1).astype(jnp.bfloat16)
        halfway = dot(left, jnp.concatenate([grid, grid], axis=0))
        high, low = two_parts(halfway)
        result = dot(jnp.concatenate([high, high, low], axis=1), right)
        result = result.reshape(count // 2, 2, ROWS, 2 * LANES)
        groups = []
        for half in range(2):
            even = result[:, 0, :, half * LANES : (half + 1) * LANES]
            odd = result[:, 1, :, half * LANES : (half + 1) * LANES]
            groups.append(jnp.where(low_half, even, pltpu.roll(odd, side, 2)))
            groups.append(jnp.where(low_half, pltpu.roll(even, side, 2), odd))
        done = jnp.concatenate(groups, axis=1).astype(jnp.bfloat16)
        for pair in range(count // 2):
            out[rows, pl.ds(pair * LANES, LANES)] = done[pair]


def in_vmem(count):
    return [pl.BlockSpec(memory_space=pltpu.VMEM)] * count


def condition(queries, left_factor, right_factor, half):
    unused, block_rows, entries = queries.shape
    side = left_factor.shape[1]
    operands = [pltpu.with_memory_space_constraint(value, pltpu.HBM) for value in (queries, left_factor, right_factor)]
    return pl.pallas_call(
        functools.partial(condition_kernel, half * side // 2, side // 2),
        in_specs=[pl.BlockSpec(memory_space=pltpu.HBM)] * 3,
        out_specs=in_vmem(1)[0],
        out_shape=jax.ShapeDtypeStruct((block_rows, entries // 2), jnp.bfloat16),
        scratch_shapes=[
            pltpu.VMEM((block_rows, entries), jnp.bfloat16),
            pltpu.VMEM((side, side), jnp.float32),
            pltpu.VMEM((side, side), jnp.float32),
            pltpu.SemaphoreType.DMA((3,)),
        ],
        compiler_params=pltpu.CompilerParams(vmem_limit_bytes=VMEM),
        cost_estimate=pl.CostEstimate(
            flops=block_rows * entries * 4096, bytes_accessed=queries.size * 4, transcendentals=0
        ),
        name="condition",
    )(*operands)


STEP = 256


def score_block(queries, store, first, write, arrived=None, step_rows=STEP):
    turned = queries.T
    width = queries.shape[1]

    def one(step, carry):
        place = pl.ds(pl.multiple_of(step * step_rows, step_rows), step_rows)
        if arrived is not None:
            arrived(step)
        value = dot(store[0, place, pl.ds(first, width)], turned)
        write(place, value.T)
        return carry

    lax.fori_loop(0, store.shape[1] // step_rows, one, 0)


def own_kernel(low, high, far_store, out, store, semaphores):
    def copy_of(step):
        place = pl.ds(pl.multiple_of(step * STEP, STEP), STEP)
        return pltpu.make_async_copy(far_store.at[0, place], store.at[0, place], semaphores.at[step])

    for step in range(store.shape[1] // STEP):
        copy_of(step).start()

    def write(place, value):
        out[:, place] = value

    queries = jnp.concatenate([low[...], high[...]], axis=1)
    score_block(queries, store, 0, write, lambda step: copy_of(step).wait())


def score_cost(count, width, examples):
    return pl.CostEstimate(
        flops=2 * count * width * examples, bytes_accessed=examples * width * 2, transcendentals=0
    )


def score_own(halves, store):
    rows, entries = halves[0].shape[0], store.shape[2]
    examples = store.shape[1]
    return pl.pallas_call(
        own_kernel,
        in_specs=in_vmem(2) + [pl.BlockSpec(memory_space=pltpu.HBM)],
        out_specs=in_vmem(1)[0],
        out_shape=jax.ShapeDtypeStruct((rows, examples), jnp.float32),
        scratch_shapes=[pltpu.VMEM(store.shape, store.dtype), pltpu.SemaphoreType.DMA((examples // STEP,))],
        compiler_params=pltpu.CompilerParams(vmem_limit_bytes=VMEM),
        cost_estimate=score_cost(rows, entries, examples),
        name="score_own",
    )(*halves, pltpu.with_memory_space_constraint(store, pltpu.HBM))


def stacked(*blocks):
    return jnp.concatenate([block[...] for block in blocks], axis=0)


def low_kernel(near, far, last, store, out):
    def write(place, value):
        out[:, place] = value

    score_block(stacked(near, far, last), store, 0, write, step_rows=store.shape[1])


def score_low(near, far, last, store):
    rows, width = far.shape
    examples = store.shape[1]
    return pl.pallas_call(
        low_kernel,
        in_specs=in_vmem(4),
        out_specs=in_vmem(1)[0],
        out_shape=jax.ShapeDtypeStruct((3 * rows, examples), jnp.float32),
        compiler_params=pltpu.CompilerParams(vmem_limit_bytes=VMEM),
        cost_estimate=score_cost(3 * rows, width, examples),
        name="score_low",
    )(near, far, last, store)


def high_kernel(first, near, far, last, store, own, low, *refs):
    outs, total = refs[:-1], refs[-1]
    rows = own.shape[0]
    total[pl.ds(0, rows), :] = own[...]

    def write(place, value):
        total[pl.ds(rows, 3 * rows), place] = value + low[:, place]

    score_block(stacked(near, far, last), store, first, write, step_rows=store.shape[1])
    home = lax.bitwise_xor(lax.axis_index("blk"), lax.axis_index("layer"))
    for mask, out in enumerate(outs):
        slot = lax.bitwise_xor(home, mask)
        out[...] = total[pl.ds(pl.multiple_of(slot * rows, rows), rows), :].astype(out.dtype)


def score_high(near, far, last, store, own, low):
    rows, width = far.shape
    examples = store.shape[1]
    return pl.pallas_call(
        functools.partial(high_kernel, store.shape[2] - width),
        in_specs=in_vmem(6),
        out_specs=in_vmem(4),
        out_shape=[
            jax.ShapeDtypeStruct((rows, examples), jnp.bfloat16 if mask else jnp.float32) for mask in range(4)
        ],
        scratch_shapes=[pltpu.VMEM((4 * rows, examples), jnp.float32)],
        compiler_params=pltpu.CompilerParams(vmem_limit_bytes=VMEM),
        cost_estimate=score_cost(3 * rows, width, examples),
        name="score_high",
    )(near, far, last, store, own, low)


def write_rows(total, layers, listed, out):
    scaled = total / jnp.sqrt(jnp.float32(layers))
    tiles_here = out.shape[1] // TILE
    first = lax.axis_index("blk") * tiles_here
    for tile in range(tiles_here):
        hit = jnp.max(jnp.where(listed == first + tile, 1.0, 0.0), axis=1, keepdims=True)
        columns = slice(tile * TILE, (tile + 1) * TILE)
        out[:, columns] = jnp.where(hit > 0.0, scaled[:, columns], 0.0).astype(out.dtype)


def finish_kernel(layers, candidates, *refs):
    parts, out = refs[:-1], refs[-1]
    total = parts[0][...].astype(jnp.float32)
    for part in parts[1:]:
        total = total + part[...].astype(jnp.float32)
    write_rows(total, layers, candidates[...], out)


def finish(parts, candidates, layers):
    return pl.pallas_call(
        functools.partial(finish_kernel, layers),
        in_specs=in_vmem(1 + len(parts)),
        out_specs=in_vmem(1)[0],
        out_shape=jax.ShapeDtypeStruct(parts[0].shape, jnp.bfloat16),
        compiler_params=pltpu.CompilerParams(vmem_limit_bytes=VMEM),
        name="finish",
    )(candidates, *parts)


def permuted(value, axis, target_of):
    count = lax.axis_size(axis)
    return lax.ppermute(value, axis, [(source, target_of(source) % count) for source in range(count)])


def swapped(value, axis, mask):
    return permuted(value, axis, lambda source: source ^ mask)


def on_line(own, store, candidates, layers):
    far = [swapped(half, "blk", 2) for half in own]
    near = [swapped(half, "blk", 1) for half in own]
    own_scores = score_own(own, store)
    far[0], near[0], own_scores = lax.optimization_barrier((far[0], near[0], own_scores))
    far[1], near[1] = lax.optimization_barrier((far[1], near[1]))
    last = [swapped(half, "blk", 1) for half in far]
    low_scores = score_low(near[0], far[0], last[0], store)
    parts = score_high(near[1], far[1], last[1], store, own_scores, low_scores)
    received = [swapped(parts[mask], "layer", mask) for mask in (1, 2, 3)]
    return finish([parts[0]] + received, candidates, layers)


def on_ring(own, store, candidates, layers):
    count = lax.axis_size("blk")
    rows = own[0].shape[0]
    slots = [score_own(own, store)]
    for _ in range(count - 1):
        own = [permuted(half, "blk", lambda source: source + 1) for half in own]
        slots.append(score_own(own, store))
    turns = lax.rem(lax.axis_index("blk") - jnp.arange(count) + count, count)
    total = jnp.stack(slots)[turns].reshape(layers, count * rows // layers, store.shape[1])
    parts = lax.all_to_all(total.astype(jnp.bfloat16), "layer", 0, 0)
    return finish([parts[layer] for layer in range(layers)], candidates, layers)


def per_device(queries, store, left_factor, right_factor, candidates):
    layers, count = lax.axis_size("layer"), lax.axis_size("blk")
    own = [condition(queries, left_factor, right_factor, half) for half in range(2)]
    way = on_line if layers == 4 and count == 4 else on_ring
    return way(own, store, candidates, layers)


def solution(mesh):
    placed = (
        P("layer", ("parts", "blk"), None),
        P("layer", ("parts", "blk"), None),
        P("layer", None, None),
        P("layer", None, None),
        P(("parts", "layer"), None),
    )
    return jax.shard_map(
        per_device,
        mesh=mesh,
        in_specs=placed,
        out_specs=P(("parts", "layer"), "blk"),
        check_vma=False,
    )
```

```python
import functools

import jax
import jax.numpy as jnp
from jax import lax
from jax.experimental import pallas as pl
from jax.experimental.pallas import tpu as pltpu
from jax.sharding import PartitionSpec as P

TILE = 128
GROUP = 32
LANES = 128
ROWS = 8
VMEM = 24 * 1024 * 1024


def two_parts(value):
    high = value.astype(jnp.bfloat16)
    low = (value - high.astype(jnp.float32)).astype(jnp.bfloat16)
    return high, low


def iota(shape, axis):
    return lax.broadcasted_iota(jnp.int32, shape, axis)


def dot(left, right):
    return jnp.dot(left, right, preferred_element_type=jnp.float32)


def ones_where(condition):
    return jnp.where(condition, 1.0, 0.0).astype(jnp.bfloat16)


def spread_left(left_factor, first, count):
    side = left_factor.shape[0]
    wide = ones_where(iota((side, side * ROWS), 1) // ROWS == iota((side, side * ROWS), 0))
    parts = [part[first : first + count] for part in two_parts(left_factor)]
    columns = dot(jnp.concatenate(parts, axis=0), wide).reshape(2, count, 1, side * ROWS)
    same = iota((1, ROWS, side * ROWS), 1) == iota((1, ROWS, side * ROWS), 2) % ROWS
    parts = [jnp.where(same, columns[part], 0.0).reshape(count * ROWS, side * ROWS) for part in range(2)]
    return jnp.concatenate([part.astype(jnp.bfloat16) for part in parts], axis=1)


def spread_right(right_factor):
    side = right_factor.shape[0]
    wide = ones_where(iota((side, 4 * side), 1) % side == iota((side, 4 * side), 0))
    same = iota((4 * side, 4 * side), 0) // side == iota((4 * side, 4 * side), 1) // side
    high, low = [
        jnp.where(same, jnp.concatenate([dot(part, wide)] * 4, axis=0), 0.0).astype(jnp.bfloat16)
        for part in two_parts(right_factor)
    ]
    return jnp.concatenate([high, low, high], axis=0)


def condition_kernel(first, count, queries_in, left_in, right_in, out, queries, left_factor, right_factor, arrived):
    copies = [
        pltpu.make_async_copy(source.at[0], target, arrived.at[place])
        for place, (source, target) in enumerate(
            [(left_in, left_factor), (right_in, right_factor), (queries_in, queries)]
        )
    ]
    for copy in copies:
        copy.start()
    side = left_factor.shape[0]
    pairs = side // 2
    copies[0].wait()
    copies[1].wait()
    left = spread_left(left_factor[...], first, count)
    right = spread_right(right_factor[...])
    low_half = iota((1, 1, LANES), 2) < side
    copies[2].wait()
    for block in range(queries.shape[0] // GROUP):
        rows = pl.ds(block * GROUP, GROUP)
        straight = jnp.stack(
            [queries[rows, pl.ds(pair * LANES, LANES)].astype(jnp.float32) for pair in range(pairs)]
        )
        swapped = pltpu.roll(straight, side, 2).reshape(pairs, GROUP // ROWS, ROWS, LANES)
        straight = straight.reshape(pairs, GROUP // ROWS, ROWS, LANES)
        columns = []
        for group in (0, 2):
            even = jnp.where(low_half, straight[:, group], swapped[:, group + 1])
            odd = jnp.where(low_half, swapped[:, group], straight[:, group + 1])
            columns.append(jnp.stack([even, odd], axis=1).reshape(side * ROWS, LANES))
        grid = jnp.concatenate(columns, axis=1).astype(jnp.bfloat16)
        halfway = dot(left, jnp.concatenate([grid, grid], axis=0))
        high, low = two_parts(halfway)
        result = dot(jnp.concatenate([high, high, low], axis=1), right)
        result = result.reshape(count // 2, 2, ROWS, 2 * LANES)
        groups = []
        for half in range(2):
            even = result[:, 0, :, half * LANES : (half + 1) * LANES]
            odd = result[:, 1, :, half * LANES : (half + 1) * LANES]
            groups.append(jnp.where(low_half, even, pltpu.roll(odd, side, 2)))
            groups.append(jnp.where(low_half, pltpu.roll(even, side, 2), odd))
        done = jnp.concatenate(groups, axis=1).astype(jnp.bfloat16)
        for pair in range(count // 2):
            out[rows, pl.ds(pair * LANES, LANES)] = done[pair]


def in_vmem(count):
    return [pl.BlockSpec(memory_space=pltpu.VMEM)] * count


def condition(queries, left_factor, right_factor, half):
    unused, block_rows, entries = queries.shape
    side = left_factor.shape[1]
    operands = [pltpu.with_memory_space_constraint(value, pltpu.HBM) for value in (queries, left_factor, right_factor)]
    return pl.pallas_call(
        functools.partial(condition_kernel, half * side // 2, side // 2),
        in_specs=[pl.BlockSpec(memory_space=pltpu.HBM)] * 3,
        out_specs=in_vmem(1)[0],
        out_shape=jax.ShapeDtypeStruct((block_rows, entries // 2), jnp.bfloat16),
        scratch_shapes=[
            pltpu.VMEM((block_rows, entries), jnp.bfloat16),
            pltpu.VMEM((side, side), jnp.float32),
            pltpu.VMEM((side, side), jnp.float32),
            pltpu.SemaphoreType.DMA((3,)),
        ],
        compiler_params=pltpu.CompilerParams(vmem_limit_bytes=VMEM),
        cost_estimate=pl.CostEstimate(
            flops=block_rows * entries * 4096, bytes_accessed=queries.size * 4, transcendentals=0
        ),
        name="condition",
    )(*operands)


STEP = 256


def score_block(queries, store, first, write, arrived=None, step_rows=STEP):
    turned = queries.T
    width = queries.shape[1]

    def one(step, carry):
        place = pl.ds(pl.multiple_of(step * step_rows, step_rows), step_rows)
        if arrived is not None:
            arrived(step)
        value = dot(store[0, place, pl.ds(first, width)], turned)
        write(place, value.T)
        return carry

    lax.fori_loop(0, store.shape[1] // step_rows, one, 0)


def own_kernel(low, high, far_store, out, store, semaphores):
    def copy_of(step):
        place = pl.ds(pl.multiple_of(step * STEP, STEP), STEP)
        return pltpu.make_async_copy(far_store.at[0, place], store.at[0, place], semaphores.at[step])

    for step in range(store.shape[1] // STEP):
        copy_of(step).start()

    def write(place, value):
        out[:, place] = value

    queries = jnp.concatenate([low[...], high[...]], axis=1)
    score_block(queries, store, 0, write, lambda step: copy_of(step).wait())


def score_cost(count, width, examples):
    return pl.CostEstimate(
        flops=2 * count * width * examples, bytes_accessed=examples * width * 2, transcendentals=0
    )


def score_own(halves, store):
    rows, entries = halves[0].shape[0], store.shape[2]
    examples = store.shape[1]
    return pl.pallas_call(
        own_kernel,
        in_specs=in_vmem(2) + [pl.BlockSpec(memory_space=pltpu.HBM)],
        out_specs=in_vmem(1)[0],
        out_shape=jax.ShapeDtypeStruct((rows, examples), jnp.float32),
        scratch_shapes=[pltpu.VMEM(store.shape, store.dtype), pltpu.SemaphoreType.DMA((examples // STEP,))],
        compiler_params=pltpu.CompilerParams(vmem_limit_bytes=VMEM),
        cost_estimate=score_cost(rows, entries, examples),
        name="score_own",
    )(*halves, pltpu.with_memory_space_constraint(store, pltpu.HBM))


def stacked(*blocks):
    return jnp.concatenate([block[...] for block in blocks], axis=0)


def low_kernel(near_first, near_second, far, last, store, out):
    def write(place, value):
        out[:, place] = value

    near = (near_first[...].astype(jnp.float32) + near_second[...].astype(jnp.float32)).astype(jnp.bfloat16)
    score_block(stacked(near, far, last), store, 0, write, step_rows=store.shape[1])


def score_low(near, far, last, store):
    rows, width = far.shape
    examples = store.shape[1]
    return pl.pallas_call(
        low_kernel,
        in_specs=in_vmem(5),
        out_specs=in_vmem(1)[0],
        out_shape=jax.ShapeDtypeStruct((3 * rows, examples), jnp.float32),
        compiler_params=pltpu.CompilerParams(vmem_limit_bytes=VMEM),
        cost_estimate=score_cost(3 * rows, width, examples),
        name="score_low",
    )(*near, far, last, store)


def high_kernel(first, near, far, last, store, own, low, *refs):
    outs, total = refs[:-1], refs[-1]
    rows = own.shape[0]
    total[pl.ds(0, rows), :] = own[...]

    def write(place, value):
        total[pl.ds(rows, 3 * rows), place] = value + low[:, place]

    score_block(stacked(near, far, last), store, first, write, step_rows=store.shape[1])
    home = lax.bitwise_xor(lax.axis_index("blk"), lax.axis_index("layer"))
    for mask, out in enumerate(outs):
        slot = lax.bitwise_xor(home, mask)
        out[...] = total[pl.ds(pl.multiple_of(slot * rows, rows), rows), :].astype(out.dtype)


def score_high(near, far, last, store, own, low):
    rows, width = far.shape
    examples = store.shape[1]
    return pl.pallas_call(
        functools.partial(high_kernel, store.shape[2] - width),
        in_specs=in_vmem(6),
        out_specs=in_vmem(4),
        out_shape=[
            jax.ShapeDtypeStruct((rows, examples), jnp.bfloat16 if mask else jnp.float32) for mask in range(4)
        ],
        scratch_shapes=[pltpu.VMEM((4 * rows, examples), jnp.float32)],
        compiler_params=pltpu.CompilerParams(vmem_limit_bytes=VMEM),
        cost_estimate=score_cost(3 * rows, width, examples),
        name="score_high",
    )(near, far, last, store, own, low)


def write_rows(total, layers, listed, out):
    scaled = total / jnp.sqrt(jnp.float32(layers))
    tiles_here = out.shape[1] // TILE
    first = lax.axis_index("blk") * tiles_here
    for tile in range(tiles_here):
        hit = jnp.max(jnp.where(listed == first + tile, 1.0, 0.0), axis=1, keepdims=True)
        columns = slice(tile * TILE, (tile + 1) * TILE)
        out[:, columns] = jnp.where(hit > 0.0, scaled[:, columns], 0.0).astype(out.dtype)


def finish_kernel(layers, candidates, *refs):
    parts, out = refs[:-1], refs[-1]
    total = parts[0][...].astype(jnp.float32)
    for part in parts[1:]:
        total = total + part[...].astype(jnp.float32)
    write_rows(total, layers, candidates[...], out)


def finish(parts, candidates, layers):
    return pl.pallas_call(
        functools.partial(finish_kernel, layers),
        in_specs=in_vmem(1 + len(parts)),
        out_specs=in_vmem(1)[0],
        out_shape=jax.ShapeDtypeStruct(parts[0].shape, jnp.bfloat16),
        compiler_params=pltpu.CompilerParams(vmem_limit_bytes=VMEM),
        name="finish",
    )(candidates, *parts)


def permuted(value, axis, target_of):
    count = lax.axis_size(axis)
    return lax.ppermute(value, axis, [(source, target_of(source) % count) for source in range(count)])


def swapped(value, axis, mask):
    return permuted(value, axis, lambda source: source ^ mask)


def on_line(own, store, candidates, layers):
    far = [swapped(half, "blk", 2) for half in own]
    near_first, near_second = [lax.ppermute(own[0], "blk", pairs) for pairs in ([(0, 1), (1, 0)], [(2, 3), (3, 2)])]
    near_high = swapped(own[1], "blk", 1)
    own_scores = score_own(own, store)
    near_first, far[0], near_second, own_scores = lax.optimization_barrier(
        (near_first, far[0], near_second, own_scores)
    )
    near_high, far[1] = lax.optimization_barrier((near_high, far[1]))
    last = [swapped(half, "blk", 1) for half in far]
    low_scores = score_low([near_first, near_second], far[0], last[0], store)
    parts = score_high(near_high, far[1], last[1], store, own_scores, low_scores)
    received = [swapped(parts[mask], "layer", mask) for mask in (1, 2, 3)]
    return finish([parts[0]] + received, candidates, layers)


def on_ring(own, store, candidates, layers):
    count = lax.axis_size("blk")
    rows = own[0].shape[0]
    slots = [score_own(own, store)]
    for _ in range(count - 1):
        own = [permuted(half, "blk", lambda source: source + 1) for half in own]
        slots.append(score_own(own, store))
    turns = lax.rem(lax.axis_index("blk") - jnp.arange(count) + count, count)
    total = jnp.stack(slots)[turns].reshape(layers, count * rows // layers, store.shape[1])
    parts = lax.all_to_all(total.astype(jnp.bfloat16), "layer", 0, 0)
    return finish([parts[layer] for layer in range(layers)], candidates, layers)


def per_device(queries, store, left_factor, right_factor, candidates):
    layers, count = lax.axis_size("layer"), lax.axis_size("blk")
    own = [condition(queries, left_factor, right_factor, half) for half in range(2)]
    way = on_line if layers == 4 and count == 4 else on_ring
    return way(own, store, candidates, layers)


def solution(mesh):
    placed = (
        P("layer", ("parts", "blk"), None),
        P("layer", ("parts", "blk"), None),
        P("layer", None, None),
        P("layer", None, None),
        P(("parts", "layer"), None),
    )
    return jax.shard_map(
        per_device,
        mesh=mesh,
        in_specs=placed,
        out_specs=P(("parts", "layer"), "blk"),
        check_vma=False,
    )
```

```python
import functools

import jax
import jax.numpy as jnp
from jax import lax
from jax.experimental import pallas as pl
from jax.experimental.pallas import tpu as pltpu
from jax.sharding import PartitionSpec as P

TILE = 128
GROUP = 32
LANES = 128
ROWS = 8
VMEM = 24 * 1024 * 1024


def two_parts(value):
    high = value.astype(jnp.bfloat16)
    low = (value - high.astype(jnp.float32)).astype(jnp.bfloat16)
    return high, low


def iota(shape, axis):
    return lax.broadcasted_iota(jnp.int32, shape, axis)


def dot(left, right):
    return jnp.dot(left, right, preferred_element_type=jnp.float32)


def ones_where(condition):
    return jnp.where(condition, 1.0, 0.0).astype(jnp.bfloat16)


def spread_left(left_factor, first, count):
    side = left_factor.shape[0]
    wide = ones_where(iota((side, side * ROWS), 1) // ROWS == iota((side, side * ROWS), 0))
    parts = [part[first : first + count] for part in two_parts(left_factor)]
    columns = dot(jnp.concatenate(parts, axis=0), wide).reshape(2, count, 1, side * ROWS)
    same = iota((1, ROWS, side * ROWS), 1) == iota((1, ROWS, side * ROWS), 2) % ROWS
    parts = [jnp.where(same, columns[part], 0.0).reshape(count * ROWS, side * ROWS) for part in range(2)]
    return jnp.concatenate([part.astype(jnp.bfloat16) for part in parts], axis=1)


def spread_right(right_factor):
    side = right_factor.shape[0]
    wide = ones_where(iota((side, 4 * side), 1) % side == iota((side, 4 * side), 0))
    same = iota((4 * side, 4 * side), 0) // side == iota((4 * side, 4 * side), 1) // side
    high, low = [
        jnp.where(same, jnp.concatenate([dot(part, wide)] * 4, axis=0), 0.0).astype(jnp.bfloat16)
        for part in two_parts(right_factor)
    ]
    return jnp.concatenate([high, low, high], axis=0)


def condition_kernel(first, count, queries_in, left_in, right_in, out, queries, left_factor, right_factor, arrived):
    copies = [
        pltpu.make_async_copy(source.at[0], target, arrived.at[place])
        for place, (source, target) in enumerate(
            [(left_in, left_factor), (right_in, right_factor), (queries_in, queries)]
        )
    ]
    for copy in copies:
        copy.start()
    side = left_factor.shape[0]
    pairs = side // 2
    copies[0].wait()
    copies[1].wait()
    left = spread_left(left_factor[...], first, count)
    right = spread_right(right_factor[...])
    low_half = iota((1, 1, LANES), 2) < side
    copies[2].wait()
    for block in range(queries.shape[0] // GROUP):
        rows = pl.ds(block * GROUP, GROUP)
        straight = jnp.stack(
            [queries[rows, pl.ds(pair * LANES, LANES)].astype(jnp.float32) for pair in range(pairs)]
        )
        swapped = pltpu.roll(straight, side, 2).reshape(pairs, GROUP // ROWS, ROWS, LANES)
        straight = straight.reshape(pairs, GROUP // ROWS, ROWS, LANES)
        columns = []
        for group in (0, 2):
            even = jnp.where(low_half, straight[:, group], swapped[:, group + 1])
            odd = jnp.where(low_half, swapped[:, group], straight[:, group + 1])
            columns.append(jnp.stack([even, odd], axis=1).reshape(side * ROWS, LANES))
        grid = jnp.concatenate(columns, axis=1).astype(jnp.bfloat16)
        halfway = dot(left, jnp.concatenate([grid, grid], axis=0))
        high, low = two_parts(halfway)
        result = dot(jnp.concatenate([high, high, low], axis=1), right)
        result = result.reshape(count // 2, 2, ROWS, 2 * LANES)
        groups = []
        for half in range(2):
            even = result[:, 0, :, half * LANES : (half + 1) * LANES]
            odd = result[:, 1, :, half * LANES : (half + 1) * LANES]
            groups.append(jnp.where(low_half, even, pltpu.roll(odd, side, 2)))
            groups.append(jnp.where(low_half, pltpu.roll(even, side, 2), odd))
        done = jnp.concatenate(groups, axis=1).astype(jnp.bfloat16)
        for pair in range(count // 2):
            out[rows, pl.ds(pair * LANES, LANES)] = done[pair]


def in_vmem(count):
    return [pl.BlockSpec(memory_space=pltpu.VMEM)] * count


def condition(queries, left_factor, right_factor, half):
    unused, block_rows, entries = queries.shape
    side = left_factor.shape[1]
    operands = [pltpu.with_memory_space_constraint(value, pltpu.HBM) for value in (queries, left_factor, right_factor)]
    return pl.pallas_call(
        functools.partial(condition_kernel, half * side // 2, side // 2),
        in_specs=[pl.BlockSpec(memory_space=pltpu.HBM)] * 3,
        out_specs=in_vmem(1)[0],
        out_shape=jax.ShapeDtypeStruct((block_rows, entries // 2), jnp.bfloat16),
        scratch_shapes=[
            pltpu.VMEM((block_rows, entries), jnp.bfloat16),
            pltpu.VMEM((side, side), jnp.float32),
            pltpu.VMEM((side, side), jnp.float32),
            pltpu.SemaphoreType.DMA((3,)),
        ],
        compiler_params=pltpu.CompilerParams(vmem_limit_bytes=VMEM),
        cost_estimate=pl.CostEstimate(
            flops=block_rows * entries * 4096, bytes_accessed=queries.size * 4, transcendentals=0
        ),
        name="condition",
    )(*operands)


STEP = 256


def score_block(queries, store, first, write, arrived=None, step_rows=STEP):
    turned = queries.T
    width = queries.shape[1]

    def one(step, carry):
        place = pl.ds(pl.multiple_of(step * step_rows, step_rows), step_rows)
        if arrived is not None:
            arrived(step)
        value = dot(store[0, place, pl.ds(first, width)], turned)
        write(place, value.T)
        return carry

    lax.fori_loop(0, store.shape[1] // step_rows, one, 0)


def own_kernel(low, high, far_store, out, store, semaphores):
    def copy_of(step):
        place = pl.ds(pl.multiple_of(step * STEP, STEP), STEP)
        return pltpu.make_async_copy(far_store.at[0, place], store.at[0, place], semaphores.at[step])

    for step in range(store.shape[1] // STEP):
        copy_of(step).start()

    def write(place, value):
        out[:, place] = value

    queries = jnp.concatenate([low[...], high[...]], axis=1)
    score_block(queries, store, 0, write, lambda step: copy_of(step).wait())


def score_cost(count, width, examples):
    return pl.CostEstimate(
        flops=2 * count * width * examples, bytes_accessed=examples * width * 2, transcendentals=0
    )


def score_own(halves, store):
    rows, entries = halves[0].shape[0], store.shape[2]
    examples = store.shape[1]
    return pl.pallas_call(
        own_kernel,
        in_specs=in_vmem(2) + [pl.BlockSpec(memory_space=pltpu.HBM)],
        out_specs=in_vmem(1)[0],
        out_shape=jax.ShapeDtypeStruct((rows, examples), jnp.float32),
        scratch_shapes=[pltpu.VMEM(store.shape, store.dtype), pltpu.SemaphoreType.DMA((examples // STEP,))],
        compiler_params=pltpu.CompilerParams(vmem_limit_bytes=VMEM),
        cost_estimate=score_cost(rows, entries, examples),
        name="score_own",
    )(*halves, pltpu.with_memory_space_constraint(store, pltpu.HBM))


def stacked(*blocks):
    return jnp.concatenate([block[...] for block in blocks], axis=0)


def low_kernel(near_first, near_second, far, last, store, out):
    def write(place, value):
        out[:, place] = value

    in_first = lax.axis_index("blk") < 2
    near = jnp.where(in_first, near_first[...].astype(jnp.float32), near_second[...].astype(jnp.float32))
    near = near.astype(jnp.bfloat16)
    score_block(stacked(near, far, last), store, 0, write, step_rows=store.shape[1])


def score_low(near, far, last, store):
    rows, width = far.shape
    examples = store.shape[1]
    return pl.pallas_call(
        low_kernel,
        in_specs=in_vmem(5),
        out_specs=in_vmem(1)[0],
        out_shape=jax.ShapeDtypeStruct((3 * rows, examples), jnp.float32),
        compiler_params=pltpu.CompilerParams(vmem_limit_bytes=VMEM),
        cost_estimate=score_cost(3 * rows, width, examples),
        name="score_low",
    )(*near, far, last, store)


def high_kernel(first, near, far, last, store, own, low, *refs):
    outs, total = refs[:-1], refs[-1]
    rows = own.shape[0]
    total[pl.ds(0, rows), :] = own[...]

    def write(place, value):
        total[pl.ds(rows, 3 * rows), place] = value + low[:, place]

    score_block(stacked(near, far, last), store, first, write, step_rows=store.shape[1])
    home = lax.bitwise_xor(lax.axis_index("blk"), lax.axis_index("layer"))
    for mask, out in enumerate(outs):
        slot = lax.bitwise_xor(home, mask)
        out[...] = total[pl.ds(pl.multiple_of(slot * rows, rows), rows), :].astype(out.dtype)


def score_high(near, far, last, store, own, low):
    rows, width = far.shape
    examples = store.shape[1]
    return pl.pallas_call(
        functools.partial(high_kernel, store.shape[2] - width),
        in_specs=in_vmem(6),
        out_specs=in_vmem(4),
        out_shape=[
            jax.ShapeDtypeStruct((rows, examples), jnp.bfloat16 if mask else jnp.float32) for mask in range(4)
        ],
        scratch_shapes=[pltpu.VMEM((4 * rows, examples), jnp.float32)],
        compiler_params=pltpu.CompilerParams(vmem_limit_bytes=VMEM),
        cost_estimate=score_cost(3 * rows, width, examples),
        name="score_high",
    )(near, far, last, store, own, low)


def write_rows(total, layers, listed, out):
    scaled = total / jnp.sqrt(jnp.float32(layers))
    tiles_here = out.shape[1] // TILE
    first = lax.axis_index("blk") * tiles_here
    for tile in range(tiles_here):
        hit = jnp.max(jnp.where(listed == first + tile, 1.0, 0.0), axis=1, keepdims=True)
        columns = slice(tile * TILE, (tile + 1) * TILE)
        out[:, columns] = jnp.where(hit > 0.0, scaled[:, columns], 0.0).astype(out.dtype)


def finish_kernel(layers, candidates, *refs):
    parts, out = refs[:-1], refs[-1]
    total = parts[0][...].astype(jnp.float32)
    for part in parts[1:]:
        total = total + part[...].astype(jnp.float32)
    write_rows(total, layers, candidates[...], out)


def finish(parts, candidates, layers):
    return pl.pallas_call(
        functools.partial(finish_kernel, layers),
        in_specs=in_vmem(1 + len(parts)),
        out_specs=in_vmem(1)[0],
        out_shape=jax.ShapeDtypeStruct(parts[0].shape, jnp.bfloat16),
        compiler_params=pltpu.CompilerParams(vmem_limit_bytes=VMEM),
        name="finish",
    )(candidates, *parts)


def permuted(value, axis, target_of):
    count = lax.axis_size(axis)
    return lax.ppermute(value, axis, [(source, target_of(source) % count) for source in range(count)])


def swapped(value, axis, mask):
    return permuted(value, axis, lambda source: source ^ mask)


def on_line(own, store, candidates, layers):
    far = [swapped(half, "blk", 2) for half in own]
    near_first, near_second = [lax.ppermute(own[0], "blk", pairs) for pairs in ([(0, 1), (1, 0), (2, 2), (3, 3)], [(0, 0), (1, 1), (2, 3), (3, 2)])]
    near_high = swapped(own[1], "blk", 1)
    own_scores = score_own(own, store)
    near_first, far[0], near_second, own_scores = lax.optimization_barrier(
        (near_first, far[0], near_second, own_scores)
    )
    near_high, far[1] = lax.optimization_barrier((near_high, far[1]))
    last = [swapped(half, "blk", 1) for half in far]
    low_scores = score_low([near_first, near_second], far[0], last[0], store)
    parts = score_high(near_high, far[1], last[1], store, own_scores, low_scores)
    received = [swapped(parts[mask], "layer", mask) for mask in (1, 2, 3)]
    return finish([parts[0]] + received, candidates, layers)


def on_ring(own, store, candidates, layers):
    count = lax.axis_size("blk")
    rows = own[0].shape[0]
    slots = [score_own(own, store)]
    for _ in range(count - 1):
        own = [permuted(half, "blk", lambda source: source + 1) for half in own]
        slots.append(score_own(own, store))
    turns = lax.rem(lax.axis_index("blk") - jnp.arange(count) + count, count)
    total = jnp.stack(slots)[turns].reshape(layers, count * rows // layers, store.shape[1])
    parts = lax.all_to_all(total.astype(jnp.bfloat16), "layer", 0, 0)
    return finish([parts[layer] for layer in range(layers)], candidates, layers)


def per_device(queries, store, left_factor, right_factor, candidates):
    layers, count = lax.axis_size("layer"), lax.axis_size("blk")
    own = [condition(queries, left_factor, right_factor, half) for half in range(2)]
    way = on_line if layers == 4 and count == 4 else on_ring
    return way(own, store, candidates, layers)


def solution(mesh):
    placed = (
        P("layer", ("parts", "blk"), None),
        P("layer", ("parts", "blk"), None),
        P("layer", None, None),
        P("layer", None, None),
        P(("parts", "layer"), None),
    )
    return jax.shard_map(
        per_device,
        mesh=mesh,
        in_specs=placed,
        out_specs=P(("parts", "layer"), "blk"),
        check_vma=False,
    )
```

```python
import functools

import jax
import jax.numpy as jnp
from jax import lax
from jax.experimental import pallas as pl
from jax.experimental.pallas import tpu as pltpu
from jax.sharding import PartitionSpec as P

TILE = 128
GROUP = 32
LANES = 128
ROWS = 8
VMEM = 24 * 1024 * 1024


def two_parts(value):
    high = value.astype(jnp.bfloat16)
    low = (value - high.astype(jnp.float32)).astype(jnp.bfloat16)
    return high, low


def iota(shape, axis):
    return lax.broadcasted_iota(jnp.int32, shape, axis)


def dot(left, right):
    return jnp.dot(left, right, preferred_element_type=jnp.float32)


def ones_where(condition):
    return jnp.where(condition, 1.0, 0.0).astype(jnp.bfloat16)


def spread_left(left_factor, first, count):
    side = left_factor.shape[0]
    wide = ones_where(iota((side, side * ROWS), 1) // ROWS == iota((side, side * ROWS), 0))
    parts = [part[first : first + count] for part in two_parts(left_factor)]
    columns = dot(jnp.concatenate(parts, axis=0), wide).reshape(2, count, 1, side * ROWS)
    same = iota((1, ROWS, side * ROWS), 1) == iota((1, ROWS, side * ROWS), 2) % ROWS
    parts = [jnp.where(same, columns[part], 0.0).reshape(count * ROWS, side * ROWS) for part in range(2)]
    return jnp.concatenate([part.astype(jnp.bfloat16) for part in parts], axis=1)


def spread_right(right_factor):
    side = right_factor.shape[0]
    wide = ones_where(iota((side, 4 * side), 1) % side == iota((side, 4 * side), 0))
    same = iota((4 * side, 4 * side), 0) // side == iota((4 * side, 4 * side), 1) // side
    high, low = [
        jnp.where(same, jnp.concatenate([dot(part, wide)] * 4, axis=0), 0.0).astype(jnp.bfloat16)
        for part in two_parts(right_factor)
    ]
    return jnp.concatenate([high, low, high], axis=0)


def condition_kernel(first, count, queries_in, left_in, right_in, out, queries, left_factor, right_factor, arrived):
    copies = [
        pltpu.make_async_copy(source.at[0], target, arrived.at[place])
        for place, (source, target) in enumerate(
            [(left_in, left_factor), (right_in, right_factor), (queries_in, queries)]
        )
    ]
    for copy in copies:
        copy.start()
    side = left_factor.shape[0]
    pairs = side // 2
    copies[0].wait()
    copies[1].wait()
    left = spread_left(left_factor[...], first, count)
    right = spread_right(right_factor[...])
    low_half = iota((1, 1, LANES), 2) < side
    copies[2].wait()
    for block in range(queries.shape[0] // GROUP):
        rows = pl.ds(block * GROUP, GROUP)
        straight = jnp.stack(
            [queries[rows, pl.ds(pair * LANES, LANES)].astype(jnp.float32) for pair in range(pairs)]
        )
        swapped = pltpu.roll(straight, side, 2).reshape(pairs, GROUP // ROWS, ROWS, LANES)
        straight = straight.reshape(pairs, GROUP // ROWS, ROWS, LANES)
        columns = []
        for group in (0, 2):
            even = jnp.where(low_half, straight[:, group], swapped[:, group + 1])
            odd = jnp.where(low_half, swapped[:, group], straight[:, group + 1])
            columns.append(jnp.stack([even, odd], axis=1).reshape(side * ROWS, LANES))
        grid = jnp.concatenate(columns, axis=1).astype(jnp.bfloat16)
        halfway = dot(left, jnp.concatenate([grid, grid], axis=0))
        high, low = two_parts(halfway)
        result = dot(jnp.concatenate([high, high, low], axis=1), right)
        result = result.reshape(count // 2, 2, ROWS, 2 * LANES)
        groups = []
        for half in range(2):
            even = result[:, 0, :, half * LANES : (half + 1) * LANES]
            odd = result[:, 1, :, half * LANES : (half + 1) * LANES]
            groups.append(jnp.where(low_half, even, pltpu.roll(odd, side, 2)))
            groups.append(jnp.where(low_half, pltpu.roll(even, side, 2), odd))
        done = jnp.concatenate(groups, axis=1).astype(jnp.bfloat16)
        for pair in range(count // 2):
            out[rows, pl.ds(pair * LANES, LANES)] = done[pair]


def in_vmem(count):
    return [pl.BlockSpec(memory_space=pltpu.VMEM)] * count


def condition(queries, left_factor, right_factor, half):
    unused, block_rows, entries = queries.shape
    side = left_factor.shape[1]
    operands = [pltpu.with_memory_space_constraint(value, pltpu.HBM) for value in (queries, left_factor, right_factor)]
    return pl.pallas_call(
        functools.partial(condition_kernel, half * side // 2, side // 2),
        in_specs=[pl.BlockSpec(memory_space=pltpu.HBM)] * 3,
        out_specs=in_vmem(1)[0],
        out_shape=jax.ShapeDtypeStruct((block_rows, entries // 2), jnp.bfloat16),
        scratch_shapes=[
            pltpu.VMEM((block_rows, entries), jnp.bfloat16),
            pltpu.VMEM((side, side), jnp.float32),
            pltpu.VMEM((side, side), jnp.float32),
            pltpu.SemaphoreType.DMA((3,)),
        ],
        compiler_params=pltpu.CompilerParams(vmem_limit_bytes=VMEM),
        cost_estimate=pl.CostEstimate(
            flops=block_rows * entries * 4096, bytes_accessed=queries.size * 4, transcendentals=0
        ),
        name="condition",
    )(*operands)


STEP = 256
MASKS = (0, 2, 3, 1)


def score_block(queries, store, first, write, arrived=None, step_rows=STEP):
    turned = queries.T
    width = queries.shape[1]

    def one(step, carry):
        place = pl.ds(pl.multiple_of(step * step_rows, step_rows), step_rows)
        if arrived is not None:
            arrived(step)
        value = dot(store[0, place, pl.ds(first, width)], turned)
        write(place, value.T)
        return carry

    lax.fori_loop(0, store.shape[1] // step_rows, one, 0)


def own_kernel(queries, far_store, out, store, semaphores):
    def copy_of(step):
        place = pl.ds(pl.multiple_of(step * STEP, STEP), STEP)
        source = far_store.at[0, place, pl.ds(0, store.shape[2])]
        return pltpu.make_async_copy(source, store.at[0, place], semaphores.at[step])

    for step in range(store.shape[1] // STEP):
        copy_of(step).start()

    def write(place, value):
        out[:, place] = value

    score_block(queries[...], store, 0, write, lambda step: copy_of(step).wait())


def score_cost(count, width, examples):
    return pl.CostEstimate(
        flops=2 * count * width * examples, bytes_accessed=examples * width * 2, transcendentals=0
    )


def score_own(queries, store):
    rows, entries = queries.shape
    examples = store.shape[1]
    return pl.pallas_call(
        own_kernel,
        in_specs=in_vmem(1) + [pl.BlockSpec(memory_space=pltpu.HBM)],
        out_specs=in_vmem(1)[0],
        out_shape=jax.ShapeDtypeStruct((rows, examples), jnp.float32),
        scratch_shapes=[
            pltpu.VMEM((1, examples, entries), store.dtype),
            pltpu.SemaphoreType.DMA((examples // STEP,)),
        ],
        compiler_params=pltpu.CompilerParams(vmem_limit_bytes=VMEM),
        cost_estimate=score_cost(rows, entries, examples),
        name="score_own",
    )(queries, pltpu.with_memory_space_constraint(store, pltpu.HBM))


def stacked(*blocks):
    return jnp.concatenate([block[...] for block in blocks], axis=0)


def low_kernel(near, far, last, store, out):
    def write(place, value):
        out[:, place] = value

    score_block(stacked(near, far, last), store, 0, write, step_rows=store.shape[1])


def score_low(near, far, last, store):
    rows, width = far.shape
    examples = store.shape[1]
    return pl.pallas_call(
        low_kernel,
        in_specs=in_vmem(4),
        out_specs=in_vmem(1)[0],
        out_shape=jax.ShapeDtypeStruct((3 * rows, examples), jnp.float32),
        compiler_params=pltpu.CompilerParams(vmem_limit_bytes=VMEM),
        cost_estimate=score_cost(3 * rows, width, examples),
        name="score_low",
    )(near, far, last, store)


def high_kernel(first, own, near, far, last, store, own_low, low, *refs):
    outs, total = refs[:-1], refs[-1]
    rows = own.shape[0]

    def write(place, value):
        total[pl.ds(0, rows), place] = value[:rows] + own_low[:, place]
        total[pl.ds(rows, 3 * rows), place] = value[rows:] + low[:, place]

    score_block(stacked(own, near, far, last), store, first, write, step_rows=store.shape[1])
    home = lax.bitwise_xor(lax.axis_index("blk"), lax.axis_index("layer"))
    for mask, out in zip(MASKS, outs):
        slot = lax.bitwise_xor(home, mask)
        out[...] = total[pl.ds(pl.multiple_of(slot * rows, rows), rows), :].astype(out.dtype)


def score_high(own, near, far, last, store, own_low, low):
    rows, width = far.shape
    examples = store.shape[1]
    return pl.pallas_call(
        functools.partial(high_kernel, store.shape[2] - width),
        in_specs=in_vmem(7),
        out_specs=in_vmem(4),
        out_shape=[
            jax.ShapeDtypeStruct((rows, examples), jnp.bfloat16 if mask else jnp.float32) for mask in MASKS
        ],
        scratch_shapes=[pltpu.VMEM((4 * rows, examples), jnp.float32)],
        compiler_params=pltpu.CompilerParams(vmem_limit_bytes=VMEM),
        cost_estimate=score_cost(4 * rows, width, examples),
        name="score_high",
    )(own, near, far, last, store, own_low, low)


def write_rows(total, layers, listed, out):
    scaled = total / jnp.sqrt(jnp.float32(layers))
    tiles_here = out.shape[1] // TILE
    first = lax.axis_index("blk") * tiles_here
    for tile in range(tiles_here):
        hit = jnp.max(jnp.where(listed == first + tile, 1.0, 0.0), axis=1, keepdims=True)
        columns = slice(tile * TILE, (tile + 1) * TILE)
        out[:, columns] = jnp.where(hit > 0.0, scaled[:, columns], 0.0).astype(out.dtype)


def finish_kernel(layers, candidates, *refs):
    parts, out = refs[:-1], refs[-1]
    total = parts[0][...].astype(jnp.float32)
    for part in parts[1:]:
        total = total + part[...].astype(jnp.float32)
    write_rows(total, layers, candidates[...], out)


def finish(parts, candidates, layers):
    return pl.pallas_call(
        functools.partial(finish_kernel, layers),
        in_specs=in_vmem(1 + len(parts)),
        out_specs=in_vmem(1)[0],
        out_shape=jax.ShapeDtypeStruct(parts[0].shape, jnp.bfloat16),
        compiler_params=pltpu.CompilerParams(vmem_limit_bytes=VMEM),
        name="finish",
    )(candidates, *parts)


def permuted(value, axis, target_of):
    count = lax.axis_size(axis)
    return lax.ppermute(value, axis, [(source, target_of(source) % count) for source in range(count)])


def swapped(value, axis, mask):
    return permuted(value, axis, lambda source: source ^ mask)


def on_line(own, store, candidates, layers):
    far = [swapped(half, "blk", 2) for half in own]
    near = [swapped(half, "blk", 1) for half in own]
    own_low = score_own(own[0], store)
    far[0], near[0], own_low = lax.optimization_barrier((far[0], near[0], own_low))
    far[1], near[1] = lax.optimization_barrier((far[1], near[1]))
    last = [swapped(half, "blk", 1) for half in far]
    low_scores = score_low(near[0], far[0], last[0], store)
    parts = score_high(own[1], near[1], far[1], last[1], store, own_low, low_scores)
    received = [swapped(part, "layer", mask) for mask, part in zip(MASKS[1:], parts[1:])]
    return finish([parts[0]] + received, candidates, layers)


def on_ring(own, store, candidates, layers):
    count = lax.axis_size("blk")
    rows = own[0].shape[0]
    moving = jnp.concatenate(own, axis=1)

    def scores():
        return lax.dot_general(moving, store[0], (((1,), (1,)), ((), ())), preferred_element_type=jnp.float32)

    slots = [scores()]
    for _ in range(count - 1):
        moving = permuted(moving, "blk", lambda source: source + 1)
        slots.append(scores())
    turns = lax.rem(lax.axis_index("blk") - jnp.arange(count) + count, count)
    total = jnp.stack(slots)[turns].reshape(layers, count * rows // layers, store.shape[1])
    parts = lax.all_to_all(total.astype(jnp.bfloat16), "layer", 0, 0)
    return finish([parts[layer] for layer in range(layers)], candidates, layers)


def per_device(queries, store, left_factor, right_factor, candidates):
    layers, count = lax.axis_size("layer"), lax.axis_size("blk")
    own = [condition(queries, left_factor, right_factor, half) for half in range(2)]
    way = on_line if layers == 4 and count == 4 else on_ring
    return way(own, store, candidates, layers)


def solution(mesh):
    placed = (
        P("layer", ("parts", "blk"), None),
        P("layer", ("parts", "blk"), None),
        P("layer", None, None),
        P("layer", None, None),
        P(("parts", "layer"), None),
    )
    return jax.shard_map(
        per_device,
        mesh=mesh,
        in_specs=placed,
        out_specs=P(("parts", "layer"), "blk"),
        check_vma=False,
    )
```

```python
import functools

import jax
import jax.numpy as jnp
from jax import lax
from jax.experimental import pallas as pl
from jax.experimental.pallas import tpu as pltpu
from jax.sharding import PartitionSpec as P

TILE = 128
GROUP = 32
LANES = 128
ROWS = 8
VMEM = 24 * 1024 * 1024


def two_parts(value):
    high = value.astype(jnp.bfloat16)
    low = (value - high.astype(jnp.float32)).astype(jnp.bfloat16)
    return high, low


def iota(shape, axis):
    return lax.broadcasted_iota(jnp.int32, shape, axis)


def dot(left, right):
    return jnp.dot(left, right, preferred_element_type=jnp.float32)


def ones_where(condition):
    return jnp.where(condition, 1.0, 0.0).astype(jnp.bfloat16)


def spread_left(left_factor, first, count):
    side = left_factor.shape[0]
    wide = ones_where(iota((side, side * ROWS), 1) // ROWS == iota((side, side * ROWS), 0))
    parts = [part[first : first + count] for part in two_parts(left_factor)]
    columns = dot(jnp.concatenate(parts, axis=0), wide).reshape(2, count, 1, side * ROWS)
    same = iota((1, ROWS, side * ROWS), 1) == iota((1, ROWS, side * ROWS), 2) % ROWS
    parts = [jnp.where(same, columns[part], 0.0).reshape(count * ROWS, side * ROWS) for part in range(2)]
    return jnp.concatenate([part.astype(jnp.bfloat16) for part in parts], axis=1)


def spread_right(right_factor):
    side = right_factor.shape[0]
    wide = ones_where(iota((side, 4 * side), 1) % side == iota((side, 4 * side), 0))
    same = iota((4 * side, 4 * side), 0) // side == iota((4 * side, 4 * side), 1) // side
    high, low = [
        jnp.where(same, jnp.concatenate([dot(part, wide)] * 4, axis=0), 0.0).astype(jnp.bfloat16)
        for part in two_parts(right_factor)
    ]
    return jnp.concatenate([high, low, high], axis=0)


def condition_kernel(first, count, queries_in, left_in, right_in, out, queries, left_factor, right_factor, arrived):
    copies = [
        pltpu.make_async_copy(source.at[0], target, arrived.at[place])
        for place, (source, target) in enumerate(
            [(left_in, left_factor), (right_in, right_factor), (queries_in, queries)]
        )
    ]
    for copy in copies:
        copy.start()
    side = left_factor.shape[0]
    pairs = side // 2
    for copy in copies:
        copy.wait()
    left = spread_left(left_factor[...], first, count)
    right = spread_right(right_factor[...])
    low_half = iota((1, 1, LANES), 2) < side
    for block in range(queries.shape[0] // GROUP):
        rows = pl.ds(block * GROUP, GROUP)
        straight = jnp.stack(
            [queries[rows, pl.ds(pair * LANES, LANES)].astype(jnp.float32) for pair in range(pairs)]
        )
        swapped = pltpu.roll(straight, side, 2).reshape(pairs, GROUP // ROWS, ROWS, LANES)
        straight = straight.reshape(pairs, GROUP // ROWS, ROWS, LANES)
        columns = []
        for group in (0, 2):
            even = jnp.where(low_half, straight[:, group], swapped[:, group + 1])
            odd = jnp.where(low_half, swapped[:, group], straight[:, group + 1])
            columns.append(jnp.stack([even, odd], axis=1).reshape(side * ROWS, LANES))
        grid = jnp.concatenate(columns, axis=1).astype(jnp.bfloat16)
        halfway = dot(left, jnp.concatenate([grid, grid], axis=0))
        high, low = two_parts(halfway)
        result = dot(jnp.concatenate([high, high, low], axis=1), right)
        result = result.reshape(count // 2, 2, ROWS, 2 * LANES)
        groups = []
        for half in range(2):
            even = result[:, 0, :, half * LANES : (half + 1) * LANES]
            odd = result[:, 1, :, half * LANES : (half + 1) * LANES]
            groups.append(jnp.where(low_half, even, pltpu.roll(odd, side, 2)))
            groups.append(jnp.where(low_half, pltpu.roll(even, side, 2), odd))
        done = jnp.concatenate(groups, axis=1).astype(jnp.bfloat16)
        for pair in range(count // 2):
            out[rows, pl.ds(pair * LANES, LANES)] = done[pair]


def in_vmem(count):
    return [pl.BlockSpec(memory_space=pltpu.VMEM)] * count


def condition(queries, left_factor, right_factor, half):
    unused, block_rows, entries = queries.shape
    side = left_factor.shape[1]
    operands = [pltpu.with_memory_space_constraint(value, pltpu.HBM) for value in (queries, left_factor, right_factor)]
    return pl.pallas_call(
        functools.partial(condition_kernel, half * side // 2, side // 2),
        in_specs=[pl.BlockSpec(memory_space=pltpu.HBM)] * 3,
        out_specs=in_vmem(1)[0],
        out_shape=jax.ShapeDtypeStruct((block_rows, entries // 2), jnp.bfloat16),
        scratch_shapes=[
            pltpu.VMEM((block_rows, entries), jnp.bfloat16),
            pltpu.VMEM((side, side), jnp.float32),
            pltpu.VMEM((side, side), jnp.float32),
            pltpu.SemaphoreType.DMA((3,)),
        ],
        compiler_params=pltpu.CompilerParams(vmem_limit_bytes=VMEM),
        cost_estimate=pl.CostEstimate(
            flops=block_rows * entries * 4096, bytes_accessed=queries.size * 4, transcendentals=0
        ),
        name="condition",
    )(*operands)


STEP = 256
MASKS = (0, 2, 3, 1)


def score_rows(queries, store, place, first):
    return dot(store[0, place, pl.ds(first, queries.shape[1])], queries.T)


def own_kernel(queries, far_store, out, store, semaphores):
    def copy_of(step):
        place = pl.ds(pl.multiple_of(step * STEP, STEP), STEP)
        source = far_store.at[0, place, pl.ds(0, store.shape[2])]
        return pltpu.make_async_copy(source, store.at[0, place], semaphores.at[step])

    steps = store.shape[1] // STEP
    for step in range(steps):
        copy_of(step).start()
    padded = jnp.concatenate([jnp.zeros_like(queries)] * 3 + [queries[...]], axis=0)

    def one(step, carry):
        copy_of(step).wait()
        place = pl.ds(pl.multiple_of(step * STEP, STEP), STEP)
        out[place, :] = score_rows(padded, store, place, 0)
        return carry

    lax.fori_loop(0, steps, one, 0)


def score_cost(count, width, examples):
    return pl.CostEstimate(
        flops=2 * count * width * examples, bytes_accessed=examples * width * 2, transcendentals=0
    )


def score_own(queries, store):
    rows, entries = queries.shape
    examples = store.shape[1]
    return pl.pallas_call(
        own_kernel,
        in_specs=in_vmem(1) + [pl.BlockSpec(memory_space=pltpu.HBM)],
        out_specs=in_vmem(1)[0],
        out_shape=jax.ShapeDtypeStruct((examples, 4 * rows), jnp.float32),
        scratch_shapes=[
            pltpu.VMEM((1, examples, entries), store.dtype),
            pltpu.SemaphoreType.DMA((examples // STEP,)),
        ],
        compiler_params=pltpu.CompilerParams(vmem_limit_bytes=VMEM),
        cost_estimate=score_cost(rows, entries, examples),
        name="score_own",
    )(queries, pltpu.with_memory_space_constraint(store, pltpu.HBM))


def stacked(*blocks):
    return jnp.concatenate([block[...] for block in blocks], axis=0)


def low_kernel(near, far, last, store, own_low, out):
    queries = stacked(near, far, last)
    queries = jnp.concatenate([queries, jnp.zeros_like(near)], axis=0)
    out[...] = score_rows(queries, store, slice(None), 0) + own_low[...]


def score_low(near, far, last, store, own_low):
    rows, width = far.shape
    examples = store.shape[1]
    return pl.pallas_call(
        low_kernel,
        in_specs=in_vmem(5),
        out_specs=in_vmem(1)[0],
        out_shape=jax.ShapeDtypeStruct((examples, 4 * rows), jnp.float32),
        compiler_params=pltpu.CompilerParams(vmem_limit_bytes=VMEM),
        cost_estimate=score_cost(3 * rows, width, examples),
        name="score_low",
    )(near, far, last, store, own_low)


def high_kernel(first, near, far, last, own, store, low, *refs):
    outs, total = refs[:-1], refs[-1]
    rows = own.shape[0]
    value = score_rows(stacked(near, far, last, own), store, slice(None), first) + low[...]
    total[...] = value.astype(total.dtype).T
    home = lax.bitwise_xor(lax.axis_index("blk"), lax.axis_index("layer"))
    for mask, out in zip(MASKS, outs):
        place = lax.bitwise_and(lax.bitwise_xor(home, mask) + 3, 3)
        out[...] = total[pl.ds(pl.multiple_of(place * rows, rows), rows), :]


def score_high(near, far, last, own, store, low):
    rows, width = far.shape
    examples = store.shape[1]
    return pl.pallas_call(
        functools.partial(high_kernel, store.shape[2] - width),
        in_specs=in_vmem(6),
        out_specs=in_vmem(4),
        out_shape=[jax.ShapeDtypeStruct((rows, examples), jnp.bfloat16)] * 4,
        scratch_shapes=[pltpu.VMEM((4 * rows, examples), jnp.bfloat16)],
        compiler_params=pltpu.CompilerParams(vmem_limit_bytes=VMEM),
        cost_estimate=score_cost(4 * rows, width, examples),
        name="score_high",
    )(near, far, last, own, store, low)


def write_rows(total, layers, listed, out):
    scaled = total / jnp.sqrt(jnp.float32(layers))
    tiles_here = out.shape[1] // TILE
    first = lax.axis_index("blk") * tiles_here
    for tile in range(tiles_here):
        hit = jnp.max(jnp.where(listed == first + tile, 1.0, 0.0), axis=1, keepdims=True)
        columns = slice(tile * TILE, (tile + 1) * TILE)
        out[:, columns] = jnp.where(hit > 0.0, scaled[:, columns], 0.0).astype(out.dtype)


def finish_kernel(layers, candidates, *refs):
    parts, out = refs[:-1], refs[-1]
    total = parts[0][...].astype(jnp.float32)
    for part in parts[1:]:
        total = total + part[...].astype(jnp.float32)
    write_rows(total, layers, candidates[...], out)


def finish(parts, candidates, layers):
    return pl.pallas_call(
        functools.partial(finish_kernel, layers),
        in_specs=in_vmem(1 + len(parts)),
        out_specs=in_vmem(1)[0],
        out_shape=jax.ShapeDtypeStruct(parts[0].shape, jnp.bfloat16),
        compiler_params=pltpu.CompilerParams(vmem_limit_bytes=VMEM),
        name="finish",
    )(candidates, *parts)


def permuted(value, axis, target_of):
    count = lax.axis_size(axis)
    return lax.ppermute(value, axis, [(source, target_of(source) % count) for source in range(count)])


def swapped(value, axis, mask):
    return permuted(value, axis, lambda source: source ^ mask)


def on_line(own, store, candidates, layers):
    far = [swapped(half, "blk", 2) for half in own]
    near = [swapped(half, "blk", 1) for half in own]
    own_low = score_own(own[0], store)
    far[0], near[0], own_low = lax.optimization_barrier((far[0], near[0], own_low))
    far[1], near[1] = lax.optimization_barrier((far[1], near[1]))
    last = [swapped(half, "blk", 1) for half in far]
    low_scores = score_low(near[0], far[0], last[0], store, own_low)
    parts = score_high(near[1], far[1], last[1], own[1], store, low_scores)
    received = [swapped(part, "layer", mask) for mask, part in zip(MASKS[1:], parts[1:])]
    return finish([parts[0]] + received, candidates, layers)


def on_ring(own, store, candidates, layers):
    count = lax.axis_size("blk")
    rows = own[0].shape[0]
    moving = jnp.concatenate(own, axis=1)

    def scores():
        return lax.dot_general(moving, store[0], (((1,), (1,)), ((), ())), preferred_element_type=jnp.float32)

    slots = [scores()]
    for _ in range(count - 1):
        moving = permuted(moving, "blk", lambda source: source + 1)
        slots.append(scores())
    turns = lax.rem(lax.axis_index("blk") - jnp.arange(count) + count, count)
    total = jnp.stack(slots)[turns].reshape(layers, count * rows // layers, store.shape[1])
    parts = lax.all_to_all(total.astype(jnp.bfloat16), "layer", 0, 0)
    return finish([parts[layer] for layer in range(layers)], candidates, layers)


def per_device(queries, store, left_factor, right_factor, candidates):
    layers, count = lax.axis_size("layer"), lax.axis_size("blk")
    own = [condition(queries, left_factor, right_factor, half) for half in range(2)]
    way = on_line if layers == 4 and count == 4 else on_ring
    return way(own, store, candidates, layers)


def solution(mesh):
    placed = (
        P("layer", ("parts", "blk"), None),
        P("layer", ("parts", "blk"), None),
        P("layer", None, None),
        P("layer", None, None),
        P(("parts", "layer"), None),
    )
    return jax.shard_map(
        per_device,
        mesh=mesh,
        in_specs=placed,
        out_specs=P(("parts", "layer"), "blk"),
        check_vma=False,
    )
```

```python
import functools

import jax
import jax.numpy as jnp
from jax import lax
from jax.experimental import pallas as pl
from jax.experimental.pallas import tpu as pltpu
from jax.sharding import PartitionSpec as P

TILE = 128
GROUP = 32
LANES = 128
ROWS = 8
VMEM = 24 * 1024 * 1024


def two_parts(value):
    high = value.astype(jnp.bfloat16)
    low = (value - high.astype(jnp.float32)).astype(jnp.bfloat16)
    return high, low


def iota(shape, axis):
    return lax.broadcasted_iota(jnp.int32, shape, axis)


def dot(left, right):
    return jnp.dot(left, right, preferred_element_type=jnp.float32)


def ones_where(condition):
    return jnp.where(condition, 1.0, 0.0).astype(jnp.bfloat16)


def spread_left(left_factor, first, count):
    side = left_factor.shape[0]
    wide = ones_where(iota((side, side * ROWS), 1) // ROWS == iota((side, side * ROWS), 0))
    parts = [part[first : first + count] for part in two_parts(left_factor)]
    columns = dot(jnp.concatenate(parts, axis=0), wide).reshape(2, count, 1, side * ROWS)
    same = iota((1, ROWS, side * ROWS), 1) == iota((1, ROWS, side * ROWS), 2) % ROWS
    parts = [jnp.where(same, columns[part], 0.0).reshape(count * ROWS, side * ROWS) for part in range(2)]
    return jnp.concatenate([part.astype(jnp.bfloat16) for part in parts], axis=1)


def spread_right(right_factor):
    side = right_factor.shape[0]
    wide = ones_where(iota((side, 4 * side), 1) % side == iota((side, 4 * side), 0))
    same = iota((4 * side, 4 * side), 0) // side == iota((4 * side, 4 * side), 1) // side
    high, low = [
        jnp.where(same, jnp.concatenate([dot(part, wide)] * 4, axis=0), 0.0).astype(jnp.bfloat16)
        for part in two_parts(right_factor)
    ]
    return jnp.concatenate([high, low, high], axis=0)


def condition_kernel(first, count, queries_in, left_in, right_in, out, queries, left_factor, right_factor, arrived):
    copies = [
        pltpu.make_async_copy(source.at[0], target, arrived.at[place])
        for place, (source, target) in enumerate(
            [(left_in, left_factor), (right_in, right_factor), (queries_in, queries)]
        )
    ]
    for copy in copies:
        copy.start()
    side = left_factor.shape[0]
    pairs = side // 2
    copies[0].wait()
    copies[1].wait()
    left = spread_left(left_factor[...], first, count)
    right = spread_right(right_factor[...])
    low_half = iota((1, 1, LANES), 2) < side
    copies[2].wait()
    for block in range(queries.shape[0] // GROUP):
        rows = pl.ds(block * GROUP, GROUP)
        straight = jnp.stack(
            [queries[rows, pl.ds(pair * LANES, LANES)].astype(jnp.float32) for pair in range(pairs)]
        )
        swapped = pltpu.roll(straight, side, 2).reshape(pairs, GROUP // ROWS, ROWS, LANES)
        straight = straight.reshape(pairs, GROUP // ROWS, ROWS, LANES)
        columns = []
        for group in (0, 2):
            even = jnp.where(low_half, straight[:, group], swapped[:, group + 1])
            odd = jnp.where(low_half, swapped[:, group], straight[:, group + 1])
            columns.append(jnp.stack([even, odd], axis=1).reshape(side * ROWS, LANES))
        grid = jnp.concatenate(columns, axis=1).astype(jnp.bfloat16)
        halfway = dot(left, jnp.concatenate([grid, grid], axis=0))
        high, low = two_parts(halfway)
        result = dot(jnp.concatenate([high, high, low], axis=1), right)
        result = result.reshape(count // 2, 2, ROWS, 2 * LANES)
        groups = []
        for half in range(2):
            even = result[:, 0, :, half * LANES : (half + 1) * LANES]
            odd = result[:, 1, :, half * LANES : (half + 1) * LANES]
            groups.append(jnp.where(low_half, even, pltpu.roll(odd, side, 2)))
            groups.append(jnp.where(low_half, pltpu.roll(even, side, 2), odd))
        done = jnp.concatenate(groups, axis=1).astype(jnp.bfloat16)
        for pair in range(count // 2):
            out[rows, pl.ds(pair * LANES, LANES)] = done[pair]


def in_vmem(count):
    return [pl.BlockSpec(memory_space=pltpu.VMEM)] * count


def condition(queries, left_factor, right_factor, half):
    unused, block_rows, entries = queries.shape
    side = left_factor.shape[1]
    operands = [pltpu.with_memory_space_constraint(value, pltpu.HBM) for value in (queries, left_factor, right_factor)]
    return pl.pallas_call(
        functools.partial(condition_kernel, half * side // 2, side // 2),
        in_specs=[pl.BlockSpec(memory_space=pltpu.HBM)] * 3,
        out_specs=in_vmem(1)[0],
        out_shape=jax.ShapeDtypeStruct((block_rows, entries // 2), jnp.bfloat16),
        scratch_shapes=[
            pltpu.VMEM((block_rows, entries), jnp.bfloat16),
            pltpu.VMEM((side, side), jnp.float32),
            pltpu.VMEM((side, side), jnp.float32),
            pltpu.SemaphoreType.DMA((3,)),
        ],
        compiler_params=pltpu.CompilerParams(vmem_limit_bytes=VMEM),
        cost_estimate=pl.CostEstimate(
            flops=block_rows * entries * 4096, bytes_accessed=queries.size * 4, transcendentals=0
        ),
        name="condition",
    )(*operands)


STEP = 256
MASKS = (3, 1, 2, 0)


def score_rows(queries, store, place, first):
    return dot(store[0, place, pl.ds(first, queries.shape[1])], queries.T)


def own_kernel(queries, far_store, out, store, semaphores):
    def copy_of(step):
        place = pl.ds(pl.multiple_of(step * STEP, STEP), STEP)
        source = far_store.at[0, place, pl.ds(0, store.shape[2])]
        return pltpu.make_async_copy(source, store.at[0, place], semaphores.at[step])

    steps = store.shape[1] // STEP
    for step in range(steps):
        copy_of(step).start()
    padded = jnp.concatenate([jnp.zeros_like(queries)] * 3 + [queries[...]], axis=0)

    def one(step, carry):
        copy_of(step).wait()
        place = pl.ds(pl.multiple_of(step * STEP, STEP), STEP)
        out[place, :] = score_rows(padded, store, place, 0)
        return carry

    lax.fori_loop(0, steps, one, 0)


def score_cost(count, width, examples):
    return pl.CostEstimate(
        flops=2 * count * width * examples, bytes_accessed=examples * width * 2, transcendentals=0
    )


def score_own(queries, store):
    rows, entries = queries.shape
    examples = store.shape[1]
    return pl.pallas_call(
        own_kernel,
        in_specs=in_vmem(1) + [pl.BlockSpec(memory_space=pltpu.HBM)],
        out_specs=in_vmem(1)[0],
        out_shape=jax.ShapeDtypeStruct((examples, 4 * rows), jnp.float32),
        scratch_shapes=[
            pltpu.VMEM((1, examples, entries), store.dtype),
            pltpu.SemaphoreType.DMA((examples // STEP,)),
        ],
        compiler_params=pltpu.CompilerParams(vmem_limit_bytes=VMEM),
        cost_estimate=score_cost(rows, entries, examples),
        name="score_own",
    )(queries, pltpu.with_memory_space_constraint(store, pltpu.HBM))


def stacked(*blocks):
    return jnp.concatenate([block[...] for block in blocks], axis=0)


def low_kernel(near, far, last, store, own_low, out):
    queries = stacked(near, far, last)
    queries = jnp.concatenate([queries, jnp.zeros_like(near)], axis=0)
    out[...] = score_rows(queries, store, slice(None), 0) + own_low[...]


def score_low(near, far, last, store, own_low):
    rows, width = far.shape
    examples = store.shape[1]
    return pl.pallas_call(
        low_kernel,
        in_specs=in_vmem(5),
        out_specs=in_vmem(1)[0],
        out_shape=jax.ShapeDtypeStruct((examples, 4 * rows), jnp.float32),
        compiler_params=pltpu.CompilerParams(vmem_limit_bytes=VMEM),
        cost_estimate=score_cost(3 * rows, width, examples),
        name="score_low",
    )(near, far, last, store, own_low)


def high_kernel(first, near, far, last, own, store, low, *refs):
    outs, total = refs[:-1], refs[-1]
    rows = own.shape[0]
    total[...] = (score_rows(stacked(near, far, last, own), store, slice(None), first) + low[...]).T
    home = lax.bitwise_xor(lax.axis_index("blk"), lax.axis_index("layer"))
    for mask, out in zip(MASKS, outs):
        place = lax.bitwise_and(lax.bitwise_xor(home, mask) + 3, 3)
        out[...] = total[pl.ds(pl.multiple_of(place * rows, rows), rows), :].astype(out.dtype)


def score_high(near, far, last, own, store, low):
    rows, width = far.shape
    examples = store.shape[1]
    kinds = {0: jnp.float32, 1: jnp.bfloat16, 2: jnp.float32, 3: jnp.bfloat16}
    return pl.pallas_call(
        functools.partial(high_kernel, store.shape[2] - width),
        in_specs=in_vmem(6),
        out_specs=in_vmem(4),
        out_shape=[jax.ShapeDtypeStruct((rows, examples), kinds[mask]) for mask in MASKS],
        scratch_shapes=[pltpu.VMEM((4 * rows, examples), jnp.float32)],
        compiler_params=pltpu.CompilerParams(vmem_limit_bytes=VMEM),
        cost_estimate=score_cost(4 * rows, width, examples),
        name="score_high",
    )(near, far, last, own, store, low)


def add_kernel(kept, received, out):
    out[...] = (kept[...] + received[...].astype(jnp.float32)).astype(out.dtype)


def add(kept, received):
    return pl.pallas_call(
        add_kernel,
        in_specs=in_vmem(2),
        out_specs=in_vmem(1)[0],
        out_shape=jax.ShapeDtypeStruct(received.shape, received.dtype),
        compiler_params=pltpu.CompilerParams(vmem_limit_bytes=VMEM),
        name="add",
    )(kept, received)


def write_rows(total, layers, listed, out):
    scaled = total / jnp.sqrt(jnp.float32(layers))
    tiles_here = out.shape[1] // TILE
    first = lax.axis_index("blk") * tiles_here
    for tile in range(tiles_here):
        hit = jnp.max(jnp.where(listed == first + tile, 1.0, 0.0), axis=1, keepdims=True)
        columns = slice(tile * TILE, (tile + 1) * TILE)
        out[:, columns] = jnp.where(hit > 0.0, scaled[:, columns], 0.0).astype(out.dtype)


def finish_kernel(layers, candidates, *refs):
    parts, out = refs[:-1], refs[-1]
    total = parts[0][...].astype(jnp.float32)
    for part in parts[1:]:
        total = total + part[...].astype(jnp.float32)
    write_rows(total, layers, candidates[...], out)


def finish(parts, candidates, layers):
    return pl.pallas_call(
        functools.partial(finish_kernel, layers),
        in_specs=in_vmem(1 + len(parts)),
        out_specs=in_vmem(1)[0],
        out_shape=jax.ShapeDtypeStruct(parts[0].shape, jnp.bfloat16),
        compiler_params=pltpu.CompilerParams(vmem_limit_bytes=VMEM),
        name="finish",
    )(candidates, *parts)


def permuted(value, axis, target_of):
    count = lax.axis_size(axis)
    return lax.ppermute(value, axis, [(source, target_of(source) % count) for source in range(count)])


def swapped(value, axis, mask):
    return permuted(value, axis, lambda source: source ^ mask)


def on_line(own, store, candidates, layers):
    far = [swapped(half, "blk", 2) for half in own]
    near = [swapped(half, "blk", 1) for half in own]
    own_low = score_own(own[0], store)
    far[0], near[0], own_low = lax.optimization_barrier((far[0], near[0], own_low))
    far[1], near[1] = lax.optimization_barrier((far[1], near[1]))
    last = [swapped(half, "blk", 1) for half in far]
    low_scores = score_low(near[0], far[0], last[0], store, own_low)
    across, beside, kept, home = score_high(near[1], far[1], last[1], own[1], store, low_scores)
    across = swapped(add(kept, swapped(across, "layer", 1)), "layer", 2)
    return finish([home, swapped(beside, "layer", 1), across], candidates, layers)


def on_ring(own, store, candidates, layers):
    count = lax.axis_size("blk")
    rows = own[0].shape[0]
    moving = jnp.concatenate(own, axis=1)

    def scores():
        return lax.dot_general(moving, store[0], (((1,), (1,)), ((), ())), preferred_element_type=jnp.float32)

    slots = [scores()]
    for _ in range(count - 1):
        moving = permuted(moving, "blk", lambda source: source + 1)
        slots.append(scores())
    turns = lax.rem(lax.axis_index("blk") - jnp.arange(count) + count, count)
    total = jnp.stack(slots)[turns].reshape(layers, count * rows // layers, store.shape[1])
    parts = lax.all_to_all(total.astype(jnp.bfloat16), "layer", 0, 0)
    return finish([parts[layer] for layer in range(layers)], candidates, layers)


def per_device(queries, store, left_factor, right_factor, candidates):
    layers, count = lax.axis_size("layer"), lax.axis_size("blk")
    own = [condition(queries, left_factor, right_factor, half) for half in range(2)]
    way = on_line if layers == 4 and count == 4 else on_ring
    return way(own, store, candidates, layers)


def solution(mesh):
    placed = (
        P("layer", ("parts", "blk"), None),
        P("layer", ("parts", "blk"), None),
        P("layer", None, None),
        P("layer", None, None),
        P(("parts", "layer"), None),
    )
    return jax.shard_map(
        per_device,
        mesh=mesh,
        in_specs=placed,
        out_specs=P(("parts", "layer"), "blk"),
        check_vma=False,
    )
```

```python
import functools

import jax
import jax.numpy as jnp
from jax import lax
from jax.experimental import pallas as pl
from jax.experimental.pallas import tpu as pltpu
from jax.sharding import PartitionSpec as P

TILE = 128
GROUP = 32
LANES = 128
ROWS = 8
VMEM = 24 * 1024 * 1024


def two_parts(value):
    high = value.astype(jnp.bfloat16)
    low = (value - high.astype(jnp.float32)).astype(jnp.bfloat16)
    return high, low


def iota(shape, axis):
    return lax.broadcasted_iota(jnp.int32, shape, axis)


def dot(left, right):
    return jnp.dot(left, right, preferred_element_type=jnp.float32)


def ones_where(condition):
    return jnp.where(condition, 1.0, 0.0).astype(jnp.bfloat16)


def spread_left(left_factor, first, count):
    side = left_factor.shape[0]
    wide = ones_where(iota((side, side * ROWS), 1) // ROWS == iota((side, side * ROWS), 0))
    parts = [part[first : first + count] for part in two_parts(left_factor)]
    columns = dot(jnp.concatenate(parts, axis=0), wide).reshape(2, count, 1, side * ROWS)
    same = iota((1, ROWS, side * ROWS), 1) == iota((1, ROWS, side * ROWS), 2) % ROWS
    parts = [jnp.where(same, columns[part], 0.0).reshape(count * ROWS, side * ROWS) for part in range(2)]
    return jnp.concatenate([part.astype(jnp.bfloat16) for part in parts], axis=1)


def spread_right(right_factor):
    side = right_factor.shape[0]
    wide = ones_where(iota((side, 4 * side), 1) % side == iota((side, 4 * side), 0))
    same = iota((4 * side, 4 * side), 0) // side == iota((4 * side, 4 * side), 1) // side
    high, low = [
        jnp.where(same, jnp.concatenate([dot(part, wide)] * 4, axis=0), 0.0).astype(jnp.bfloat16)
        for part in two_parts(right_factor)
    ]
    return jnp.concatenate([high, low, high], axis=0)


def condition_kernel(first, count, queries_in, left_in, right_in, out, queries, left_factor, right_factor, arrived):
    copies = [
        pltpu.make_async_copy(source.at[0], target, arrived.at[place])
        for place, (source, target) in enumerate(
            [(left_in, left_factor), (right_in, right_factor), (queries_in, queries)]
        )
    ]
    for copy in copies:
        copy.start()
    side = left_factor.shape[0]
    pairs = side // 2
    copies[0].wait()
    copies[1].wait()
    left = spread_left(left_factor[...], first, count)
    right = spread_right(right_factor[...])
    low_half = iota((1, 1, LANES), 2) < side
    copies[2].wait()
    for block in range(queries.shape[0] // GROUP):
        rows = pl.ds(block * GROUP, GROUP)
        straight = jnp.stack(
            [queries[rows, pl.ds(pair * LANES, LANES)].astype(jnp.float32) for pair in range(pairs)]
        )
        swapped = pltpu.roll(straight, side, 2).reshape(pairs, GROUP // ROWS, ROWS, LANES)
        straight = straight.reshape(pairs, GROUP // ROWS, ROWS, LANES)
        columns = []
        for group in (0, 2):
            even = jnp.where(low_half, straight[:, group], swapped[:, group + 1])
            odd = jnp.where(low_half, swapped[:, group], straight[:, group + 1])
            columns.append(jnp.stack([even, odd], axis=1).reshape(side * ROWS, LANES))
        grid = jnp.concatenate(columns, axis=1).astype(jnp.bfloat16)
        halfway = dot(left, jnp.concatenate([grid, grid], axis=0))
        high, low = two_parts(halfway)
        result = dot(jnp.concatenate([high, high, low], axis=1), right)
        result = result.reshape(count // 2, 2, ROWS, 2 * LANES)
        groups = []
        for half in range(2):
            even = result[:, 0, :, half * LANES : (half + 1) * LANES]
            odd = result[:, 1, :, half * LANES : (half + 1) * LANES]
            groups.append(jnp.where(low_half, even, pltpu.roll(odd, side, 2)))
            groups.append(jnp.where(low_half, pltpu.roll(even, side, 2), odd))
        done = jnp.concatenate(groups, axis=1).astype(jnp.bfloat16)
        for pair in range(count // 2):
            out[rows, pl.ds(pair * LANES, LANES)] = done[pair]


def in_vmem(count):
    return [pl.BlockSpec(memory_space=pltpu.VMEM)] * count


def condition(queries, left_factor, right_factor, half):
    unused, block_rows, entries = queries.shape
    side = left_factor.shape[1]
    operands = [pltpu.with_memory_space_constraint(value, pltpu.HBM) for value in (queries, left_factor, right_factor)]
    return pl.pallas_call(
        functools.partial(condition_kernel, half * side // 2, side // 2),
        in_specs=[pl.BlockSpec(memory_space=pltpu.HBM)] * 3,
        out_specs=in_vmem(1)[0],
        out_shape=jax.ShapeDtypeStruct((block_rows, entries // 2), jnp.bfloat16),
        scratch_shapes=[
            pltpu.VMEM((block_rows, entries), jnp.bfloat16),
            pltpu.VMEM((side, side), jnp.float32),
            pltpu.VMEM((side, side), jnp.float32),
            pltpu.SemaphoreType.DMA((3,)),
        ],
        compiler_params=pltpu.CompilerParams(vmem_limit_bytes=VMEM),
        cost_estimate=pl.CostEstimate(
            flops=block_rows * entries * 4096, bytes_accessed=queries.size * 4, transcendentals=0
        ),
        name="condition",
    )(*operands)


STEP = 256
MASKS = (3, 1, 2, 0)


def score_rows(queries, store, place, first):
    return dot(store[0, place, pl.ds(first, queries.shape[1])], queries.T)


def own_kernel(queries, far_store, out, store, semaphores):
    def copy_of(step):
        place = pl.ds(pl.multiple_of(step * STEP, STEP), STEP)
        source = far_store.at[0, place, pl.ds(0, store.shape[2])]
        return pltpu.make_async_copy(source, store.at[0, place], semaphores.at[step])

    steps = store.shape[1] // STEP
    for step in range(steps):
        copy_of(step).start()
    padded = jnp.concatenate([jnp.zeros_like(queries)] * 3 + [queries[...]], axis=0)

    def one(step, carry):
        copy_of(step).wait()
        place = pl.ds(pl.multiple_of(step * STEP, STEP), STEP)
        out[place, :] = score_rows(padded, store, place, 0)
        return carry

    lax.fori_loop(0, steps, one, 0)


def score_cost(count, width, examples):
    return pl.CostEstimate(
        flops=2 * count * width * examples, bytes_accessed=examples * width * 2, transcendentals=0
    )


def score_own(queries, store):
    rows, entries = queries.shape
    examples = store.shape[1]
    return pl.pallas_call(
        own_kernel,
        in_specs=in_vmem(1) + [pl.BlockSpec(memory_space=pltpu.HBM)],
        out_specs=in_vmem(1)[0],
        out_shape=jax.ShapeDtypeStruct((examples, 4 * rows), jnp.float32),
        scratch_shapes=[
            pltpu.VMEM((1, examples, entries), store.dtype),
            pltpu.SemaphoreType.DMA((examples // STEP,)),
        ],
        compiler_params=pltpu.CompilerParams(vmem_limit_bytes=VMEM),
        cost_estimate=score_cost(rows, entries, examples),
        name="score_own",
    )(queries, pltpu.with_memory_space_constraint(store, pltpu.HBM))


def stacked(*blocks):
    return jnp.concatenate([block[...] for block in blocks], axis=0)


def low_kernel(near, far, last, store, own_low, out):
    queries = stacked(near, far, last)
    queries = jnp.concatenate([queries, jnp.zeros_like(near)], axis=0)
    out[...] = score_rows(queries, store, slice(None), 0) + own_low[...]


def score_low(near, far, last, store, own_low):
    rows, width = far.shape
    examples = store.shape[1]
    return pl.pallas_call(
        low_kernel,
        in_specs=in_vmem(5),
        out_specs=in_vmem(1)[0],
        out_shape=jax.ShapeDtypeStruct((examples, 4 * rows), jnp.float32),
        compiler_params=pltpu.CompilerParams(vmem_limit_bytes=VMEM),
        cost_estimate=score_cost(3 * rows, width, examples),
        name="score_low",
    )(near, far, last, store, own_low)


def high_kernel(first, near, far, last, own, store, low, *refs):
    outs, total = refs[:-1], refs[-1]
    rows = own.shape[0]
    total[...] = (score_rows(stacked(near, far, last, own), store, slice(None), first) + low[...]).T
    home = lax.bitwise_xor(lax.axis_index("blk"), lax.axis_index("layer"))
    for mask, out in zip(MASKS, outs):
        place = lax.bitwise_and(lax.bitwise_xor(home, mask) + 3, 3)
        out[...] = total[pl.ds(pl.multiple_of(place * rows, rows), rows), :].astype(out.dtype)


def score_high(near, far, last, own, store, low):
    rows, width = far.shape
    examples = store.shape[1]
    kinds = {0: jnp.float32, 1: jnp.bfloat16, 2: jnp.float32, 3: jnp.bfloat16}
    return pl.pallas_call(
        functools.partial(high_kernel, store.shape[2] - width),
        in_specs=in_vmem(6),
        out_specs=in_vmem(4),
        out_shape=[jax.ShapeDtypeStruct((rows, examples), kinds[mask]) for mask in MASKS],
        scratch_shapes=[pltpu.VMEM((4 * rows, examples), jnp.float32)],
        compiler_params=pltpu.CompilerParams(vmem_limit_bytes=VMEM),
        cost_estimate=score_cost(4 * rows, width, examples),
        name="score_high",
    )(near, far, last, own, store, low)


def add_kernel(kept, received, out):
    out[...] = (kept[...] + received[...].astype(jnp.float32)).astype(out.dtype)


def add(kept, received):
    return pl.pallas_call(
        add_kernel,
        in_specs=in_vmem(2),
        out_specs=in_vmem(1)[0],
        out_shape=jax.ShapeDtypeStruct(received.shape, received.dtype),
        compiler_params=pltpu.CompilerParams(vmem_limit_bytes=VMEM),
        name="add",
    )(kept, received)


def write_rows(total, layers, listed, out):
    scaled = total / jnp.sqrt(jnp.float32(layers))
    tiles_here = out.shape[1] // TILE
    first = lax.axis_index("blk") * tiles_here
    for tile in range(tiles_here):
        hit = jnp.max(jnp.where(listed == first + tile, 1.0, 0.0), axis=1, keepdims=True)
        columns = slice(tile * TILE, (tile + 1) * TILE)
        out[:, columns] = jnp.where(hit > 0.0, scaled[:, columns], 0.0).astype(out.dtype)


def finish_kernel(layers, candidates, *refs):
    parts, out = refs[:-1], refs[-1]
    total = parts[0][...].astype(jnp.float32)
    for part in parts[1:]:
        total = total + part[...].astype(jnp.float32)
    write_rows(total, layers, candidates[...], out)


def finish(parts, candidates, layers):
    return pl.pallas_call(
        functools.partial(finish_kernel, layers),
        in_specs=in_vmem(1 + len(parts)),
        out_specs=in_vmem(1)[0],
        out_shape=jax.ShapeDtypeStruct(parts[0].shape, jnp.bfloat16),
        compiler_params=pltpu.CompilerParams(vmem_limit_bytes=VMEM),
        name="finish",
    )(candidates, *parts)


def permuted(value, axis, target_of):
    count = lax.axis_size(axis)
    return lax.ppermute(value, axis, [(source, target_of(source) % count) for source in range(count)])


def swapped(value, axis, mask):
    return permuted(value, axis, lambda source: source ^ mask)


def on_line(own, store, candidates, layers):
    far = [swapped(half, "blk", 2) for half in own]
    near = [swapped(half, "blk", 1) for half in own]
    own_low = score_own(own[0], store)
    near[0], far[0], own_low = lax.optimization_barrier((near[0], far[0], own_low))
    near[1], far[1] = lax.optimization_barrier((near[1], far[1]))
    last = [swapped(half, "blk", 1) for half in far]
    low_scores = score_low(near[0], far[0], last[0], store, own_low)
    across, beside, kept, home = score_high(near[1], far[1], last[1], own[1], store, low_scores)
    across = swapped(add(kept, swapped(across, "layer", 1)), "layer", 2)
    return finish([home, swapped(beside, "layer", 1), across], candidates, layers)


def on_ring(own, store, candidates, layers):
    count = lax.axis_size("blk")
    rows = own[0].shape[0]
    moving = jnp.concatenate(own, axis=1)

    def scores():
        return lax.dot_general(moving, store[0], (((1,), (1,)), ((), ())), preferred_element_type=jnp.float32)

    slots = [scores()]
    for _ in range(count - 1):
        moving = permuted(moving, "blk", lambda source: source + 1)
        slots.append(scores())
    turns = lax.rem(lax.axis_index("blk") - jnp.arange(count) + count, count)
    total = jnp.stack(slots)[turns].reshape(layers, count * rows // layers, store.shape[1])
    parts = lax.all_to_all(total.astype(jnp.bfloat16), "layer", 0, 0)
    return finish([parts[layer] for layer in range(layers)], candidates, layers)


def per_device(queries, store, left_factor, right_factor, candidates):
    layers, count = lax.axis_size("layer"), lax.axis_size("blk")
    own = [condition(queries, left_factor, right_factor, half) for half in range(2)]
    way = on_line if layers == 4 and count == 4 else on_ring
    return way(own, store, candidates, layers)


def solution(mesh):
    placed = (
        P("layer", ("parts", "blk"), None),
        P("layer", ("parts", "blk"), None),
        P("layer", None, None),
        P("layer", None, None),
        P(("parts", "layer"), None),
    )
    return jax.shard_map(
        per_device,
        mesh=mesh,
        in_specs=placed,
        out_specs=P(("parts", "layer"), "blk"),
        check_vma=False,
    )
```

```python
import functools

import jax
import jax.numpy as jnp
from jax import lax
from jax.experimental import pallas as pl
from jax.experimental.pallas import tpu as pltpu
from jax.sharding import PartitionSpec as P

TILE = 128
GROUP = 32
LANES = 128
ROWS = 8
VMEM = 24 * 1024 * 1024


def two_parts(value):
    high = value.astype(jnp.bfloat16)
    low = (value - high.astype(jnp.float32)).astype(jnp.bfloat16)
    return high, low


def iota(shape, axis):
    return lax.broadcasted_iota(jnp.int32, shape, axis)


def dot(left, right):
    return jnp.dot(left, right, preferred_element_type=jnp.float32)


def ones_where(condition):
    return jnp.where(condition, 1.0, 0.0).astype(jnp.bfloat16)


def spread_left(left_factor, first, count):
    side = left_factor.shape[0]
    wide = ones_where(iota((side, side * ROWS), 1) // ROWS == iota((side, side * ROWS), 0))
    parts = [part[first : first + count] for part in two_parts(left_factor)]
    columns = dot(jnp.concatenate(parts, axis=0), wide).reshape(2, count, 1, side * ROWS)
    same = iota((1, ROWS, side * ROWS), 1) == iota((1, ROWS, side * ROWS), 2) % ROWS
    parts = [jnp.where(same, columns[part], 0.0).reshape(count * ROWS, side * ROWS) for part in range(2)]
    return jnp.concatenate([part.astype(jnp.bfloat16) for part in parts], axis=1)


def spread_right(right_factor):
    side = right_factor.shape[0]
    wide = ones_where(iota((side, 4 * side), 1) % side == iota((side, 4 * side), 0))
    same = iota((4 * side, 4 * side), 0) // side == iota((4 * side, 4 * side), 1) // side
    high, low = [
        jnp.where(same, jnp.concatenate([dot(part, wide)] * 4, axis=0), 0.0).astype(jnp.bfloat16)
        for part in two_parts(right_factor)
    ]
    return jnp.concatenate([high, low, high], axis=0)


def condition_kernel(first, count, queries_in, left_in, right_in, out, queries, left_factor, right_factor, arrived):
    copies = [
        pltpu.make_async_copy(source.at[0], target, arrived.at[place])
        for place, (source, target) in enumerate(
            [(left_in, left_factor), (right_in, right_factor), (queries_in, queries)]
        )
    ]
    for copy in copies:
        copy.start()
    side = left_factor.shape[0]
    pairs = side // 2
    copies[0].wait()
    copies[1].wait()
    left = spread_left(left_factor[...], first, count)
    right = spread_right(right_factor[...])
    low_half = iota((1, 1, LANES), 2) < side
    copies[2].wait()
    for block in range(queries.shape[0] // GROUP):
        rows = pl.ds(block * GROUP, GROUP)
        straight = jnp.stack(
            [queries[rows, pl.ds(pair * LANES, LANES)].astype(jnp.float32) for pair in range(pairs)]
        )
        swapped = pltpu.roll(straight, side, 2).reshape(pairs, GROUP // ROWS, ROWS, LANES)
        straight = straight.reshape(pairs, GROUP // ROWS, ROWS, LANES)
        columns = []
        for group in (0, 2):
            even = jnp.where(low_half, straight[:, group], swapped[:, group + 1])
            odd = jnp.where(low_half, swapped[:, group], straight[:, group + 1])
            columns.append(jnp.stack([even, odd], axis=1).reshape(side * ROWS, LANES))
        grid = jnp.concatenate(columns, axis=1).astype(jnp.bfloat16)
        halfway = dot(left, jnp.concatenate([grid, grid], axis=0))
        high, low = two_parts(halfway)
        result = dot(jnp.concatenate([high, high, low], axis=1), right)
        result = result.reshape(count // 2, 2, ROWS, 2 * LANES)
        groups = []
        for half in range(2):
            even = result[:, 0, :, half * LANES : (half + 1) * LANES]
            odd = result[:, 1, :, half * LANES : (half + 1) * LANES]
            groups.append(jnp.where(low_half, even, pltpu.roll(odd, side, 2)))
            groups.append(jnp.where(low_half, pltpu.roll(even, side, 2), odd))
        done = jnp.concatenate(groups, axis=1).astype(jnp.bfloat16)
        for pair in range(count // 2):
            out[rows, pl.ds(pair * LANES, LANES)] = done[pair]


def in_vmem(count):
    return [pl.BlockSpec(memory_space=pltpu.VMEM)] * count


def condition(queries, left_factor, right_factor, first, count):
    unused, block_rows, entries = queries.shape
    side = left_factor.shape[1]
    operands = [pltpu.with_memory_space_constraint(value, pltpu.HBM) for value in (queries, left_factor, right_factor)]
    return pl.pallas_call(
        functools.partial(condition_kernel, first, count),
        in_specs=[pl.BlockSpec(memory_space=pltpu.HBM)] * 3,
        out_specs=in_vmem(1)[0],
        out_shape=jax.ShapeDtypeStruct((block_rows, count * side), jnp.bfloat16),
        scratch_shapes=[
            pltpu.VMEM((block_rows, entries), jnp.bfloat16),
            pltpu.VMEM((side, side), jnp.float32),
            pltpu.VMEM((side, side), jnp.float32),
            pltpu.SemaphoreType.DMA((3,)),
        ],
        compiler_params=pltpu.CompilerParams(vmem_limit_bytes=VMEM),
        cost_estimate=pl.CostEstimate(
            flops=block_rows * entries * 4096, bytes_accessed=queries.size * 4, transcendentals=0
        ),
        name="condition",
    )(*operands)


STEP = 256
LOW_PART = 17
MASKS = (3, 1, 2, 0)


def score_rows(queries, store, place, first):
    return dot(store[0, place, pl.ds(first, queries.shape[1])], queries.T)


def own_kernel(queries, far_store, out, store, semaphores):
    def copy_of(step):
        place = pl.ds(pl.multiple_of(step * STEP, STEP), STEP)
        source = far_store.at[0, place, pl.ds(0, store.shape[2])]
        return pltpu.make_async_copy(source, store.at[0, place], semaphores.at[step])

    steps = store.shape[1] // STEP
    for step in range(steps):
        copy_of(step).start()
    padded = jnp.concatenate([jnp.zeros_like(queries)] * 3 + [queries[...]], axis=0)

    def one(step, carry):
        copy_of(step).wait()
        place = pl.ds(pl.multiple_of(step * STEP, STEP), STEP)
        out[place, :] = score_rows(padded, store, place, 0)
        return carry

    lax.fori_loop(0, steps, one, 0)


def score_cost(count, width, examples):
    return pl.CostEstimate(
        flops=2 * count * width * examples, bytes_accessed=examples * width * 2, transcendentals=0
    )


def score_own(queries, store):
    rows, entries = queries.shape
    examples = store.shape[1]
    return pl.pallas_call(
        own_kernel,
        in_specs=in_vmem(1) + [pl.BlockSpec(memory_space=pltpu.HBM)],
        out_specs=in_vmem(1)[0],
        out_shape=jax.ShapeDtypeStruct((examples, 4 * rows), jnp.float32),
        scratch_shapes=[
            pltpu.VMEM((1, examples, entries), store.dtype),
            pltpu.SemaphoreType.DMA((examples // STEP,)),
        ],
        compiler_params=pltpu.CompilerParams(vmem_limit_bytes=VMEM),
        cost_estimate=score_cost(rows, entries, examples),
        name="score_own",
    )(queries, pltpu.with_memory_space_constraint(store, pltpu.HBM))


def stacked(*blocks):
    return jnp.concatenate([block[...] for block in blocks], axis=0)


def low_kernel(near, far, last, store, own_low, out):
    queries = stacked(near, far, last)
    queries = jnp.concatenate([queries, jnp.zeros_like(near)], axis=0)
    out[...] = score_rows(queries, store, slice(None), 0) + own_low[...]


def score_low(near, far, last, store, own_low):
    rows, width = far.shape
    examples = store.shape[1]
    return pl.pallas_call(
        low_kernel,
        in_specs=in_vmem(5),
        out_specs=in_vmem(1)[0],
        out_shape=jax.ShapeDtypeStruct((examples, 4 * rows), jnp.float32),
        compiler_params=pltpu.CompilerParams(vmem_limit_bytes=VMEM),
        cost_estimate=score_cost(3 * rows, width, examples),
        name="score_low",
    )(near, far, last, store, own_low)


def high_kernel(first, near, far, last, own, store, low, *refs):
    outs, total = refs[:-1], refs[-1]
    rows = own.shape[0]
    total[...] = (score_rows(stacked(near, far, last, own), store, slice(None), first) + low[...]).T
    home = lax.bitwise_xor(lax.axis_index("blk"), lax.axis_index("layer"))
    for mask, out in zip(MASKS, outs):
        place = lax.bitwise_and(lax.bitwise_xor(home, mask) + 3, 3)
        out[...] = total[pl.ds(pl.multiple_of(place * rows, rows), rows), :].astype(out.dtype)


def score_high(near, far, last, own, store, low):
    rows, width = far.shape
    examples = store.shape[1]
    kinds = {0: jnp.float32, 1: jnp.bfloat16, 2: jnp.float32, 3: jnp.bfloat16}
    return pl.pallas_call(
        functools.partial(high_kernel, store.shape[2] - width),
        in_specs=in_vmem(6),
        out_specs=in_vmem(4),
        out_shape=[jax.ShapeDtypeStruct((rows, examples), kinds[mask]) for mask in MASKS],
        scratch_shapes=[pltpu.VMEM((4 * rows, examples), jnp.float32)],
        compiler_params=pltpu.CompilerParams(vmem_limit_bytes=VMEM),
        cost_estimate=score_cost(4 * rows, width, examples),
        name="score_high",
    )(near, far, last, own, store, low)


def add_kernel(kept, received, out):
    out[...] = (kept[...] + received[...].astype(jnp.float32)).astype(out.dtype)


def add(kept, received):
    return pl.pallas_call(
        add_kernel,
        in_specs=in_vmem(2),
        out_specs=in_vmem(1)[0],
        out_shape=jax.ShapeDtypeStruct(received.shape, received.dtype),
        compiler_params=pltpu.CompilerParams(vmem_limit_bytes=VMEM),
        name="add",
    )(kept, received)


def write_rows(total, layers, listed, out):
    scaled = total / jnp.sqrt(jnp.float32(layers))
    tiles_here = out.shape[1] // TILE
    first = lax.axis_index("blk") * tiles_here
    for tile in range(tiles_here):
        hit = jnp.max(jnp.where(listed == first + tile, 1.0, 0.0), axis=1, keepdims=True)
        columns = slice(tile * TILE, (tile + 1) * TILE)
        out[:, columns] = jnp.where(hit > 0.0, scaled[:, columns], 0.0).astype(out.dtype)


def finish_kernel(layers, candidates, *refs):
    parts, out = refs[:-1], refs[-1]
    total = parts[0][...].astype(jnp.float32)
    for part in parts[1:]:
        total = total + part[...].astype(jnp.float32)
    write_rows(total, layers, candidates[...], out)


def finish(parts, candidates, layers):
    return pl.pallas_call(
        functools.partial(finish_kernel, layers),
        in_specs=in_vmem(1 + len(parts)),
        out_specs=in_vmem(1)[0],
        out_shape=jax.ShapeDtypeStruct(parts[0].shape, jnp.bfloat16),
        compiler_params=pltpu.CompilerParams(vmem_limit_bytes=VMEM),
        name="finish",
    )(candidates, *parts)


def permuted(value, axis, target_of):
    count = lax.axis_size(axis)
    return lax.ppermute(value, axis, [(source, target_of(source) % count) for source in range(count)])


def swapped(value, axis, mask):
    return permuted(value, axis, lambda source: source ^ mask)


def on_line(own, store, candidates, layers):
    far = [swapped(half, "blk", 2) for half in own]
    near = [swapped(half, "blk", 1) for half in own]
    own_low = score_own(own[0], store)
    near[0], far[0], own_low = lax.optimization_barrier((near[0], far[0], own_low))
    near[1], far[1] = lax.optimization_barrier((near[1], far[1]))
    last = [swapped(half, "blk", 1) for half in far]
    low_scores = score_low(near[0], far[0], last[0], store, own_low)
    across, beside, kept, home = score_high(near[1], far[1], last[1], own[1], store, low_scores)
    across = swapped(add(kept, swapped(across, "layer", 1)), "layer", 2)
    return finish([home, swapped(beside, "layer", 1), across], candidates, layers)


def on_ring(own, store, candidates, layers):
    count = lax.axis_size("blk")
    rows = own[0].shape[0]
    moving = jnp.concatenate(own, axis=1)

    def scores():
        return lax.dot_general(moving, store[0], (((1,), (1,)), ((), ())), preferred_element_type=jnp.float32)

    slots = [scores()]
    for _ in range(count - 1):
        moving = permuted(moving, "blk", lambda source: source + 1)
        slots.append(scores())
    turns = lax.rem(lax.axis_index("blk") - jnp.arange(count) + count, count)
    total = jnp.stack(slots)[turns].reshape(layers, count * rows // layers, store.shape[1])
    parts = lax.all_to_all(total.astype(jnp.bfloat16), "layer", 0, 0)
    return finish([parts[layer] for layer in range(layers)], candidates, layers)


def per_device(queries, store, left_factor, right_factor, candidates):
    layers, count = lax.axis_size("layer"), lax.axis_size("blk")
    side = left_factor.shape[1]
    low = side * LOW_PART // 32
    own = [condition(queries, left_factor, right_factor, *part) for part in ((0, low), (low, side - low))]
    way = on_line if layers == 4 and count == 4 else on_ring
    return way(own, store, candidates, layers)


def solution(mesh):
    placed = (
        P("layer", ("parts", "blk"), None),
        P("layer", ("parts", "blk"), None),
        P("layer", None, None),
        P("layer", None, None),
        P(("parts", "layer"), None),
    )
    return jax.shard_map(
        per_device,
        mesh=mesh,
        in_specs=placed,
        out_specs=P(("parts", "layer"), "blk"),
        check_vma=False,
    )
```

```python
import functools

import jax
import jax.numpy as jnp
from jax import lax
from jax.experimental import pallas as pl
from jax.experimental.pallas import tpu as pltpu
from jax.sharding import PartitionSpec as P

TILE = 128
GROUP = 32
LANES = 128
ROWS = 8
VMEM = 24 * 1024 * 1024


def two_parts(value):
    high = value.astype(jnp.bfloat16)
    low = (value - high.astype(jnp.float32)).astype(jnp.bfloat16)
    return high, low


def iota(shape, axis):
    return lax.broadcasted_iota(jnp.int32, shape, axis)


def dot(left, right):
    return jnp.dot(left, right, preferred_element_type=jnp.float32)


def ones_where(condition):
    return jnp.where(condition, 1.0, 0.0).astype(jnp.bfloat16)


def spread_left(left_factor, first, count):
    side = left_factor.shape[0]
    wide = ones_where(iota((side, side * ROWS), 1) // ROWS == iota((side, side * ROWS), 0))
    parts = [part[first : first + count] for part in two_parts(left_factor)]
    columns = dot(jnp.concatenate(parts, axis=0), wide).reshape(2, count, 1, side * ROWS)
    same = iota((1, ROWS, side * ROWS), 1) == iota((1, ROWS, side * ROWS), 2) % ROWS
    parts = [jnp.where(same, columns[part], 0.0).reshape(count * ROWS, side * ROWS) for part in range(2)]
    return jnp.concatenate([part.astype(jnp.bfloat16) for part in parts], axis=1)


def spread_right(right_factor):
    side = right_factor.shape[0]
    wide = ones_where(iota((side, 4 * side), 1) % side == iota((side, 4 * side), 0))
    same = iota((4 * side, 4 * side), 0) // side == iota((4 * side, 4 * side), 1) // side
    high, low = [
        jnp.where(same, jnp.concatenate([dot(part, wide)] * 4, axis=0), 0.0).astype(jnp.bfloat16)
        for part in two_parts(right_factor)
    ]
    return jnp.concatenate([high, low, high], axis=0)


def condition_kernel(first, count, queries_in, left_in, right_in, out, queries, left_factor, right_factor, arrived):
    copies = [
        pltpu.make_async_copy(source.at[0], target, arrived.at[place])
        for place, (source, target) in enumerate(
            [(left_in, left_factor), (right_in, right_factor), (queries_in, queries)]
        )
    ]
    for copy in copies:
        copy.start()
    side = left_factor.shape[0]
    pairs = side // 2
    copies[0].wait()
    copies[1].wait()
    left = spread_left(left_factor[...], first, count)
    right = spread_right(right_factor[...])
    low_half = iota((1, 1, LANES), 2) < side
    copies[2].wait()
    for block in range(queries.shape[0] // GROUP):
        rows = pl.ds(block * GROUP, GROUP)
        straight = jnp.stack(
            [queries[rows, pl.ds(pair * LANES, LANES)].astype(jnp.float32) for pair in range(pairs)]
        )
        swapped = pltpu.roll(straight, side, 2).reshape(pairs, GROUP // ROWS, ROWS, LANES)
        straight = straight.reshape(pairs, GROUP // ROWS, ROWS, LANES)
        columns = []
        for group in (0, 2):
            even = jnp.where(low_half, straight[:, group], swapped[:, group + 1])
            odd = jnp.where(low_half, swapped[:, group], straight[:, group + 1])
            columns.append(jnp.stack([even, odd], axis=1).reshape(side * ROWS, LANES))
        grid = jnp.concatenate(columns, axis=1).astype(jnp.bfloat16)
        halfway = dot(left, jnp.concatenate([grid, grid], axis=0))
        high, low = two_parts(halfway)
        result = dot(jnp.concatenate([high, high, low], axis=1), right)
        result = result.reshape(count // 2, 2, ROWS, 2 * LANES)
        groups = []
        for half in range(2):
            even = result[:, 0, :, half * LANES : (half + 1) * LANES]
            odd = result[:, 1, :, half * LANES : (half + 1) * LANES]
            groups.append(jnp.where(low_half, even, pltpu.roll(odd, side, 2)))
            groups.append(jnp.where(low_half, pltpu.roll(even, side, 2), odd))
        done = jnp.concatenate(groups, axis=1).astype(jnp.bfloat16)
        for pair in range(count // 2):
            out[rows, pl.ds(pair * LANES, LANES)] = done[pair]


def in_vmem(count):
    return [pl.BlockSpec(memory_space=pltpu.VMEM)] * count


def condition(queries, left_factor, right_factor, first, count):
    unused, block_rows, entries = queries.shape
    side = left_factor.shape[1]
    operands = [pltpu.with_memory_space_constraint(value, pltpu.HBM) for value in (queries, left_factor, right_factor)]
    return pl.pallas_call(
        functools.partial(condition_kernel, first, count),
        in_specs=[pl.BlockSpec(memory_space=pltpu.HBM)] * 3,
        out_specs=in_vmem(1)[0],
        out_shape=jax.ShapeDtypeStruct((block_rows, count * side), jnp.bfloat16),
        scratch_shapes=[
            pltpu.VMEM((block_rows, entries), jnp.bfloat16),
            pltpu.VMEM((side, side), jnp.float32),
            pltpu.VMEM((side, side), jnp.float32),
            pltpu.SemaphoreType.DMA((3,)),
        ],
        compiler_params=pltpu.CompilerParams(vmem_limit_bytes=VMEM),
        cost_estimate=pl.CostEstimate(
            flops=block_rows * entries * 4096, bytes_accessed=queries.size * 4, transcendentals=0
        ),
        name="condition",
    )(*operands)


STEP = 256
LOW_PART = 18
MASKS = (3, 1, 2, 0)


def score_rows(queries, store, place, first):
    return dot(store[0, place, pl.ds(first, queries.shape[1])], queries.T)


def own_kernel(queries, far_store, out, store, semaphores):
    def copy_of(step):
        place = pl.ds(pl.multiple_of(step * STEP, STEP), STEP)
        source = far_store.at[0, place, pl.ds(0, store.shape[2])]
        return pltpu.make_async_copy(source, store.at[0, place], semaphores.at[step])

    steps = store.shape[1] // STEP
    for step in range(steps):
        copy_of(step).start()
    padded = jnp.concatenate([jnp.zeros_like(queries)] * 3 + [queries[...]], axis=0)

    def one(step, carry):
        copy_of(step).wait()
        place = pl.ds(pl.multiple_of(step * STEP, STEP), STEP)
        out[place, :] = score_rows(padded, store, place, 0)
        return carry

    lax.fori_loop(0, steps, one, 0)


def score_cost(count, width, examples):
    return pl.CostEstimate(
        flops=2 * count * width * examples, bytes_accessed=examples * width * 2, transcendentals=0
    )


def score_own(queries, store):
    rows, entries = queries.shape
    examples = store.shape[1]
    return pl.pallas_call(
        own_kernel,
        in_specs=in_vmem(1) + [pl.BlockSpec(memory_space=pltpu.HBM)],
        out_specs=in_vmem(1)[0],
        out_shape=jax.ShapeDtypeStruct((examples, 4 * rows), jnp.float32),
        scratch_shapes=[
            pltpu.VMEM((1, examples, entries), store.dtype),
            pltpu.SemaphoreType.DMA((examples // STEP,)),
        ],
        compiler_params=pltpu.CompilerParams(vmem_limit_bytes=VMEM),
        cost_estimate=score_cost(rows, entries, examples),
        name="score_own",
    )(queries, pltpu.with_memory_space_constraint(store, pltpu.HBM))


def stacked(*blocks):
    return jnp.concatenate([block[...] for block in blocks], axis=0)


def low_kernel(near, far, last, store, own_low, out):
    queries = stacked(near, far, last)
    queries = jnp.concatenate([queries, jnp.zeros_like(near)], axis=0)
    out[...] = score_rows(queries, store, slice(None), 0) + own_low[...]


def score_low(near, far, last, store, own_low):
    rows, width = far.shape
    examples = store.shape[1]
    return pl.pallas_call(
        low_kernel,
        in_specs=in_vmem(5),
        out_specs=in_vmem(1)[0],
        out_shape=jax.ShapeDtypeStruct((examples, 4 * rows), jnp.float32),
        compiler_params=pltpu.CompilerParams(vmem_limit_bytes=VMEM),
        cost_estimate=score_cost(3 * rows, width, examples),
        name="score_low",
    )(near, far, last, store, own_low)


def high_kernel(first, near, far, last, own, store, low, *refs):
    outs, total = refs[:-1], refs[-1]
    rows = own.shape[0]
    total[...] = (score_rows(stacked(near, far, last, own), store, slice(None), first) + low[...]).T
    home = lax.bitwise_xor(lax.axis_index("blk"), lax.axis_index("layer"))
    for mask, out in zip(MASKS, outs):
        place = lax.bitwise_and(lax.bitwise_xor(home, mask) + 3, 3)
        out[...] = total[pl.ds(pl.multiple_of(place * rows, rows), rows), :].astype(out.dtype)


def score_high(near, far, last, own, store, low):
    rows, width = far.shape
    examples = store.shape[1]
    kinds = {0: jnp.float32, 1: jnp.bfloat16, 2: jnp.float32, 3: jnp.bfloat16}
    return pl.pallas_call(
        functools.partial(high_kernel, store.shape[2] - width),
        in_specs=in_vmem(6),
        out_specs=in_vmem(4),
        out_shape=[jax.ShapeDtypeStruct((rows, examples), kinds[mask]) for mask in MASKS],
        scratch_shapes=[pltpu.VMEM((4 * rows, examples), jnp.float32)],
        compiler_params=pltpu.CompilerParams(vmem_limit_bytes=VMEM),
        cost_estimate=score_cost(4 * rows, width, examples),
        name="score_high",
    )(near, far, last, own, store, low)


def add_kernel(kept, received, out):
    out[...] = (kept[...] + received[...].astype(jnp.float32)).astype(out.dtype)


def add(kept, received):
    return pl.pallas_call(
        add_kernel,
        in_specs=in_vmem(2),
        out_specs=in_vmem(1)[0],
        out_shape=jax.ShapeDtypeStruct(received.shape, received.dtype),
        compiler_params=pltpu.CompilerParams(vmem_limit_bytes=VMEM),
        name="add",
    )(kept, received)


def write_rows(total, layers, listed, out):
    scaled = total / jnp.sqrt(jnp.float32(layers))
    tiles_here = out.shape[1] // TILE
    first = lax.axis_index("blk") * tiles_here
    for tile in range(tiles_here):
        hit = jnp.max(jnp.where(listed == first + tile, 1.0, 0.0), axis=1, keepdims=True)
        columns = slice(tile * TILE, (tile + 1) * TILE)
        out[:, columns] = jnp.where(hit > 0.0, scaled[:, columns], 0.0).astype(out.dtype)


def finish_kernel(layers, candidates, *refs):
    parts, out = refs[:-1], refs[-1]
    total = parts[0][...].astype(jnp.float32)
    for part in parts[1:]:
        total = total + part[...].astype(jnp.float32)
    write_rows(total, layers, candidates[...], out)


def finish(parts, candidates, layers):
    return pl.pallas_call(
        functools.partial(finish_kernel, layers),
        in_specs=in_vmem(1 + len(parts)),
        out_specs=in_vmem(1)[0],
        out_shape=jax.ShapeDtypeStruct(parts[0].shape, jnp.bfloat16),
        compiler_params=pltpu.CompilerParams(vmem_limit_bytes=VMEM),
        name="finish",
    )(candidates, *parts)


def permuted(value, axis, target_of):
    count = lax.axis_size(axis)
    return lax.ppermute(value, axis, [(source, target_of(source) % count) for source in range(count)])


def swapped(value, axis, mask):
    return permuted(value, axis, lambda source: source ^ mask)


def on_line(own, store, candidates, layers):
    far = [swapped(half, "blk", 2) for half in own]
    near = [swapped(half, "blk", 1) for half in own]
    own_low = score_own(own[0], store)
    near[0], far[0], own_low = lax.optimization_barrier((near[0], far[0], own_low))
    near[1], far[1] = lax.optimization_barrier((near[1], far[1]))
    last = [swapped(half, "blk", 1) for half in far]
    low_scores = score_low(near[0], far[0], last[0], store, own_low)
    across, beside, kept, home = score_high(near[1], far[1], last[1], own[1], store, low_scores)
    across = swapped(add(kept, swapped(across, "layer", 1)), "layer", 2)
    return finish([home, swapped(beside, "layer", 1), across], candidates, layers)


def on_ring(own, store, candidates, layers):
    count = lax.axis_size("blk")
    rows = own[0].shape[0]
    moving = jnp.concatenate(own, axis=1)

    def scores():
        return lax.dot_general(moving, store[0], (((1,), (1,)), ((), ())), preferred_element_type=jnp.float32)

    slots = [scores()]
    for _ in range(count - 1):
        moving = permuted(moving, "blk", lambda source: source + 1)
        slots.append(scores())
    turns = lax.rem(lax.axis_index("blk") - jnp.arange(count) + count, count)
    total = jnp.stack(slots)[turns].reshape(layers, count * rows // layers, store.shape[1])
    parts = lax.all_to_all(total.astype(jnp.bfloat16), "layer", 0, 0)
    return finish([parts[layer] for layer in range(layers)], candidates, layers)


def per_device(queries, store, left_factor, right_factor, candidates):
    layers, count = lax.axis_size("layer"), lax.axis_size("blk")
    side = left_factor.shape[1]
    low = side * LOW_PART // 32
    own = [condition(queries, left_factor, right_factor, *part) for part in ((0, low), (low, side - low))]
    way = on_line if layers == 4 and count == 4 else on_ring
    return way(own, store, candidates, layers)


def solution(mesh):
    placed = (
        P("layer", ("parts", "blk"), None),
        P("layer", ("parts", "blk"), None),
        P("layer", None, None),
        P("layer", None, None),
        P(("parts", "layer"), None),
    )
    return jax.shard_map(
        per_device,
        mesh=mesh,
        in_specs=placed,
        out_specs=P(("parts", "layer"), "blk"),
        check_vma=False,
    )
```

```python
import functools

import jax
import jax.numpy as jnp
from jax import lax
from jax.experimental import pallas as pl
from jax.experimental.pallas import tpu as pltpu
from jax.sharding import PartitionSpec as P

TILE = 128
GROUP = 32
LANES = 128
ROWS = 8
VMEM = 24 * 1024 * 1024


def two_parts(value):
    high = value.astype(jnp.bfloat16)
    low = (value - high.astype(jnp.float32)).astype(jnp.bfloat16)
    return high, low


def iota(shape, axis):
    return lax.broadcasted_iota(jnp.int32, shape, axis)


def dot(left, right):
    return jnp.dot(left, right, preferred_element_type=jnp.float32)


def ones_where(condition):
    return jnp.where(condition, 1.0, 0.0).astype(jnp.bfloat16)


def spread_left(left_factor, first, count):
    side = left_factor.shape[0]
    wide = ones_where(iota((side, side * ROWS), 1) // ROWS == iota((side, side * ROWS), 0))
    parts = [part[first : first + count] for part in two_parts(left_factor)]
    columns = dot(jnp.concatenate(parts, axis=0), wide).reshape(2, count, 1, side * ROWS)
    same = iota((1, ROWS, side * ROWS), 1) == iota((1, ROWS, side * ROWS), 2) % ROWS
    parts = [jnp.where(same, columns[part], 0.0).reshape(count * ROWS, side * ROWS) for part in range(2)]
    return jnp.concatenate([part.astype(jnp.bfloat16) for part in parts], axis=1)


def spread_right(right_factor):
    side = right_factor.shape[0]
    wide = ones_where(iota((side, 4 * side), 1) % side == iota((side, 4 * side), 0))
    same = iota((4 * side, 4 * side), 0) // side == iota((4 * side, 4 * side), 1) // side
    high, low = [
        jnp.where(same, jnp.concatenate([dot(part, wide)] * 4, axis=0), 0.0).astype(jnp.bfloat16)
        for part in two_parts(right_factor)
    ]
    return jnp.concatenate([high, low, high], axis=0)


def condition_kernel(first, count, queries_in, left_in, right_in, out, queries, left_factor, right_factor, arrived):
    copies = [
        pltpu.make_async_copy(source.at[0], target, arrived.at[place])
        for place, (source, target) in enumerate(
            [(left_in, left_factor), (right_in, right_factor), (queries_in, queries)]
        )
    ]
    for copy in copies:
        copy.start()
    side = left_factor.shape[0]
    pairs = side // 2
    copies[0].wait()
    copies[1].wait()
    left = spread_left(left_factor[...], first, count)
    right = spread_right(right_factor[...])
    low_half = iota((1, 1, LANES), 2) < side
    copies[2].wait()
    for block in range(queries.shape[0] // GROUP):
        rows = pl.ds(block * GROUP, GROUP)
        straight = jnp.stack(
            [queries[rows, pl.ds(pair * LANES, LANES)].astype(jnp.float32) for pair in range(pairs)]
        )
        swapped = pltpu.roll(straight, side, 2).reshape(pairs, GROUP // ROWS, ROWS, LANES)
        straight = straight.reshape(pairs, GROUP // ROWS, ROWS, LANES)
        columns = []
        for group in (0, 2):
            even = jnp.where(low_half, straight[:, group], swapped[:, group + 1])
            odd = jnp.where(low_half, swapped[:, group], straight[:, group + 1])
            columns.append(jnp.stack([even, odd], axis=1).reshape(side * ROWS, LANES))
        grid = jnp.concatenate(columns, axis=1).astype(jnp.bfloat16)
        halfway = dot(left, jnp.concatenate([grid, grid], axis=0))
        high, low = two_parts(halfway)
        result = dot(jnp.concatenate([high, high, low], axis=1), right)
        result = result.reshape(count // 2, 2, ROWS, 2 * LANES)
        groups = []
        for half in range(2):
            even = result[:, 0, :, half * LANES : (half + 1) * LANES]
            odd = result[:, 1, :, half * LANES : (half + 1) * LANES]
            groups.append(jnp.where(low_half, even, pltpu.roll(odd, side, 2)))
            groups.append(jnp.where(low_half, pltpu.roll(even, side, 2), odd))
        done = jnp.concatenate(groups, axis=1).astype(jnp.bfloat16)
        for pair in range(count // 2):
            out[rows, pl.ds(pair * LANES, LANES)] = done[pair]


def in_vmem(count):
    return [pl.BlockSpec(memory_space=pltpu.VMEM)] * count


def condition(queries, left_factor, right_factor, first, count):
    unused, block_rows, entries = queries.shape
    side = left_factor.shape[1]
    operands = [pltpu.with_memory_space_constraint(value, pltpu.HBM) for value in (queries, left_factor, right_factor)]
    return pl.pallas_call(
        functools.partial(condition_kernel, first, count),
        in_specs=[pl.BlockSpec(memory_space=pltpu.HBM)] * 3,
        out_specs=in_vmem(1)[0],
        out_shape=jax.ShapeDtypeStruct((block_rows, count * side), jnp.bfloat16),
        scratch_shapes=[
            pltpu.VMEM((block_rows, entries), jnp.bfloat16),
            pltpu.VMEM((side, side), jnp.float32),
            pltpu.VMEM((side, side), jnp.float32),
            pltpu.SemaphoreType.DMA((3,)),
        ],
        compiler_params=pltpu.CompilerParams(vmem_limit_bytes=VMEM),
        cost_estimate=pl.CostEstimate(
            flops=block_rows * entries * 4096, bytes_accessed=queries.size * 4, transcendentals=0
        ),
        name="condition",
    )(*operands)


STEP = 256
LOW_PART = 20
MASKS = (3, 1, 2, 0)


def score_rows(queries, store, place, first):
    return dot(store[0, place, pl.ds(first, queries.shape[1])], queries.T)


def own_kernel(queries, far_store, out, store, semaphores):
    def copy_of(step):
        place = pl.ds(pl.multiple_of(step * STEP, STEP), STEP)
        source = far_store.at[0, place, pl.ds(0, store.shape[2])]
        return pltpu.make_async_copy(source, store.at[0, place], semaphores.at[step])

    steps = store.shape[1] // STEP
    for step in range(steps):
        copy_of(step).start()
    padded = jnp.concatenate([jnp.zeros_like(queries)] * 3 + [queries[...]], axis=0)

    def one(step, carry):
        copy_of(step).wait()
        place = pl.ds(pl.multiple_of(step * STEP, STEP), STEP)
        out[place, :] = score_rows(padded, store, place, 0)
        return carry

    lax.fori_loop(0, steps, one, 0)


def score_cost(count, width, examples):
    return pl.CostEstimate(
        flops=2 * count * width * examples, bytes_accessed=examples * width * 2, transcendentals=0
    )


def score_own(queries, store):
    rows, entries = queries.shape
    examples = store.shape[1]
    return pl.pallas_call(
        own_kernel,
        in_specs=in_vmem(1) + [pl.BlockSpec(memory_space=pltpu.HBM)],
        out_specs=in_vmem(1)[0],
        out_shape=jax.ShapeDtypeStruct((examples, 4 * rows), jnp.float32),
        scratch_shapes=[
            pltpu.VMEM((1, examples, entries), store.dtype),
            pltpu.SemaphoreType.DMA((examples // STEP,)),
        ],
        compiler_params=pltpu.CompilerParams(vmem_limit_bytes=VMEM),
        cost_estimate=score_cost(rows, entries, examples),
        name="score_own",
    )(queries, pltpu.with_memory_space_constraint(store, pltpu.HBM))


def stacked(*blocks):
    return jnp.concatenate([block[...] for block in blocks], axis=0)


def low_kernel(near, far, last, store, own_low, out):
    queries = stacked(near, far, last)
    queries = jnp.concatenate([queries, jnp.zeros_like(near)], axis=0)
    out[...] = score_rows(queries, store, slice(None), 0) + own_low[...]


def score_low(near, far, last, store, own_low):
    rows, width = far.shape
    examples = store.shape[1]
    return pl.pallas_call(
        low_kernel,
        in_specs=in_vmem(5),
        out_specs=in_vmem(1)[0],
        out_shape=jax.ShapeDtypeStruct((examples, 4 * rows), jnp.float32),
        compiler_params=pltpu.CompilerParams(vmem_limit_bytes=VMEM),
        cost_estimate=score_cost(3 * rows, width, examples),
        name="score_low",
    )(near, far, last, store, own_low)


def high_kernel(first, near, far, last, own, store, low, *refs):
    outs, total = refs[:-1], refs[-1]
    rows = own.shape[0]
    total[...] = (score_rows(stacked(near, far, last, own), store, slice(None), first) + low[...]).T
    home = lax.bitwise_xor(lax.axis_index("blk"), lax.axis_index("layer"))
    for mask, out in zip(MASKS, outs):
        place = lax.bitwise_and(lax.bitwise_xor(home, mask) + 3, 3)
        out[...] = total[pl.ds(pl.multiple_of(place * rows, rows), rows), :].astype(out.dtype)


def score_high(near, far, last, own, store, low):
    rows, width = far.shape
    examples = store.shape[1]
    kinds = {0: jnp.float32, 1: jnp.bfloat16, 2: jnp.float32, 3: jnp.bfloat16}
    return pl.pallas_call(
        functools.partial(high_kernel, store.shape[2] - width),
        in_specs=in_vmem(6),
        out_specs=in_vmem(4),
        out_shape=[jax.ShapeDtypeStruct((rows, examples), kinds[mask]) for mask in MASKS],
        scratch_shapes=[pltpu.VMEM((4 * rows, examples), jnp.float32)],
        compiler_params=pltpu.CompilerParams(vmem_limit_bytes=VMEM),
        cost_estimate=score_cost(4 * rows, width, examples),
        name="score_high",
    )(near, far, last, own, store, low)


def add_kernel(kept, received, out):
    out[...] = (kept[...] + received[...].astype(jnp.float32)).astype(out.dtype)


def add(kept, received):
    return pl.pallas_call(
        add_kernel,
        in_specs=in_vmem(2),
        out_specs=in_vmem(1)[0],
        out_shape=jax.ShapeDtypeStruct(received.shape, received.dtype),
        compiler_params=pltpu.CompilerParams(vmem_limit_bytes=VMEM),
        name="add",
    )(kept, received)


def write_rows(total, layers, listed, out):
    scaled = total / jnp.sqrt(jnp.float32(layers))
    tiles_here = out.shape[1] // TILE
    first = lax.axis_index("blk") * tiles_here
    for tile in range(tiles_here):
        hit = jnp.max(jnp.where(listed == first + tile, 1.0, 0.0), axis=1, keepdims=True)
        columns = slice(tile * TILE, (tile + 1) * TILE)
        out[:, columns] = jnp.where(hit > 0.0, scaled[:, columns], 0.0).astype(out.dtype)


def finish_kernel(layers, candidates, *refs):
    parts, out = refs[:-1], refs[-1]
    total = parts[0][...].astype(jnp.float32)
    for part in parts[1:]:
        total = total + part[...].astype(jnp.float32)
    write_rows(total, layers, candidates[...], out)


def finish(parts, candidates, layers):
    return pl.pallas_call(
        functools.partial(finish_kernel, layers),
        in_specs=in_vmem(1 + len(parts)),
        out_specs=in_vmem(1)[0],
        out_shape=jax.ShapeDtypeStruct(parts[0].shape, jnp.bfloat16),
        compiler_params=pltpu.CompilerParams(vmem_limit_bytes=VMEM),
        name="finish",
    )(candidates, *parts)


def permuted(value, axis, target_of):
    count = lax.axis_size(axis)
    return lax.ppermute(value, axis, [(source, target_of(source) % count) for source in range(count)])


def swapped(value, axis, mask):
    return permuted(value, axis, lambda source: source ^ mask)


def on_line(own, store, candidates, layers):
    far = [swapped(half, "blk", 2) for half in own]
    near = [swapped(half, "blk", 1) for half in own]
    own_low = score_own(own[0], store)
    near[0], far[0], own_low = lax.optimization_barrier((near[0], far[0], own_low))
    near[1], far[1] = lax.optimization_barrier((near[1], far[1]))
    last = [swapped(half, "blk", 1) for half in far]
    low_scores = score_low(near[0], far[0], last[0], store, own_low)
    across, beside, kept, home = score_high(near[1], far[1], last[1], own[1], store, low_scores)
    across = swapped(add(kept, swapped(across, "layer", 1)), "layer", 2)
    return finish([home, swapped(beside, "layer", 1), across], candidates, layers)


def on_ring(own, store, candidates, layers):
    count = lax.axis_size("blk")
    rows = own[0].shape[0]
    moving = jnp.concatenate(own, axis=1)

    def scores():
        return lax.dot_general(moving, store[0], (((1,), (1,)), ((), ())), preferred_element_type=jnp.float32)

    slots = [scores()]
    for _ in range(count - 1):
        moving = permuted(moving, "blk", lambda source: source + 1)
        slots.append(scores())
    turns = lax.rem(lax.axis_index("blk") - jnp.arange(count) + count, count)
    total = jnp.stack(slots)[turns].reshape(layers, count * rows // layers, store.shape[1])
    parts = lax.all_to_all(total.astype(jnp.bfloat16), "layer", 0, 0)
    return finish([parts[layer] for layer in range(layers)], candidates, layers)


def per_device(queries, store, left_factor, right_factor, candidates):
    layers, count = lax.axis_size("layer"), lax.axis_size("blk")
    side = left_factor.shape[1]
    low = side * LOW_PART // 32
    own = [condition(queries, left_factor, right_factor, *part) for part in ((0, low), (low, side - low))]
    way = on_line if layers == 4 and count == 4 else on_ring
    return way(own, store, candidates, layers)


def solution(mesh):
    placed = (
        P("layer", ("parts", "blk"), None),
        P("layer", ("parts", "blk"), None),
        P("layer", None, None),
        P("layer", None, None),
        P(("parts", "layer"), None),
    )
    return jax.shard_map(
        per_device,
        mesh=mesh,
        in_specs=placed,
        out_specs=P(("parts", "layer"), "blk"),
        check_vma=False,
    )
```

```python
import functools

import jax
import jax.numpy as jnp
from jax import lax
from jax.experimental import pallas as pl
from jax.experimental.pallas import tpu as pltpu
from jax.sharding import PartitionSpec as P

TILE = 128
GROUP = 32
LANES = 128
ROWS = 8
VMEM = 24 * 1024 * 1024


def two_parts(value):
    high = value.astype(jnp.bfloat16)
    low = (value - high.astype(jnp.float32)).astype(jnp.bfloat16)
    return high, low


def iota(shape, axis):
    return lax.broadcasted_iota(jnp.int32, shape, axis)


def dot(left, right):
    return jnp.dot(left, right, preferred_element_type=jnp.float32)


def ones_where(condition):
    return jnp.where(condition, 1.0, 0.0).astype(jnp.bfloat16)


def spread_left(left_factor, first, count):
    side = left_factor.shape[0]
    wide = ones_where(iota((side, side * ROWS), 1) // ROWS == iota((side, side * ROWS), 0))
    parts = [part[first : first + count] for part in two_parts(left_factor)]
    columns = dot(jnp.concatenate(parts, axis=0), wide).reshape(2, count, 1, side * ROWS)
    same = iota((1, ROWS, side * ROWS), 1) == iota((1, ROWS, side * ROWS), 2) % ROWS
    parts = [jnp.where(same, columns[part], 0.0).reshape(count * ROWS, side * ROWS) for part in range(2)]
    return jnp.concatenate([part.astype(jnp.bfloat16) for part in parts], axis=1)


def spread_right(right_factor):
    side = right_factor.shape[0]
    wide = ones_where(iota((side, 4 * side), 1) % side == iota((side, 4 * side), 0))
    same = iota((4 * side, 4 * side), 0) // side == iota((4 * side, 4 * side), 1) // side
    high, low = [
        jnp.where(same, jnp.concatenate([dot(part, wide)] * 4, axis=0), 0.0).astype(jnp.bfloat16)
        for part in two_parts(right_factor)
    ]
    return jnp.concatenate([high, low, high], axis=0)


def condition_kernel(first, count, queries_in, left_in, right_in, out, queries, left_factor, right_factor, arrived):
    copies = [
        pltpu.make_async_copy(source.at[0], target, arrived.at[place])
        for place, (source, target) in enumerate(
            [(left_in, left_factor), (right_in, right_factor), (queries_in, queries)]
        )
    ]
    for copy in copies:
        copy.start()
    side = left_factor.shape[0]
    pairs = side // 2
    copies[0].wait()
    copies[1].wait()
    left = spread_left(left_factor[...], first, count)
    right = spread_right(right_factor[...])
    low_half = iota((1, 1, LANES), 2) < side
    copies[2].wait()
    for block in range(queries.shape[0] // GROUP):
        rows = pl.ds(block * GROUP, GROUP)
        straight = jnp.stack(
            [queries[rows, pl.ds(pair * LANES, LANES)].astype(jnp.float32) for pair in range(pairs)]
        )
        swapped = pltpu.roll(straight, side, 2).reshape(pairs, GROUP // ROWS, ROWS, LANES)
        straight = straight.reshape(pairs, GROUP // ROWS, ROWS, LANES)
        columns = []
        for group in (0, 2):
            even = jnp.where(low_half, straight[:, group], swapped[:, group + 1])
            odd = jnp.where(low_half, swapped[:, group], straight[:, group + 1])
            columns.append(jnp.stack([even, odd], axis=1).reshape(side * ROWS, LANES))
        grid = jnp.concatenate(columns, axis=1).astype(jnp.bfloat16)
        halfway = dot(left, jnp.concatenate([grid, grid], axis=0))
        high, low = two_parts(halfway)
        result = dot(jnp.concatenate([high, high, low], axis=1), right)
        result = result.reshape(count // 2, 2, ROWS, 2 * LANES)
        groups = []
        for half in range(2):
            even = result[:, 0, :, half * LANES : (half + 1) * LANES]
            odd = result[:, 1, :, half * LANES : (half + 1) * LANES]
            groups.append(jnp.where(low_half, even, pltpu.roll(odd, side, 2)))
            groups.append(jnp.where(low_half, pltpu.roll(even, side, 2), odd))
        done = jnp.concatenate(groups, axis=1).astype(jnp.bfloat16)
        for pair in range(count // 2):
            out[rows, pl.ds(pair * LANES, LANES)] = done[pair]


def in_vmem(count):
    return [pl.BlockSpec(memory_space=pltpu.VMEM)] * count


def condition(queries, left_factor, right_factor, first, count):
    unused, block_rows, entries = queries.shape
    side = left_factor.shape[1]
    operands = [pltpu.with_memory_space_constraint(value, pltpu.HBM) for value in (queries, left_factor, right_factor)]
    return pl.pallas_call(
        functools.partial(condition_kernel, first, count),
        in_specs=[pl.BlockSpec(memory_space=pltpu.HBM)] * 3,
        out_specs=in_vmem(1)[0],
        out_shape=jax.ShapeDtypeStruct((block_rows, count * side), jnp.bfloat16),
        scratch_shapes=[
            pltpu.VMEM((block_rows, entries), jnp.bfloat16),
            pltpu.VMEM((side, side), jnp.float32),
            pltpu.VMEM((side, side), jnp.float32),
            pltpu.SemaphoreType.DMA((3,)),
        ],
        compiler_params=pltpu.CompilerParams(vmem_limit_bytes=VMEM),
        cost_estimate=pl.CostEstimate(
            flops=block_rows * entries * 4096, bytes_accessed=queries.size * 4, transcendentals=0
        ),
        name="condition",
    )(*operands)


STEP = 256
LOW_PART = 20
MASKS = (3, 1, 2, 0)


def score_rows(queries, store, place, first):
    return dot(store[0, place, pl.ds(first, queries.shape[1])], queries.T)


def own_kernel(queries, far_store, out, store, semaphores):
    def copy_of(step):
        place = pl.ds(pl.multiple_of(step * STEP, STEP), STEP)
        source = far_store.at[0, place, pl.ds(0, store.shape[2])]
        return pltpu.make_async_copy(source, store.at[0, place], semaphores.at[step])

    steps = store.shape[1] // STEP
    for step in range(steps):
        copy_of(step).start()
    padded = jnp.concatenate([jnp.zeros_like(queries)] * 3 + [queries[...]], axis=0)

    def one(step, carry):
        copy_of(step).wait()
        place = pl.ds(pl.multiple_of(step * STEP, STEP), STEP)
        out[place, :] = score_rows(padded, store, place, 0)
        return carry

    lax.fori_loop(0, steps, one, 0)


def score_cost(count, width, examples):
    return pl.CostEstimate(
        flops=2 * count * width * examples, bytes_accessed=examples * width * 2, transcendentals=0
    )


def score_own(queries, store):
    rows, entries = queries.shape
    examples = store.shape[1]
    return pl.pallas_call(
        own_kernel,
        in_specs=in_vmem(1) + [pl.BlockSpec(memory_space=pltpu.HBM)],
        out_specs=in_vmem(1)[0],
        out_shape=jax.ShapeDtypeStruct((examples, 4 * rows), jnp.float32),
        scratch_shapes=[
            pltpu.VMEM((1, examples, entries), store.dtype),
            pltpu.SemaphoreType.DMA((examples // STEP,)),
        ],
        compiler_params=pltpu.CompilerParams(vmem_limit_bytes=VMEM),
        cost_estimate=score_cost(rows, entries, examples),
        name="score_own",
    )(queries, pltpu.with_memory_space_constraint(store, pltpu.HBM))


def stacked(*blocks):
    return jnp.concatenate([block[...] for block in blocks], axis=0)


def low_kernel(near, far, last, store, own_low, out):
    queries = stacked(near, far, last)
    queries = jnp.concatenate([queries, jnp.zeros_like(near)], axis=0)
    out[...] = score_rows(queries, store, slice(None), 0) + own_low[...]


def score_low(near, far, last, store, own_low):
    rows, width = far.shape
    examples = store.shape[1]
    return pl.pallas_call(
        low_kernel,
        in_specs=in_vmem(5),
        out_specs=in_vmem(1)[0],
        out_shape=jax.ShapeDtypeStruct((examples, 4 * rows), jnp.float32),
        compiler_params=pltpu.CompilerParams(vmem_limit_bytes=VMEM),
        cost_estimate=score_cost(3 * rows, width, examples),
        name="score_low",
    )(near, far, last, store, own_low)


def high_kernel(first, near, far, last, own, store, low, *refs):
    outs, total = refs[:-1], refs[-1]
    rows = own.shape[0]
    total[...] = (score_rows(stacked(near, far, last, own), store, slice(None), first) + low[...]).T
    home = lax.bitwise_xor(lax.axis_index("blk"), lax.axis_index("layer"))
    for mask, out in zip(MASKS, outs):
        place = lax.bitwise_and(lax.bitwise_xor(home, mask) + 3, 3)
        out[...] = total[pl.ds(pl.multiple_of(place * rows, rows), rows), :].astype(out.dtype)


def score_high(near, far, last, own, store, low):
    rows, width = far.shape
    examples = store.shape[1]
    kinds = {0: jnp.float32, 1: jnp.bfloat16, 2: jnp.float32, 3: jnp.bfloat16}
    return pl.pallas_call(
        functools.partial(high_kernel, store.shape[2] - width),
        in_specs=in_vmem(6),
        out_specs=in_vmem(4),
        out_shape=[jax.ShapeDtypeStruct((rows, examples), kinds[mask]) for mask in MASKS],
        scratch_shapes=[pltpu.VMEM((4 * rows, examples), jnp.float32)],
        compiler_params=pltpu.CompilerParams(vmem_limit_bytes=VMEM),
        cost_estimate=score_cost(4 * rows, width, examples),
        name="score_high",
    )(near, far, last, own, store, low)


def add_kernel(kept, received, out):
    out[...] = (kept[...] + received[...].astype(jnp.float32)).astype(out.dtype)


def add(kept, received):
    return pl.pallas_call(
        add_kernel,
        in_specs=in_vmem(2),
        out_specs=in_vmem(1)[0],
        out_shape=jax.ShapeDtypeStruct(received.shape, received.dtype),
        compiler_params=pltpu.CompilerParams(vmem_limit_bytes=VMEM),
        name="add",
    )(kept, received)


def write_rows(total, layers, listed, out):
    scaled = total / jnp.sqrt(jnp.float32(layers))
    tiles_here = out.shape[1] // TILE
    first = lax.axis_index("blk") * tiles_here
    for tile in range(tiles_here):
        hit = jnp.max(jnp.where(listed == first + tile, 1.0, 0.0), axis=1, keepdims=True)
        columns = slice(tile * TILE, (tile + 1) * TILE)
        out[:, columns] = jnp.where(hit > 0.0, scaled[:, columns], 0.0).astype(out.dtype)


def finish_kernel(layers, candidates, *refs):
    parts, out = refs[:-1], refs[-1]
    total = parts[0][...].astype(jnp.float32)
    for part in parts[1:]:
        total = total + part[...].astype(jnp.float32)
    write_rows(total, layers, candidates[...], out)


def finish(parts, candidates, layers):
    return pl.pallas_call(
        functools.partial(finish_kernel, layers),
        in_specs=in_vmem(1 + len(parts)),
        out_specs=in_vmem(1)[0],
        out_shape=jax.ShapeDtypeStruct(parts[0].shape, jnp.bfloat16),
        compiler_params=pltpu.CompilerParams(vmem_limit_bytes=VMEM),
        name="finish",
    )(candidates, *parts)


def permuted(value, axis, target_of):
    count = lax.axis_size(axis)
    return lax.ppermute(value, axis, [(source, target_of(source) % count) for source in range(count)])


def swapped(value, axis, mask):
    return permuted(value, axis, lambda source: source ^ mask)


def on_line(own, store, candidates, layers):
    far = [swapped(half, "blk", 2) for half in own]
    near = [swapped(half, "blk", 1) for half in own]
    own_first, own[1] = lax.optimization_barrier((own[0], own[1]))
    own_low = score_own(own_first, store)
    near[0], far[0], own_low = lax.optimization_barrier((near[0], far[0], own_low))
    near[1], far[1] = lax.optimization_barrier((near[1], far[1]))
    last = [swapped(half, "blk", 1) for half in far]
    low_scores = score_low(near[0], far[0], last[0], store, own_low)
    across, beside, kept, home = score_high(near[1], far[1], last[1], own[1], store, low_scores)
    across = swapped(add(kept, swapped(across, "layer", 1)), "layer", 2)
    return finish([home, swapped(beside, "layer", 1), across], candidates, layers)


def on_ring(own, store, candidates, layers):
    count = lax.axis_size("blk")
    rows = own[0].shape[0]
    moving = jnp.concatenate(own, axis=1)

    def scores():
        return lax.dot_general(moving, store[0], (((1,), (1,)), ((), ())), preferred_element_type=jnp.float32)

    slots = [scores()]
    for _ in range(count - 1):
        moving = permuted(moving, "blk", lambda source: source + 1)
        slots.append(scores())
    turns = lax.rem(lax.axis_index("blk") - jnp.arange(count) + count, count)
    total = jnp.stack(slots)[turns].reshape(layers, count * rows // layers, store.shape[1])
    parts = lax.all_to_all(total.astype(jnp.bfloat16), "layer", 0, 0)
    return finish([parts[layer] for layer in range(layers)], candidates, layers)


def per_device(queries, store, left_factor, right_factor, candidates):
    layers, count = lax.axis_size("layer"), lax.axis_size("blk")
    side = left_factor.shape[1]
    low = side * LOW_PART // 32
    own = [condition(queries, left_factor, right_factor, *part) for part in ((0, low), (low, side - low))]
    way = on_line if layers == 4 and count == 4 else on_ring
    return way(own, store, candidates, layers)


def solution(mesh):
    placed = (
        P("layer", ("parts", "blk"), None),
        P("layer", ("parts", "blk"), None),
        P("layer", None, None),
        P("layer", None, None),
        P(("parts", "layer"), None),
    )
    return jax.shard_map(
        per_device,
        mesh=mesh,
        in_specs=placed,
        out_specs=P(("parts", "layer"), "blk"),
        check_vma=False,
    )
```

```python
import functools

import jax
import jax.numpy as jnp
from jax import lax
from jax.experimental import pallas as pl
from jax.experimental.pallas import tpu as pltpu
from jax.sharding import PartitionSpec as P

TILE = 128
GROUP = 32
LANES = 128
ROWS = 8
VMEM = 24 * 1024 * 1024


def two_parts(value):
    high = value.astype(jnp.bfloat16)
    low = (value - high.astype(jnp.float32)).astype(jnp.bfloat16)
    return high, low


def iota(shape, axis):
    return lax.broadcasted_iota(jnp.int32, shape, axis)


def dot(left, right):
    return jnp.dot(left, right, preferred_element_type=jnp.float32)


def ones_where(condition):
    return jnp.where(condition, 1.0, 0.0).astype(jnp.bfloat16)


def spread_left(left_factor, first, count):
    side = left_factor.shape[0]
    wide = ones_where(iota((side, side * ROWS), 1) // ROWS == iota((side, side * ROWS), 0))
    parts = [part[first : first + count] for part in two_parts(left_factor)]
    columns = dot(jnp.concatenate(parts, axis=0), wide).reshape(2, count, 1, side * ROWS)
    same = iota((1, ROWS, side * ROWS), 1) == iota((1, ROWS, side * ROWS), 2) % ROWS
    parts = [jnp.where(same, columns[part], 0.0).reshape(count * ROWS, side * ROWS) for part in range(2)]
    return jnp.concatenate([part.astype(jnp.bfloat16) for part in parts], axis=1)


def spread_right(right_factor):
    side = right_factor.shape[0]
    wide = ones_where(iota((side, 4 * side), 1) % side == iota((side, 4 * side), 0))
    same = iota((4 * side, 4 * side), 0) // side == iota((4 * side, 4 * side), 1) // side
    high, low = [
        jnp.where(same, jnp.concatenate([dot(part, wide)] * 4, axis=0), 0.0).astype(jnp.bfloat16)
        for part in two_parts(right_factor)
    ]
    return jnp.concatenate([high, low, high], axis=0)


def condition_kernel(first, count, queries_in, left_in, right_in, out, queries, left_factor, right_factor, arrived):
    copies = [
        pltpu.make_async_copy(source.at[0], target, arrived.at[place])
        for place, (source, target) in enumerate(
            [(queries_in, queries), (left_in, left_factor), (right_in, right_factor)]
        )
    ]
    for copy in copies:
        copy.start()
    side = left_factor.shape[0]
    pairs = side // 2
    copies[1].wait()
    copies[2].wait()
    left = spread_left(left_factor[...], first, count)
    right = spread_right(right_factor[...])
    low_half = iota((1, 1, LANES), 2) < side
    copies[0].wait()
    for block in range(queries.shape[0] // GROUP):
        rows = pl.ds(block * GROUP, GROUP)
        straight = jnp.stack(
            [queries[rows, pl.ds(pair * LANES, LANES)].astype(jnp.float32) for pair in range(pairs)]
        )
        swapped = pltpu.roll(straight, side, 2).reshape(pairs, GROUP // ROWS, ROWS, LANES)
        straight = straight.reshape(pairs, GROUP // ROWS, ROWS, LANES)
        columns = []
        for group in (0, 2):
            even = jnp.where(low_half, straight[:, group], swapped[:, group + 1])
            odd = jnp.where(low_half, swapped[:, group], straight[:, group + 1])
            columns.append(jnp.stack([even, odd], axis=1).reshape(side * ROWS, LANES))
        grid = jnp.concatenate(columns, axis=1).astype(jnp.bfloat16)
        halfway = dot(left, jnp.concatenate([grid, grid], axis=0))
        high, low = two_parts(halfway)
        result = dot(jnp.concatenate([high, high, low], axis=1), right)
        result = result.reshape(count // 2, 2, ROWS, 2 * LANES)
        groups = []
        for half in range(2):
            even = result[:, 0, :, half * LANES : (half + 1) * LANES]
            odd = result[:, 1, :, half * LANES : (half + 1) * LANES]
            groups.append(jnp.where(low_half, even, pltpu.roll(odd, side, 2)))
            groups.append(jnp.where(low_half, pltpu.roll(even, side, 2), odd))
        done = jnp.concatenate(groups, axis=1).astype(jnp.bfloat16)
        for pair in range(count // 2):
            out[rows, pl.ds(pair * LANES, LANES)] = done[pair]


def in_vmem(count):
    return [pl.BlockSpec(memory_space=pltpu.VMEM)] * count


def condition(queries, left_factor, right_factor, first, count):
    unused, block_rows, entries = queries.shape
    side = left_factor.shape[1]
    operands = [pltpu.with_memory_space_constraint(value, pltpu.HBM) for value in (queries, left_factor, right_factor)]
    return pl.pallas_call(
        functools.partial(condition_kernel, first, count),
        in_specs=[pl.BlockSpec(memory_space=pltpu.HBM)] * 3,
        out_specs=in_vmem(1)[0],
        out_shape=jax.ShapeDtypeStruct((block_rows, count * side), jnp.bfloat16),
        scratch_shapes=[
            pltpu.VMEM((block_rows, entries), jnp.bfloat16),
            pltpu.VMEM((side, side), jnp.float32),
            pltpu.VMEM((side, side), jnp.float32),
            pltpu.SemaphoreType.DMA((3,)),
        ],
        compiler_params=pltpu.CompilerParams(vmem_limit_bytes=VMEM),
        cost_estimate=pl.CostEstimate(
            flops=block_rows * entries * 4096, bytes_accessed=queries.size * 4, transcendentals=0
        ),
        name="condition",
    )(*operands)


STEP = 256
LOW_PART = 18
MASKS = (3, 1, 2, 0)


def score_rows(queries, store, place, first):
    return dot(store[0, place, pl.ds(first, queries.shape[1])], queries.T)


def own_kernel(queries, far_store, out, store, semaphores):
    def copy_of(step):
        place = pl.ds(pl.multiple_of(step * STEP, STEP), STEP)
        source = far_store.at[0, place, pl.ds(0, store.shape[2])]
        return pltpu.make_async_copy(source, store.at[0, place], semaphores.at[step])

    steps = store.shape[1] // STEP
    for step in range(steps):
        copy_of(step).start()
    padded = jnp.concatenate([jnp.zeros_like(queries)] * 3 + [queries[...]], axis=0)

    def one(step, carry):
        copy_of(step).wait()
        place = pl.ds(pl.multiple_of(step * STEP, STEP), STEP)
        out[place, :] = score_rows(padded, store, place, 0)
        return carry

    lax.fori_loop(0, steps, one, 0)


def score_cost(count, width, examples):
    return pl.CostEstimate(
        flops=2 * count * width * examples, bytes_accessed=examples * width * 2, transcendentals=0
    )


def score_own(queries, store):
    rows, entries = queries.shape
    examples = store.shape[1]
    return pl.pallas_call(
        own_kernel,
        in_specs=in_vmem(1) + [pl.BlockSpec(memory_space=pltpu.HBM)],
        out_specs=in_vmem(1)[0],
        out_shape=jax.ShapeDtypeStruct((examples, 4 * rows), jnp.float32),
        scratch_shapes=[
            pltpu.VMEM((1, examples, entries), store.dtype),
            pltpu.SemaphoreType.DMA((examples // STEP,)),
        ],
        compiler_params=pltpu.CompilerParams(vmem_limit_bytes=VMEM),
        cost_estimate=score_cost(rows, entries, examples),
        name="score_own",
    )(queries, pltpu.with_memory_space_constraint(store, pltpu.HBM))


def stacked(*blocks):
    return jnp.concatenate([block[...] for block in blocks], axis=0)


def low_kernel(near, far, last, store, own_low, out):
    queries = stacked(near, far, last)
    queries = jnp.concatenate([queries, jnp.zeros_like(near)], axis=0)
    out[...] = score_rows(queries, store, slice(None), 0) + own_low[...]


def score_low(near, far, last, store, own_low):
    rows, width = far.shape
    examples = store.shape[1]
    return pl.pallas_call(
        low_kernel,
        in_specs=in_vmem(5),
        out_specs=in_vmem(1)[0],
        out_shape=jax.ShapeDtypeStruct((examples, 4 * rows), jnp.float32),
        compiler_params=pltpu.CompilerParams(vmem_limit_bytes=VMEM),
        cost_estimate=score_cost(3 * rows, width, examples),
        name="score_low",
    )(near, far, last, store, own_low)


def high_kernel(first, near, far, last, own, store, low, *refs):
    outs, total = refs[:-1], refs[-1]
    rows = own.shape[0]
    total[...] = (score_rows(stacked(near, far, last, own), store, slice(None), first) + low[...]).T
    home = lax.bitwise_xor(lax.axis_index("blk"), lax.axis_index("layer"))
    for mask, out in zip(MASKS, outs):
        place = lax.bitwise_and(lax.bitwise_xor(home, mask) + 3, 3)
        out[...] = total[pl.ds(pl.multiple_of(place * rows, rows), rows), :].astype(out.dtype)


def score_high(near, far, last, own, store, low):
    rows, width = far.shape
    examples = store.shape[1]
    kinds = {0: jnp.float32, 1: jnp.bfloat16, 2: jnp.float32, 3: jnp.bfloat16}
    return pl.pallas_call(
        functools.partial(high_kernel, store.shape[2] - width),
        in_specs=in_vmem(6),
        out_specs=in_vmem(4),
        out_shape=[jax.ShapeDtypeStruct((rows, examples), kinds[mask]) for mask in MASKS],
        scratch_shapes=[pltpu.VMEM((4 * rows, examples), jnp.float32)],
        compiler_params=pltpu.CompilerParams(vmem_limit_bytes=VMEM),
        cost_estimate=score_cost(4 * rows, width, examples),
        name="score_high",
    )(near, far, last, own, store, low)


def add_kernel(kept, received, out):
    out[...] = (kept[...] + received[...].astype(jnp.float32)).astype(out.dtype)


def add(kept, received):
    return pl.pallas_call(
        add_kernel,
        in_specs=in_vmem(2),
        out_specs=in_vmem(1)[0],
        out_shape=jax.ShapeDtypeStruct(received.shape, received.dtype),
        compiler_params=pltpu.CompilerParams(vmem_limit_bytes=VMEM),
        name="add",
    )(kept, received)


def finish_kernel(layers, candidates, *refs):
    parts, (out, staged, semaphores) = refs[:-3], refs[-3:]
    tiles_here = out.shape[1] // TILE
    first = lax.axis_index("blk") * tiles_here
    listed = candidates[...]
    width = out.shape[1] // semaphores.shape[0]
    copies = []
    for place in range(semaphores.shape[0]):
        for tile in range(place * width // TILE, (place + 1) * width // TILE):
            columns = slice(tile * TILE, (tile + 1) * TILE)
            total = parts[0][:, columns].astype(jnp.float32)
            for part in parts[1:]:
                total = total + part[:, columns].astype(jnp.float32)
            scaled = total / jnp.sqrt(jnp.float32(layers))
            hit = jnp.max(jnp.where(listed == first + tile, 1.0, 0.0), axis=1, keepdims=True)
            staged[:, columns] = jnp.where(hit > 0.0, scaled, 0.0).astype(staged.dtype)
        here = pl.ds(place * width, width)
        copies.append(pltpu.make_async_copy(staged.at[:, here], out.at[:, here], semaphores.at[place]))
        copies[-1].start()
    for copy in copies:
        copy.wait()


def finish(parts, candidates, layers):
    shape = parts[0].shape
    return pl.pallas_call(
        functools.partial(finish_kernel, layers),
        in_specs=in_vmem(1 + len(parts)),
        out_specs=pl.BlockSpec(memory_space=pltpu.HBM),
        out_shape=jax.ShapeDtypeStruct(shape, jnp.bfloat16),
        scratch_shapes=[pltpu.VMEM(shape, jnp.bfloat16), pltpu.SemaphoreType.DMA((4,))],
        compiler_params=pltpu.CompilerParams(vmem_limit_bytes=VMEM),
        name="finish",
    )(candidates, *parts)


def permuted(value, axis, target_of):
    count = lax.axis_size(axis)
    return lax.ppermute(value, axis, [(source, target_of(source) % count) for source in range(count)])


def swapped(value, axis, mask):
    return permuted(value, axis, lambda source: source ^ mask)


def on_line(own, store, candidates, layers):
    far = [swapped(half, "blk", 2) for half in own]
    near = [swapped(half, "blk", 1) for half in own]
    own_low = score_own(own[0], store)
    near[0], far[0], own_low = lax.optimization_barrier((near[0], far[0], own_low))
    near[1], far[1] = lax.optimization_barrier((near[1], far[1]))
    last = [swapped(half, "blk", 1) for half in far]
    low_scores = score_low(near[0], far[0], last[0], store, own_low)
    across, beside, kept, home = score_high(near[1], far[1], last[1], own[1], store, low_scores)
    across = swapped(add(kept, swapped(across, "layer", 1)), "layer", 2)
    return finish([home, swapped(beside, "layer", 1), across], candidates, layers)


def on_ring(own, store, candidates, layers):
    count = lax.axis_size("blk")
    rows = own[0].shape[0]
    moving = jnp.concatenate(own, axis=1)

    def scores():
        return lax.dot_general(moving, store[0], (((1,), (1,)), ((), ())), preferred_element_type=jnp.float32)

    slots = [scores()]
    for _ in range(count - 1):
        moving = permuted(moving, "blk", lambda source: source + 1)
        slots.append(scores())
    turns = lax.rem(lax.axis_index("blk") - jnp.arange(count) + count, count)
    total = jnp.stack(slots)[turns].reshape(layers, count * rows // layers, store.shape[1])
    parts = lax.all_to_all(total.astype(jnp.bfloat16), "layer", 0, 0)
    return finish([parts[layer] for layer in range(layers)], candidates, layers)


def per_device(queries, store, left_factor, right_factor, candidates):
    layers, count = lax.axis_size("layer"), lax.axis_size("blk")
    side = left_factor.shape[1]
    low = side * LOW_PART // 32
    own = [condition(queries, left_factor, right_factor, *part) for part in ((0, low), (low, side - low))]
    way = on_line if layers == 4 and count == 4 else on_ring
    return way(own, store, candidates, layers)


def solution(mesh):
    placed = (
        P("layer", ("parts", "blk"), None),
        P("layer", ("parts", "blk"), None),
        P("layer", None, None),
        P("layer", None, None),
        P(("parts", "layer"), None),
    )
    return jax.shard_map(
        per_device,
        mesh=mesh,
        in_specs=placed,
        out_specs=P(("parts", "layer"), "blk"),
        check_vma=False,
    )
```

```python
import functools

import jax
import jax.numpy as jnp
from jax import lax
from jax.experimental import pallas as pl
from jax.experimental.pallas import tpu as pltpu
from jax.sharding import PartitionSpec as P

TILE = 128
GROUP = 32
LANES = 128
ROWS = 8
VMEM = 24 * 1024 * 1024


def two_parts(value):
    high = value.astype(jnp.bfloat16)
    low = (value - high.astype(jnp.float32)).astype(jnp.bfloat16)
    return high, low


def iota(shape, axis):
    return lax.broadcasted_iota(jnp.int32, shape, axis)


def dot(left, right):
    return jnp.dot(left, right, preferred_element_type=jnp.float32)


def ones_where(condition):
    return jnp.where(condition, 1.0, 0.0).astype(jnp.bfloat16)


def spread_left(factor_rows):
    count, side = factor_rows.shape
    wide = ones_where(iota((side, side * ROWS), 1) // ROWS == iota((side, side * ROWS), 0))
    same = iota((1, ROWS, side * ROWS), 1) == iota((1, ROWS, side * ROWS), 2) % ROWS

    def one(part):
        columns = dot(part, wide).reshape(count, 1, side * ROWS)
        return jnp.where(same, columns, 0.0).reshape(count * ROWS, side * ROWS).astype(jnp.bfloat16)

    return jnp.concatenate([one(part) for part in two_parts(factor_rows)], axis=1)


def spread_right(right_factor):
    side = right_factor.shape[0]
    wide = ones_where(iota((side, 4 * side), 1) % side == iota((side, 4 * side), 0))
    same = iota((4 * side, 4 * side), 0) // side == iota((4 * side, 4 * side), 1) // side
    high, low = [
        jnp.where(same, jnp.concatenate([dot(part, wide)] * 4, axis=0), 0.0).astype(jnp.bfloat16)
        for part in two_parts(right_factor)
    ]
    return jnp.concatenate([high, low, high], axis=0)


def condition_kernel(first, count, queries_in, left_in, right_in, out, queries, left_factor, right_factor, arrived):
    copies = [
        pltpu.make_async_copy(source.at[0], target, arrived.at[place])
        for place, (source, target) in enumerate(
            [(left_in, left_factor), (right_in, right_factor), (queries_in, queries)]
        )
    ]
    for copy in copies:
        copy.start()
    side = left_factor.shape[0]
    pairs = side // 2
    copies[0].wait()
    copies[1].wait()
    left = spread_left(left_factor[pl.ds(first, count), :])
    right = spread_right(right_factor[...])
    low_half = iota((1, 1, LANES), 2) < side
    copies[2].wait()
    for block in range(queries.shape[0] // GROUP):
        rows = pl.ds(block * GROUP, GROUP)
        straight = jnp.stack(
            [queries[rows, pl.ds(pair * LANES, LANES)].astype(jnp.float32) for pair in range(pairs)]
        )
        swapped = pltpu.roll(straight, side, 2).reshape(pairs, GROUP // ROWS, ROWS, LANES)
        straight = straight.reshape(pairs, GROUP // ROWS, ROWS, LANES)
        columns = []
        for group in (0, 2):
            even = jnp.where(low_half, straight[:, group], swapped[:, group + 1])
            odd = jnp.where(low_half, swapped[:, group], straight[:, group + 1])
            columns.append(jnp.stack([even, odd], axis=1).reshape(side * ROWS, LANES))
        grid = jnp.concatenate(columns, axis=1).astype(jnp.bfloat16)
        halfway = dot(left, jnp.concatenate([grid, grid], axis=0))
        high, low = two_parts(halfway)
        result = dot(jnp.concatenate([high, high, low], axis=1), right)
        result = result.reshape(count // 2, 2, ROWS, 2 * LANES)
        groups = []
        for half in range(2):
            even = result[:, 0, :, half * LANES : (half + 1) * LANES]
            odd = result[:, 1, :, half * LANES : (half + 1) * LANES]
            groups.append(jnp.where(low_half, even, pltpu.roll(odd, side, 2)))
            groups.append(jnp.where(low_half, pltpu.roll(even, side, 2), odd))
        done = jnp.concatenate(groups, axis=1).astype(jnp.bfloat16)
        for pair in range(count // 2):
            out[rows, pl.ds(pair * LANES, LANES)] = done[pair]


def in_vmem(count):
    return [pl.BlockSpec(memory_space=pltpu.VMEM)] * count


def condition(queries, left_factor, right_factor, first, count):
    unused, block_rows, entries = queries.shape
    side = left_factor.shape[1]
    operands = [pltpu.with_memory_space_constraint(value, pltpu.HBM) for value in (queries, left_factor, right_factor)]
    return pl.pallas_call(
        functools.partial(condition_kernel, first, count),
        in_specs=[pl.BlockSpec(memory_space=pltpu.HBM)] * 3,
        out_specs=in_vmem(1)[0],
        out_shape=jax.ShapeDtypeStruct((block_rows, count * side), jnp.bfloat16),
        scratch_shapes=[
            pltpu.VMEM((block_rows, entries), jnp.bfloat16),
            pltpu.VMEM((side, side), jnp.float32),
            pltpu.VMEM((side, side), jnp.float32),
            pltpu.SemaphoreType.DMA((3,)),
        ],
        compiler_params=pltpu.CompilerParams(vmem_limit_bytes=VMEM),
        cost_estimate=pl.CostEstimate(
            flops=block_rows * entries * 4096, bytes_accessed=queries.size * 4, transcendentals=0
        ),
        name="condition",
    )(*operands)


STEP = 256
LOW_PART = 18
MASKS = (3, 1, 2, 0)


def score_rows(queries, store, place, first):
    return dot(store[0, place, pl.ds(first, queries.shape[1])], queries.T)


def own_kernel(queries, far_store, out, store, semaphores):
    def copy_of(step):
        place = pl.ds(pl.multiple_of(step * STEP, STEP), STEP)
        source = far_store.at[0, place, pl.ds(0, store.shape[2])]
        return pltpu.make_async_copy(source, store.at[0, place], semaphores.at[step])

    steps = store.shape[1] // STEP
    for step in range(steps):
        copy_of(step).start()
    padded = jnp.concatenate([jnp.zeros_like(queries)] * 3 + [queries[...]], axis=0)

    def one(step, carry):
        copy_of(step).wait()
        place = pl.ds(pl.multiple_of(step * STEP, STEP), STEP)
        out[place, :] = score_rows(padded, store, place, 0)
        return carry

    lax.fori_loop(0, steps, one, 0)


def score_cost(count, width, examples):
    return pl.CostEstimate(
        flops=2 * count * width * examples, bytes_accessed=examples * width * 2, transcendentals=0
    )


def score_own(queries, store):
    rows, entries = queries.shape
    examples = store.shape[1]
    return pl.pallas_call(
        own_kernel,
        in_specs=in_vmem(1) + [pl.BlockSpec(memory_space=pltpu.HBM)],
        out_specs=in_vmem(1)[0],
        out_shape=jax.ShapeDtypeStruct((examples, 4 * rows), jnp.float32),
        scratch_shapes=[
            pltpu.VMEM((1, examples, entries), store.dtype),
            pltpu.SemaphoreType.DMA((examples // STEP,)),
        ],
        compiler_params=pltpu.CompilerParams(vmem_limit_bytes=VMEM),
        cost_estimate=score_cost(rows, entries, examples),
        name="score_own",
    )(queries, pltpu.with_memory_space_constraint(store, pltpu.HBM))


def stacked(*blocks):
    return jnp.concatenate([block[...] for block in blocks], axis=0)


def low_kernel(near, far, last, store, own_low, out):
    queries = stacked(near, far, last)
    queries = jnp.concatenate([queries, jnp.zeros_like(near)], axis=0)
    out[...] = score_rows(queries, store, slice(None), 0) + own_low[...]


def score_low(near, far, last, store, own_low):
    rows, width = far.shape
    examples = store.shape[1]
    return pl.pallas_call(
        low_kernel,
        in_specs=in_vmem(5),
        out_specs=in_vmem(1)[0],
        out_shape=jax.ShapeDtypeStruct((examples, 4 * rows), jnp.float32),
        compiler_params=pltpu.CompilerParams(vmem_limit_bytes=VMEM),
        cost_estimate=score_cost(3 * rows, width, examples),
        name="score_low",
    )(near, far, last, store, own_low)


def high_kernel(first, near, far, last, own, store, low, *refs):
    outs, total = refs[:-1], refs[-1]
    rows = own.shape[0]
    total[...] = (score_rows(stacked(near, far, last, own), store, slice(None), first) + low[...]).T
    home = lax.bitwise_xor(lax.axis_index("blk"), lax.axis_index("layer"))
    for mask, out in zip(MASKS, outs):
        place = lax.bitwise_and(lax.bitwise_xor(home, mask) + 3, 3)
        out[...] = total[pl.ds(pl.multiple_of(place * rows, rows), rows), :].astype(out.dtype)


def score_high(near, far, last, own, store, low):
    rows, width = far.shape
    examples = store.shape[1]
    kinds = {0: jnp.float32, 1: jnp.bfloat16, 2: jnp.float32, 3: jnp.bfloat16}
    return pl.pallas_call(
        functools.partial(high_kernel, store.shape[2] - width),
        in_specs=in_vmem(6),
        out_specs=in_vmem(4),
        out_shape=[jax.ShapeDtypeStruct((rows, examples), kinds[mask]) for mask in MASKS],
        scratch_shapes=[pltpu.VMEM((4 * rows, examples), jnp.float32)],
        compiler_params=pltpu.CompilerParams(vmem_limit_bytes=VMEM),
        cost_estimate=score_cost(4 * rows, width, examples),
        name="score_high",
    )(near, far, last, own, store, low)


def add_kernel(kept, received, out):
    out[...] = (kept[...] + received[...].astype(jnp.float32)).astype(out.dtype)


def add(kept, received):
    return pl.pallas_call(
        add_kernel,
        in_specs=in_vmem(2),
        out_specs=in_vmem(1)[0],
        out_shape=jax.ShapeDtypeStruct(received.shape, received.dtype),
        compiler_params=pltpu.CompilerParams(vmem_limit_bytes=VMEM),
        name="add",
    )(kept, received)


def write_rows(total, layers, listed, out):
    scaled = total / jnp.sqrt(jnp.float32(layers))
    tiles_here = out.shape[1] // TILE
    first = lax.axis_index("blk") * tiles_here
    for tile in range(tiles_here):
        hit = jnp.max(jnp.where(listed == first + tile, 1.0, 0.0), axis=1, keepdims=True)
        columns = slice(tile * TILE, (tile + 1) * TILE)
        out[:, columns] = jnp.where(hit > 0.0, scaled[:, columns], 0.0).astype(out.dtype)


def finish_kernel(layers, candidates, *refs):
    parts, out = refs[:-1], refs[-1]
    total = parts[0][...].astype(jnp.float32)
    for part in parts[1:]:
        total = total + part[...].astype(jnp.float32)
    write_rows(total, layers, candidates[...], out)


def finish(parts, candidates, layers):
    return pl.pallas_call(
        functools.partial(finish_kernel, layers),
        in_specs=in_vmem(1 + len(parts)),
        out_specs=in_vmem(1)[0],
        out_shape=jax.ShapeDtypeStruct(parts[0].shape, jnp.bfloat16),
        compiler_params=pltpu.CompilerParams(vmem_limit_bytes=VMEM),
        name="finish",
    )(candidates, *parts)


def permuted(value, axis, target_of):
    count = lax.axis_size(axis)
    return lax.ppermute(value, axis, [(source, target_of(source) % count) for source in range(count)])


def swapped(value, axis, mask):
    return permuted(value, axis, lambda source: source ^ mask)


def on_line(own, store, candidates, layers):
    far = [swapped(half, "blk", 2) for half in own]
    near = [swapped(half, "blk", 1) for half in own]
    own_low = score_own(own[0], store)
    near[0], far[0], own_low = lax.optimization_barrier((near[0], far[0], own_low))
    near[1], far[1] = lax.optimization_barrier((near[1], far[1]))
    last = [swapped(half, "blk", 1) for half in far]
    low_scores = score_low(near[0], far[0], last[0], store, own_low)
    across, beside, kept, home = score_high(near[1], far[1], last[1], own[1], store, low_scores)
    across = swapped(add(kept, swapped(across, "layer", 1)), "layer", 2)
    return finish([home, swapped(beside, "layer", 1), across], candidates, layers)


def on_ring(own, store, candidates, layers):
    count = lax.axis_size("blk")
    rows = own[0].shape[0]
    moving = jnp.concatenate(own, axis=1)

    def scores():
        return lax.dot_general(moving, store[0], (((1,), (1,)), ((), ())), preferred_element_type=jnp.float32)

    slots = [scores()]
    for _ in range(count - 1):
        moving = permuted(moving, "blk", lambda source: source + 1)
        slots.append(scores())
    turns = lax.rem(lax.axis_index("blk") - jnp.arange(count) + count, count)
    total = jnp.stack(slots)[turns].reshape(layers, count * rows // layers, store.shape[1])
    parts = lax.all_to_all(total.astype(jnp.bfloat16), "layer", 0, 0)
    return finish([parts[layer] for layer in range(layers)], candidates, layers)


def per_device(queries, store, left_factor, right_factor, candidates):
    layers, count = lax.axis_size("layer"), lax.axis_size("blk")
    side = left_factor.shape[1]
    low = side * LOW_PART // 32
    own = [condition(queries, left_factor, right_factor, *part) for part in ((0, low), (low, side - low))]
    way = on_line if layers == 4 and count == 4 else on_ring
    return way(own, store, candidates, layers)


def solution(mesh):
    placed = (
        P("layer", ("parts", "blk"), None),
        P("layer", ("parts", "blk"), None),
        P("layer", None, None),
        P("layer", None, None),
        P(("parts", "layer"), None),
    )
    return jax.shard_map(
        per_device,
        mesh=mesh,
        in_specs=placed,
        out_specs=P(("parts", "layer"), "blk"),
        check_vma=False,
    )
```

```python
import functools

import jax
import jax.numpy as jnp
from jax import lax
from jax.experimental import pallas as pl
from jax.experimental.pallas import tpu as pltpu
from jax.sharding import PartitionSpec as P

TILE = 128
GROUP = 32
LANES = 128
ROWS = 8
VMEM = 24 * 1024 * 1024


def two_parts(value):
    high = value.astype(jnp.bfloat16)
    low = (value - high.astype(jnp.float32)).astype(jnp.bfloat16)
    return high, low


def iota(shape, axis):
    return lax.broadcasted_iota(jnp.int32, shape, axis)


def dot(left, right):
    return jnp.dot(left, right, preferred_element_type=jnp.float32)


def ones_where(condition):
    return jnp.where(condition, 1.0, 0.0).astype(jnp.bfloat16)


def spread_left(factor_rows):
    count, side = factor_rows.shape
    wide = ones_where(iota((side, side * ROWS), 1) // ROWS == iota((side, side * ROWS), 0))
    same = iota((1, ROWS, side * ROWS), 1) == iota((1, ROWS, side * ROWS), 2) % ROWS

    def one(part):
        columns = dot(part, wide).reshape(count, 1, side * ROWS)
        return jnp.where(same, columns, 0.0).reshape(count * ROWS, side * ROWS).astype(jnp.bfloat16)

    return jnp.concatenate([one(part) for part in two_parts(factor_rows)], axis=1)


def spread_right(right_factor):
    side = right_factor.shape[0]
    wide = ones_where(iota((side, 4 * side), 1) % side == iota((side, 4 * side), 0))
    same = iota((4 * side, 4 * side), 0) // side == iota((4 * side, 4 * side), 1) // side
    high, low = [
        jnp.where(same, jnp.concatenate([dot(part, wide)] * 4, axis=0), 0.0).astype(jnp.bfloat16)
        for part in two_parts(right_factor)
    ]
    return jnp.concatenate([high, low, high], axis=0)


def condition_kernel(first, count, queries_in, left_in, right_in, out, queries, left_factor, right_factor, arrived):
    copies = [
        pltpu.make_async_copy(source.at[0], target, arrived.at[place])
        for place, (source, target) in enumerate(
            [(left_in, left_factor), (right_in, right_factor), (queries_in, queries)]
        )
    ]
    for copy in copies:
        copy.start()
    side = left_factor.shape[0]
    pairs = side // 2
    copies[0].wait()
    copies[1].wait()
    left = spread_left(left_factor[pl.ds(first, count), :])
    right = spread_right(right_factor[...])
    low_half = iota((1, 1, LANES), 2) < side
    copies[2].wait()
    for block in range(queries.shape[0] // GROUP):
        rows = pl.ds(block * GROUP, GROUP)
        straight = jnp.stack(
            [queries[rows, pl.ds(pair * LANES, LANES)].astype(jnp.float32) for pair in range(pairs)]
        )
        swapped = pltpu.roll(straight, side, 2).reshape(pairs, GROUP // ROWS, ROWS, LANES)
        straight = straight.reshape(pairs, GROUP // ROWS, ROWS, LANES)
        columns = []
        for group in (0, 2):
            even = jnp.where(low_half, straight[:, group], swapped[:, group + 1])
            odd = jnp.where(low_half, swapped[:, group], straight[:, group + 1])
            columns.append(jnp.stack([even, odd], axis=1).reshape(side * ROWS, LANES))
        grid = jnp.concatenate(columns, axis=1).astype(jnp.bfloat16)
        halfway = dot(left, jnp.concatenate([grid, grid], axis=0))
        high, low = two_parts(halfway)
        result = dot(jnp.concatenate([high, high, low], axis=1), right)
        result = result.reshape(count // 2, 2, ROWS, 2 * LANES)
        groups = []
        for half in range(2):
            even = result[:, 0, :, half * LANES : (half + 1) * LANES]
            odd = result[:, 1, :, half * LANES : (half + 1) * LANES]
            groups.append(jnp.where(low_half, even, pltpu.roll(odd, side, 2)))
            groups.append(jnp.where(low_half, pltpu.roll(even, side, 2), odd))
        done = jnp.concatenate(groups, axis=1).astype(jnp.bfloat16)
        for pair in range(count // 2):
            out[rows, pl.ds(pair * LANES, LANES)] = done[pair]


def in_vmem(count):
    return [pl.BlockSpec(memory_space=pltpu.VMEM)] * count


def condition(queries, left_factor, right_factor, first, count):
    unused, block_rows, entries = queries.shape
    side = left_factor.shape[1]
    operands = [pltpu.with_memory_space_constraint(value, pltpu.HBM) for value in (queries, left_factor, right_factor)]
    return pl.pallas_call(
        functools.partial(condition_kernel, first, count),
        in_specs=[pl.BlockSpec(memory_space=pltpu.HBM)] * 3,
        out_specs=in_vmem(1)[0],
        out_shape=jax.ShapeDtypeStruct((block_rows, count * side), jnp.bfloat16),
        scratch_shapes=[
            pltpu.VMEM((block_rows, entries), jnp.bfloat16),
            pltpu.VMEM((side, side), jnp.float32),
            pltpu.VMEM((side, side), jnp.float32),
            pltpu.SemaphoreType.DMA((3,)),
        ],
        compiler_params=pltpu.CompilerParams(vmem_limit_bytes=VMEM),
        cost_estimate=pl.CostEstimate(
            flops=block_rows * entries * 4096, bytes_accessed=queries.size * 4, transcendentals=0
        ),
        name="condition",
    )(*operands)


STEP = 256
LOW_PART = 19
MASKS = (3, 1, 2, 0)


def score_rows(queries, store, place, first):
    return dot(store[0, place, pl.ds(first, queries.shape[1])], queries.T)


def own_kernel(queries, far_store, out, store, semaphores):
    def copy_of(step):
        place = pl.ds(pl.multiple_of(step * STEP, STEP), STEP)
        source = far_store.at[0, place, pl.ds(0, store.shape[2])]
        return pltpu.make_async_copy(source, store.at[0, place], semaphores.at[step])

    steps = store.shape[1] // STEP
    for step in range(steps):
        copy_of(step).start()
    padded = jnp.concatenate([jnp.zeros_like(queries)] * 3 + [queries[...]], axis=0)

    def one(step, carry):
        copy_of(step).wait()
        place = pl.ds(pl.multiple_of(step * STEP, STEP), STEP)
        out[place, :] = score_rows(padded, store, place, 0)
        return carry

    lax.fori_loop(0, steps, one, 0)


def score_cost(count, width, examples):
    return pl.CostEstimate(
        flops=2 * count * width * examples, bytes_accessed=examples * width * 2, transcendentals=0
    )


def score_own(queries, store):
    rows, entries = queries.shape
    examples = store.shape[1]
    return pl.pallas_call(
        own_kernel,
        in_specs=in_vmem(1) + [pl.BlockSpec(memory_space=pltpu.HBM)],
        out_specs=in_vmem(1)[0],
        out_shape=jax.ShapeDtypeStruct((examples, 4 * rows), jnp.float32),
        scratch_shapes=[
            pltpu.VMEM((1, examples, entries), store.dtype),
            pltpu.SemaphoreType.DMA((examples // STEP,)),
        ],
        compiler_params=pltpu.CompilerParams(vmem_limit_bytes=VMEM),
        cost_estimate=score_cost(rows, entries, examples),
        name="score_own",
    )(queries, pltpu.with_memory_space_constraint(store, pltpu.HBM))


def stacked(*blocks):
    return jnp.concatenate([block[...] for block in blocks], axis=0)


def low_kernel(near, far, last, store, own_low, out):
    queries = stacked(near, far, last)
    queries = jnp.concatenate([queries, jnp.zeros_like(near)], axis=0)
    out[...] = score_rows(queries, store, slice(None), 0) + own_low[...]


def score_low(near, far, last, store, own_low):
    rows, width = far.shape
    examples = store.shape[1]
    return pl.pallas_call(
        low_kernel,
        in_specs=in_vmem(5),
        out_specs=in_vmem(1)[0],
        out_shape=jax.ShapeDtypeStruct((examples, 4 * rows), jnp.float32),
        compiler_params=pltpu.CompilerParams(vmem_limit_bytes=VMEM),
        cost_estimate=score_cost(3 * rows, width, examples),
        name="score_low",
    )(near, far, last, store, own_low)


def high_kernel(first, near, far, last, own, store, low, *refs):
    outs, total = refs[:-1], refs[-1]
    rows = own.shape[0]
    total[...] = (score_rows(stacked(near, far, last, own), store, slice(None), first) + low[...]).T
    home = lax.bitwise_xor(lax.axis_index("blk"), lax.axis_index("layer"))
    for mask, out in zip(MASKS, outs):
        place = lax.bitwise_and(lax.bitwise_xor(home, mask) + 3, 3)
        out[...] = total[pl.ds(pl.multiple_of(place * rows, rows), rows), :].astype(out.dtype)


def score_high(near, far, last, own, store, low):
    rows, width = far.shape
    examples = store.shape[1]
    kinds = {0: jnp.float32, 1: jnp.bfloat16, 2: jnp.float32, 3: jnp.bfloat16}
    return pl.pallas_call(
        functools.partial(high_kernel, store.shape[2] - width),
        in_specs=in_vmem(6),
        out_specs=in_vmem(4),
        out_shape=[jax.ShapeDtypeStruct((rows, examples), kinds[mask]) for mask in MASKS],
        scratch_shapes=[pltpu.VMEM((4 * rows, examples), jnp.float32)],
        compiler_params=pltpu.CompilerParams(vmem_limit_bytes=VMEM),
        cost_estimate=score_cost(4 * rows, width, examples),
        name="score_high",
    )(near, far, last, own, store, low)


def add_kernel(kept, received, out):
    out[...] = (kept[...] + received[...].astype(jnp.float32)).astype(out.dtype)


def add(kept, received):
    return pl.pallas_call(
        add_kernel,
        in_specs=in_vmem(2),
        out_specs=in_vmem(1)[0],
        out_shape=jax.ShapeDtypeStruct(received.shape, received.dtype),
        compiler_params=pltpu.CompilerParams(vmem_limit_bytes=VMEM),
        name="add",
    )(kept, received)


def write_rows(total, layers, listed, out):
    scaled = total / jnp.sqrt(jnp.float32(layers))
    tiles_here = out.shape[1] // TILE
    first = lax.axis_index("blk") * tiles_here
    for tile in range(tiles_here):
        hit = jnp.max(jnp.where(listed == first + tile, 1.0, 0.0), axis=1, keepdims=True)
        columns = slice(tile * TILE, (tile + 1) * TILE)
        out[:, columns] = jnp.where(hit > 0.0, scaled[:, columns], 0.0).astype(out.dtype)


def finish_kernel(layers, candidates, *refs):
    parts, out = refs[:-1], refs[-1]
    total = parts[0][...].astype(jnp.float32)
    for part in parts[1:]:
        total = total + part[...].astype(jnp.float32)
    write_rows(total, layers, candidates[...], out)


def finish(parts, candidates, layers):
    return pl.pallas_call(
        functools.partial(finish_kernel, layers),
        in_specs=in_vmem(1 + len(parts)),
        out_specs=in_vmem(1)[0],
        out_shape=jax.ShapeDtypeStruct(parts[0].shape, jnp.bfloat16),
        compiler_params=pltpu.CompilerParams(vmem_limit_bytes=VMEM),
        name="finish",
    )(candidates, *parts)


def permuted(value, axis, target_of):
    count = lax.axis_size(axis)
    return lax.ppermute(value, axis, [(source, target_of(source) % count) for source in range(count)])


def swapped(value, axis, mask):
    return permuted(value, axis, lambda source: source ^ mask)


def on_line(own, store, candidates, layers):
    far = [swapped(half, "blk", 2) for half in own]
    near = [swapped(half, "blk", 1) for half in own]
    own_low = score_own(own[0], store)
    near[0], far[0], own_low = lax.optimization_barrier((near[0], far[0], own_low))
    near[1], far[1] = lax.optimization_barrier((near[1], far[1]))
    last = [swapped(half, "blk", 1) for half in far]
    low_scores = score_low(near[0], far[0], last[0], store, own_low)
    across, beside, kept, home = score_high(near[1], far[1], last[1], own[1], store, low_scores)
    across = swapped(add(kept, swapped(across, "layer", 1)), "layer", 2)
    return finish([home, swapped(beside, "layer", 1), across], candidates, layers)


def on_ring(own, store, candidates, layers):
    count = lax.axis_size("blk")
    rows = own[0].shape[0]
    moving = jnp.concatenate(own, axis=1)

    def scores():
        return lax.dot_general(moving, store[0], (((1,), (1,)), ((), ())), preferred_element_type=jnp.float32)

    slots = [scores()]
    for _ in range(count - 1):
        moving = permuted(moving, "blk", lambda source: source + 1)
        slots.append(scores())
    turns = lax.rem(lax.axis_index("blk") - jnp.arange(count) + count, count)
    total = jnp.stack(slots)[turns].reshape(layers, count * rows // layers, store.shape[1])
    parts = lax.all_to_all(total.astype(jnp.bfloat16), "layer", 0, 0)
    return finish([parts[layer] for layer in range(layers)], candidates, layers)


def per_device(queries, store, left_factor, right_factor, candidates):
    layers, count = lax.axis_size("layer"), lax.axis_size("blk")
    side = left_factor.shape[1]
    low = side * LOW_PART // 32
    own = [condition(queries, left_factor, right_factor, *part) for part in ((0, low), (low, side - low))]
    way = on_line if layers == 4 and count == 4 else on_ring
    return way(own, store, candidates, layers)


def solution(mesh):
    placed = (
        P("layer", ("parts", "blk"), None),
        P("layer", ("parts", "blk"), None),
        P("layer", None, None),
        P("layer", None, None),
        P(("parts", "layer"), None),
    )
    return jax.shard_map(
        per_device,
        mesh=mesh,
        in_specs=placed,
        out_specs=P(("parts", "layer"), "blk"),
        check_vma=False,
    )
```
